32 devices in a mesh: inst: 1, ep: 8 (over z, y), dp: 4 (over x, core).
Axes of the slice: x: 2, y: 2, z: 4, core: 2. Of those that a mesh axis runs over, the one named last changes fastest.
Arguments:
- hidden: bfloat16 [64, 7168], P(('inst', 'ep', 'dp')), may hold values from -6 to 6
- routes: int32 [64, 4], P(('inst', 'ep', 'dp')), may hold values from 0 to 7, all different within a row; in each aligned block of 8 rows (0 to 7, 8 to 15, ...) at most 8 rows name the same one
- route_weight: float32 [64, 4], P(('inst', 'ep', 'dp')), may hold values from 0.2 to 1
- gate_weight: bfloat16 [8, 7168, 2048], P('ep', None, 'dp'), may hold values from -0.0625 to 0.0625
- up_weight: bfloat16 [8, 7168, 2048], P('ep', None, 'dp'), may hold values from -0.0625 to 0.0625
- down_weight: bfloat16 [8, 2048, 7168], P('ep', 'dp'), may hold values from -0.125 to 0.125
- queries: bfloat16 [64, 36864], P(('inst', 'ep', 'dp')), may hold values from -5600 to 5600
- latent_pool: bfloat16 [768, 18432], P(('inst', 'ep', 'dp')), may hold values from -4 to 4
- lengths: int32 [64], P(('inst', 'ep', 'dp')), may hold values from 65 to 384
- page_table: int32 [64, 12], P(('inst', 'ep', 'dp')), may hold values from 0 to 31, as said below
- moved_page: int32 [32, 6], P(('inst', 'ep', 'dp')), may hold values from 0 to 23, as said below
- moved_dest: int32 [32, 6], P(('inst', 'ep', 'dp')), may hold values from 0 to 3, as said below
Outputs:
- expert_mix: bfloat16 [64, 7168], P(('inst', 'ep', 'dp'))
- attended: bfloat16 [64, 32768], P(('inst', 'ep', 'dp'))
The draws below stay inside these ranges and needn't reach their ends.
Inputs may be any that keep to these rules, and one draw needn't show every extreme that they name: `routes`: a row names 4 different experts; in each aligned block of 8 rows (one dp group) no expert is named by more than 8 rows, a bound that some block reaches. `page_table`: the 12 entries of a row name distinct slots, and no two rows of one device share a slot; every page below a row's length names a slot that holds data after migration; every slot that receives a page is named by a live page. `moved_page`: 6 distinct pages of the sending device. `moved_dest`: never the sender's own dp index; each other dp index is named by exactly 2 entries of a device.
All inputs are finite; a program needn't handle non-finite values.
Results may differ from the reference program's by a relative error of at most 0.0059.
Values may be sent and summed in bfloat16 or wider, within the bound.
No kernel may reach another device: no remote copies, remote signals or barrier semaphores. Data moves between devices by JAX's collectives and lax.ppermute only.
A program may use at most 128 MiB of HBM per device.

```python
import math
import jax
import jax.numpy as jnp
import numpy as np
from jax import lax

D = 7168
FF = 2048
HEADS = 64
LAT = 576
VL = 512
TOPK = 4
ROWS_DEV = 2
PAGE = 32
MAXP = 12
MCAP = 2
MIG = 6
EXPERTS = 8
ROWS = 64
GROUP = 8
CAP = 8
OWN = 24
POOL = 768
MAXLEN = 384
MINLEN = 65
N_EP = 8
N_DP = 4


def layout(key):
    device_count = N_EP * N_DP
    slot_count = OWN + N_DP * MCAP
    subkeys = jax.random.split(key, 6)
    dest_base = jnp.arange(MIG, dtype=jnp.int32) // MCAP + 1
    order_scores = jax.random.randint(subkeys[0], (device_count, MIG), 0, 1 << 16) * MIG + jnp.arange(MIG, dtype=jnp.int32)
    order = jnp.argsort(order_scores, axis=1).astype(jnp.int32)
    chosen = dest_base[order]
    own_index = jnp.arange(device_count, dtype=jnp.int32) % N_DP
    moved_dest = ((own_index[:, None] + chosen) % N_DP).astype(jnp.int32)
    page_scores = jax.random.randint(subkeys[1], (device_count, OWN), 0, 1 << 16) * OWN + jnp.arange(OWN, dtype=jnp.int32)
    moved_page = jnp.argsort(page_scores, axis=1)[:, :MIG].astype(jnp.int32)
    counts = jnp.sum((moved_dest[:, :, None] == jnp.arange(N_DP, dtype=jnp.int32)[None, None, :]).astype(jnp.int32), axis=1)
    counts = counts.reshape(N_EP, N_DP, N_DP).transpose(0, 2, 1).reshape(device_count, N_DP)
    filled = jnp.arange(MCAP, dtype=jnp.int32)[None, None, :] < counts[:, :, None]
    category = jnp.concatenate([jnp.ones((device_count, OWN), jnp.int32), jnp.where(filled.reshape(device_count, N_DP * MCAP), 0, 2).astype(jnp.int32)], axis=1)
    slot_scores = category * (1 << 26) + jax.random.randint(subkeys[2], (device_count, slot_count), 0, 1 << 16) * slot_count + jnp.arange(slot_count, dtype=jnp.int32)
    slot_order = jnp.argsort(slot_scores, axis=1).astype(jnp.int32)[:, :ROWS_DEV * MAXP]
    page_rows = slot_order.reshape(device_count, MAXP, ROWS_DEV).transpose(0, 2, 1).reshape(device_count * ROWS_DEV, MAXP)
    length_span = MAXLEN - MINLEN
    first_draw = jax.random.randint(subkeys[3], (device_count * ROWS_DEV,), 0, length_span + 1)
    second_draw = jax.random.randint(subkeys[4], (device_count * ROWS_DEV,), 0, length_span + 1)
    row_lengths = MINLEN + first_draw * second_draw // length_span
    longest = jax.random.randint(subkeys[5], (), 0, device_count * ROWS_DEV)
    row_lengths = jnp.where(jnp.arange(device_count * ROWS_DEV, dtype=jnp.int32) == longest, MAXLEN, row_lengths).astype(jnp.int32)
    return (moved_page, moved_dest, page_rows, row_lengths)


def draw_moved_page(key, part):
    return layout(key)[0]


def draw_moved_dest(key, part):
    return layout(key)[1]


def draw_page_table(key, part):
    return layout(key)[2]


def draw_lengths(key, part):
    return layout(key)[3]


def draw_queries(key, part):
    key = jax.random.fold_in(key, 11)
    subkeys = jax.random.split(key, 1)
    drawn = jnp.clip(jax.random.normal(subkeys[0], (ROWS, HEADS, LAT), jnp.float32), -4.0, 4.0)
    return drawn.reshape(ROWS, HEADS * LAT).astype(jnp.bfloat16)


def draw_latent_pool(key, part):
    key = jax.random.fold_in(key, 12)
    drawn = jnp.clip(jax.random.normal(key, (POOL, PAGE, LAT), jnp.float32), -4.0, 4.0)
    return drawn.reshape(POOL, PAGE * LAT).astype(jnp.bfloat16)


def block_levels(key, shape, pieces, low, largest):
    def one(position, blocks):
        heights = jax.random.uniform(jax.random.fold_in(jax.random.fold_in(key, 6), position), (blocks,), jnp.float32, low / len(pieces), largest / len(pieces))
        return jnp.repeat(jnp.exp(heights), shape[position] // blocks).reshape((-1,) + (1,) * (len(shape) - position - 1))

    factor_of = one(*pieces[0])
    for cut in pieces[1:]:
        factor_of = factor_of * one(*cut)
    return factor_of


def assign_block(rng, own, number, rows, amount, top, most, slope):
    sequence = jax.random.permutation(rng, amount)
    heavy_load, ordinary = load_shares(amount, rows * top, most, slope, True), load_shares(amount, rows * top, most, slope, False)
    places = jnp.arange(amount)

    def named(tallies, offset_by):
        used = int((tallies > 0).sum())
        fixed = max(1, used // 4)
        moved = fixed + (places - fixed + offset_by * (used - fixed)) % max(1, amount - fixed)
        return jnp.zeros((amount,), jnp.int32).at[sequence[jnp.where(places < fixed, places, moved)]].set(jnp.asarray(tallies, jnp.int32))

    tallies = jnp.where(number % 4 == 0, named(heavy_load, number // 4), named(ordinary, number - number // 4 - 1))
    mixed = jax.random.permutation(jax.random.fold_in(own, 3), amount)
    donor, sink = mixed[0:amount // 2 * 2:2], mixed[1:amount // 2 * 2:2]
    slack = jnp.minimum(tallies[donor] - 1, most - tallies[sink]) // 2
    slack = jnp.where((donor == sequence[0]) | (sink == sequence[0]) | (tallies[sink] == 0), 0, jnp.maximum(slack, 0))
    moved = jax.random.randint(jax.random.fold_in(own, 4), (amount // 2,), 0, 1 << 20) % (slack + 1)
    tallies = tallies.at[donor].add(-moved).at[sink].add(moved)
    members = jnp.searchsorted(jnp.cumsum(tallies), jnp.arange(rows * top), side="right").astype(jnp.int32)
    listing = members.reshape(top, rows).T
    listing = listing[jax.random.permutation(jax.random.fold_in(own, 1), rows)]
    offset_by = jax.random.randint(jax.random.fold_in(own, 2), (rows, 1), 0, top)
    return jnp.take_along_axis(listing, (jnp.arange(top)[None, :] + offset_by) % top, axis=1)


def load_shares(amount, total, most, lean, full):
    loads = [(1 << 20) // math.isqrt(rank ** lean) + 1 for rank in range(1, amount + 1)]
    largest = most if full else min(most, max(-(-total // amount), total * loads[0] // sum(loads)))
    least = 1 if total - largest >= amount - 1 else 0
    given, rest = [largest] + [least] * (amount - 1), total - largest - least * (amount - 1)
    while rest > 0:
        movable = [i for i in range(1, amount) if given[i] < largest] or [i for i in range(1, amount) if given[i] < most]
        whole, remaining = sum([loads[i] for i in movable]), rest
        for i in movable:
            more = min(most - given[i], max(1, remaining * loads[i] // whole), rest)
            given[i] = given[i] + more
            rest = rest - more
    return np.array(given)


def noise(rng, extent, scale, most, shards=(), held_as=jnp.bfloat16):
    gain = block_levels(rng, extent, shards, -0.22, 0.18) if shards else 1.0
    values = jax.random.normal(rng, extent, jnp.float32) * scale * gain
    return jnp.minimum(jnp.maximum(values, -most), most).astype(held_as)


def setup_inputs(seed: int = 0, part: int = 0) -> dict:
    key_of = jax.random.split(jax.random.key(seed), 13)
    part_keys = jax.random.split(jax.random.fold_in(key_of[12], part), 13)
    hidden = noise(part_keys[0], (ROWS, D), 1.0, 6.0, ((0, 32),))
    routes_keys = jax.random.split(jax.random.fold_in(part_keys[1], 1), ROWS // GROUP)
    routes_turns = jax.random.permutation(jax.random.fold_in(part_keys[1], 3), ROWS // GROUP)
    routes = jax.vmap(lambda own, number: assign_block(jax.random.fold_in(part_keys[1], 2), own, number, GROUP, N_EP, TOPK, CAP, 2))(routes_keys, routes_turns).reshape((ROWS, TOPK))
    route_weight = jnp.clip(0.2 + 0.8 * jax.random.uniform(part_keys[2], (ROWS, TOPK), jnp.float32) ** block_levels(part_keys[2], (ROWS, TOPK), ((0, 32),), -0.2, 0.2), 0.2, 1.0)
    gate_weight = noise(key_of[3], (EXPERTS, D, FF), D ** -0.5, 0.0625, ((0, 8), (2, 4)))
    up_weight = noise(key_of[4], (EXPERTS, D, FF), D ** -0.5, 0.0625, ((0, 8), (2, 4)))
    down_weight = noise(key_of[5], (EXPERTS, FF, D), FF ** -0.5, 0.125, ((0, 8), (1, 4)))
    queries = draw_queries(jax.random.fold_in(jax.random.fold_in(key_of[12], part), 71), part)
    latent_pool = draw_latent_pool(jax.random.fold_in(jax.random.fold_in(key_of[12], part), 71), part)
    lengths = draw_lengths(jax.random.fold_in(jax.random.fold_in(key_of[12], part), 71), part)
    page_table = draw_page_table(jax.random.fold_in(jax.random.fold_in(key_of[12], part), 71), part)
    moved_page = draw_moved_page(jax.random.fold_in(jax.random.fold_in(key_of[12], part), 71), part)
    moved_dest = draw_moved_dest(jax.random.fold_in(jax.random.fold_in(key_of[12], part), 71), part)
    return {"hidden": hidden, "routes": routes, "route_weight": route_weight, "gate_weight": gate_weight, "up_weight": up_weight, "down_weight": down_weight, "queries": queries, "latent_pool": latent_pool, "lengths": lengths, "page_table": page_table, "moved_page": moved_page, "moved_dest": moved_dest}


score_scale = 192.0 ** -0.5


def migrate(latent_pool, moved_page, moved_dest):
    device_count = N_EP * N_DP
    width = PAGE * LAT
    pool_dev = latent_pool.reshape(device_count, OWN, width)
    same_dest = moved_dest[:, :, None] == moved_dest[:, None, :]
    earlier = jnp.arange(MIG, dtype=jnp.int32)[None, :] < jnp.arange(MIG, dtype=jnp.int32)[:, None]
    entry_rank = jnp.sum((same_dest & earlier[None]).astype(jnp.int32), axis=2).astype(jnp.int32)
    bucket = (moved_dest * MCAP + entry_rank).astype(jnp.int32)
    device_ids = jnp.arange(device_count, dtype=jnp.int32)[:, None]
    sent_pages = pool_dev[device_ids, moved_page]
    outgoing = jnp.zeros((device_count, N_DP * MCAP, width), jnp.bfloat16)
    outgoing = outgoing.at[device_ids, bucket].set(sent_pages)
    outgoing = outgoing.reshape(N_EP, N_DP, N_DP, MCAP, width).transpose(0, 2, 1, 3, 4)
    outgoing = outgoing.reshape(device_count, N_DP * MCAP, width)
    return jnp.concatenate([pool_dev, outgoing], axis=1)


def attend_device(inputs):
    pool_dev, page_rows, row_lengths, query_rows = inputs
    cache_rows = pool_dev[page_rows].reshape(ROWS_DEV, MAXP * PAGE, LAT).astype(jnp.float32)
    scores = jnp.einsum("rhl,rtl->rht", query_rows.astype(jnp.float32), cache_rows, precision=lax.Precision.HIGHEST) * score_scale
    live_mask = jnp.arange(MAXP * PAGE, dtype=jnp.int32)[None, :] < row_lengths[:, None]
    scores = jnp.where(live_mask[:, None, :], scores, -jnp.inf)
    row_max = jnp.max(scores, axis=2, keepdims=True)
    shifted = jnp.exp(scores - row_max)
    attn_probs = (shifted / jnp.sum(shifted, axis=2, keepdims=True)).astype(jnp.bfloat16)
    attended = jnp.einsum("rht,rtv->rhv", attn_probs.astype(jnp.float32), cache_rows[:, :, :VL], precision=lax.Precision.HIGHEST)
    return attended.astype(jnp.bfloat16)


def mix_experts(hidden, routes, route_weight, gate_weight, up_weight, down_weight):
    slot_total = min(ROWS, N_EP * CAP)

    def one_expert(running, expert):
        route_hits = routes == expert
        chosen = jnp.any(route_hits, axis=1)
        weight = jnp.sum(jnp.where(route_hits, route_weight, 0.0), axis=1)
        picked = jnp.argsort(jnp.where(chosen, 0, 1).astype(jnp.int32), stable=True)[:slot_total].astype(jnp.int32)
        rows_in = hidden[picked]
        gate_vals = jnp.dot(rows_in, gate_weight[expert], preferred_element_type=jnp.float32)
        up_vals = jnp.dot(rows_in, up_weight[expert], preferred_element_type=jnp.float32)
        inner_act = (jax.nn.silu(gate_vals) * up_vals).astype(jnp.bfloat16)
        expert_out = jnp.dot(inner_act, down_weight[expert], preferred_element_type=jnp.float32).astype(jnp.bfloat16)
        running = running.at[picked].add(weight[picked][:, None] * expert_out.astype(jnp.float32))
        return running, None

    running, _ = lax.scan(one_expert, jnp.zeros((ROWS, D), jnp.float32), jnp.arange(N_EP, dtype=jnp.int32))
    return running.astype(jnp.bfloat16)


def reference(hidden, routes, route_weight, gate_weight, up_weight, down_weight, queries, latent_pool, lengths, page_table, moved_page, moved_dest):
    device_count = N_EP * N_DP
    expert_mix = mix_experts(hidden, routes, route_weight, gate_weight, up_weight, down_weight)
    pool_after = migrate(latent_pool, moved_page, moved_dest)
    attended = lax.map(attend_device, (pool_after, page_table.reshape(device_count, ROWS_DEV, MAXP), lengths.reshape(device_count, ROWS_DEV), queries.reshape(device_count, ROWS_DEV, HEADS, LAT)))
    return expert_mix, attended.reshape(ROWS, HEADS * VL)
```

```python
import jax
import jax.numpy as jnp
from jax import lax
from jax.sharding import PartitionSpec as P

HEADS = 64
LAT = 576
VL = 512
MCAP = 2
AXES = ("ep", "dp")

score_scale = 192.0 ** (-0.5)


def partner_bits(count):
    bits = []
    b = count // 2
    while b:
        bits.append(b)
        b //= 2
    return bits


def swap(x, count, bit):
    return lax.ppermute(x, AXES, [(i, i ^ bit) for i in range(count)])


def gather_rows(x, count):
    for bit in partner_bits(count):
        x = jnp.concatenate([x, swap(x, count, bit)], axis=0)
    return x


def scatter_sum(x, count):
    for bit in reversed(partner_bits(count)):
        half = x.shape[0] // 2
        got = swap(x[half:].astype(jnp.bfloat16), count, bit)
        x = x[:half] + got.astype(jnp.float32)
    return x


def weight_columns(routes, route_weight, ep_count):
    experts = jnp.arange(ep_count, dtype=jnp.int32)
    table = jnp.sum(jnp.where(routes[:, :, None] == experts, route_weight[:, :, None], 0.0), axis=1)
    high = table.astype(jnp.bfloat16)
    low = (table - high.astype(jnp.float32)).astype(jnp.bfloat16)
    return jnp.pad(jnp.concatenate([high, low], axis=1), ((0, 0), (0, 128 - 2 * ep_count)))


def body(
    hidden,
    routes,
    route_weight,
    gate_weight,
    up_weight,
    down_weight,
    queries,
    latent_pool,
    lengths,
    page_table,
    moved_page,
    moved_dest,
):
    ep_count = lax.axis_size("ep")
    dp_count = lax.axis_size("dp")
    count = ep_count * dp_count
    rows_dev, model_width = hidden.shape
    payload = jnp.concatenate([hidden, weight_columns(routes, route_weight, ep_count)], axis=1)
    everyone = gather_rows(payload, count)
    rows_in = everyone[:, :model_width]
    table = everyone[:, model_width:].astype(jnp.float32)
    mine = jnp.arange(table.shape[1], dtype=jnp.int32) % ep_count == lax.axis_index("ep")
    mine = mine & (jnp.arange(table.shape[1], dtype=jnp.int32) < 2 * ep_count)
    row_weight = jnp.sum(jnp.where(mine, table, 0.0), axis=1, keepdims=True)

    gate_vals = jnp.dot(rows_in, gate_weight[0], preferred_element_type=jnp.float32)
    up_vals = jnp.dot(rows_in, up_weight[0], preferred_element_type=jnp.float32)
    inner_act = (jax.nn.silu(gate_vals) * up_vals).astype(jnp.bfloat16)
    partial_out = jnp.dot(inner_act, down_weight[0], preferred_element_type=jnp.float32) * row_weight
    expert_mix = scatter_sum(partial_out, count).astype(jnp.bfloat16)

    page_dest = moved_dest[0]
    page_pick = moved_page[0]
    entries = page_dest.shape[0]
    same_dest = page_dest[:, None] == page_dest[None, :]
    earlier = (
        jnp.arange(entries, dtype=jnp.int32)[None, :]
        < jnp.arange(entries, dtype=jnp.int32)[:, None]
    )
    entry_rank = jnp.sum((same_dest & earlier).astype(jnp.int32), axis=1)
    bucket = page_dest * MCAP + entry_rank
    bucket_ids = jnp.arange(dp_count * MCAP, dtype=jnp.int32)
    own_slots = jnp.arange(latent_pool.shape[0], dtype=jnp.int32)
    select_pages = jnp.any(
        (bucket[None, :] == bucket_ids[:, None])[:, :, None]
        & (page_pick[None, :, None] == own_slots[None, None, :]),
        axis=1,
    )
    outgoing_pages = jnp.dot(
        select_pages.astype(jnp.bfloat16), latent_pool, preferred_element_type=jnp.float32
    ).astype(jnp.bfloat16)
    outgoing_pages = outgoing_pages.reshape(dp_count, MCAP, latent_pool.shape[1])
    arrived_pages = lax.all_to_all(outgoing_pages, "dp", split_axis=0, concat_axis=0, tiled=True)
    pool_after = jnp.concatenate(
        [latent_pool, arrived_pages.reshape(dp_count * MCAP, latent_pool.shape[1])], axis=0
    )
    key_rows = jnp.take(pool_after, page_table, axis=0).reshape(rows_dev, -1, LAT)
    query_rows = queries.reshape(rows_dev, HEADS, LAT)
    scores = (
        jnp.einsum("rhl,rtl->rht", query_rows, key_rows, preferred_element_type=jnp.float32)
        * score_scale
    )
    live_mask = jnp.arange(key_rows.shape[1], dtype=jnp.int32)[None, :] < lengths[:, None]
    scores = jnp.where(live_mask[:, None, :], scores, -jnp.inf)
    row_max = jnp.max(scores, axis=2, keepdims=True)
    shifted = jnp.exp(scores - row_max)
    attn_probs = (shifted / jnp.sum(shifted, axis=2, keepdims=True)).astype(jnp.bfloat16)
    attended = jnp.einsum(
        "rht,rtv->rhv", attn_probs, key_rows[:, :, :VL], preferred_element_type=jnp.float32
    ).astype(jnp.bfloat16)
    return (expert_mix, attended.reshape(rows_dev, HEADS * VL))


def solution(mesh):
    in_specs = (
        P(("inst", "ep", "dp"), None),
        P(("inst", "ep", "dp"), None),
        P(("inst", "ep", "dp"), None),
        P("ep", None, "dp"),
        P("ep", None, "dp"),
        P("ep", "dp", None),
        P(("inst", "ep", "dp"), None),
        P(("inst", "ep", "dp"), None),
        P(("inst", "ep", "dp")),
        P(("inst", "ep", "dp"), None),
        P(("inst", "ep", "dp"), None),
        P(("inst", "ep", "dp"), None),
    )
    out_specs = (P(("inst", "ep", "dp"), None), P(("inst", "ep", "dp"), None))
    return jax.shard_map(body, mesh=mesh, in_specs=in_specs, out_specs=out_specs, check_vma=False)
```

```python
import functools

import jax
import jax.numpy as jnp
from jax import lax
from jax.experimental import pallas as pl
from jax.experimental.pallas import tpu as pltpu
from jax.sharding import PartitionSpec as P

HEADS = 64
LAT = 576
VL = 512
MCAP = 2
PAGE = 32
LANES = 128
AXES = ("ep", "dp")
MIB = 1 << 20

score_scale = 192.0 ** (-0.5)
bf16 = jnp.bfloat16
f32 = jnp.float32


def in_vmem():
    return pl.BlockSpec(memory_space=pltpu.VMEM)


def in_smem():
    return pl.BlockSpec(memory_space=pltpu.SMEM)


def vmem(x):
    return pltpu.with_memory_space_constraint(x, pltpu.VMEM)


def partner_bits(count):
    bits = []
    b = count // 2
    while b:
        bits.append(b)
        b //= 2
    return bits


def swap(x, axes, count, bit):
    return lax.ppermute(x, axes, [(i, i ^ bit) for i in range(count)])


def payload_kernel(ep_count, hidden_ref, routes_ref, weight_ref, out_ref):
    rows, width = hidden_ref.shape
    out_ref[:, :width] = hidden_ref[...]
    column = lax.broadcasted_iota(jnp.int32, (rows, LANES), 1)
    expert = jnp.where(column < ep_count, column, column - ep_count)
    total = jnp.zeros((rows, LANES), f32)
    for k in range(routes_ref.shape[1]):
        total += jnp.where(routes_ref[:, k : k + 1] == expert, weight_ref[:, k : k + 1], 0.0)
    high = total.astype(bf16).astype(f32)
    low = total - high
    value = jnp.where(column < ep_count, high, jnp.where(column < 2 * ep_count, low, 0.0))
    out_ref[:, width:] = value.astype(bf16)


def make_payload(hidden, routes, route_weight, ep_count):
    rows, width = hidden.shape
    return pl.pallas_call(
        functools.partial(payload_kernel, ep_count),
        out_shape=jax.ShapeDtypeStruct((rows, width + LANES), bf16),
        in_specs=[in_vmem()] * 3,
        out_specs=in_vmem(),
        cost_estimate=pl.CostEstimate(flops=0, bytes_accessed=4 * rows * width, transcendentals=0),
    )(hidden, routes, route_weight)


def expert_kernel(ep_count, step, near_ref, far_ref, gate_ref, up_ref, down_ref, keep_ref, send_ref, gate_acc, up_acc):
    half = near_ref.shape[0]
    width, hidden_units = gate_ref.shape[1], gate_ref.shape[2]
    ep = lax.axis_index("ep")

    def rows_at(columns):
        return jnp.concatenate([near_ref[:, columns], far_ref[:, columns]], axis=0)

    table = rows_at(slice(width, width + LANES)).astype(f32)
    column = lax.broadcasted_iota(jnp.int32, table.shape, 1)
    mine = (column == ep) | (column == ep + ep_count)
    row_weight = jnp.sum(jnp.where(mine, table, 0.0), axis=1, keepdims=True)

    gate_acc[...] = jnp.zeros_like(gate_acc)
    up_acc[...] = jnp.zeros_like(up_acc)

    @pl.loop(0, width // step)
    def _(i):
        columns = pl.ds(pl.multiple_of(i * step, step), step)
        x = rows_at(columns)
        gate_acc[...] += jnp.dot(x, gate_ref[0, columns, :], preferred_element_type=f32)
        up_acc[...] += jnp.dot(x, up_ref[0, columns, :], preferred_element_type=f32)

    gate = gate_acc[...]
    inner = (gate / (1.0 + jnp.exp(-gate)) * up_acc[...]).astype(bf16)

    @pl.loop(0, width // step)
    def _(i):
        columns = pl.ds(pl.multiple_of(i * step, step), step)
        out = jnp.dot(inner, down_ref[0, :, columns], preferred_element_type=f32) * row_weight
        keep_ref[:, columns] = out[:half]
        send_ref[:, columns] = out[half:].astype(bf16)


def run_experts(near, far, gate_weight, up_weight, down_weight, ep_count):
    half = near.shape[0]
    width, units = gate_weight.shape[1], gate_weight.shape[2]
    step = 1024
    return pl.pallas_call(
        functools.partial(expert_kernel, ep_count, step),
        out_shape=(jax.ShapeDtypeStruct((half, width), f32), jax.ShapeDtypeStruct((half, width), bf16)),
        in_specs=[in_vmem()] * 5,
        out_specs=(in_vmem(), in_vmem()),
        scratch_shapes=[pltpu.VMEM((2 * half, units), f32), pltpu.VMEM((2 * half, units), f32)],
        compiler_params=pltpu.CompilerParams(vmem_limit_bytes=40 * MIB),
        cost_estimate=pl.CostEstimate(
            flops=12 * half * width * units, bytes_accessed=6 * width * units, transcendentals=2 * half * units
        ),
    )(near, far, vmem(gate_weight), vmem(up_weight), vmem(down_weight))


def pages_kernel(dp_count, page_ref, dest_ref, pool_ref, low_ref, high_ref):
    own, width = pool_ref.shape
    me = lax.axis_index("dp")
    slots = dp_count * MCAP
    row = lax.broadcasted_iota(jnp.int32, (slots, own), 0)
    column = lax.broadcasted_iota(jnp.int32, (slots, own), 1)
    pick = jnp.zeros((slots, own), f32)
    entries = page_ref.shape[1]
    for m in range(entries):
        rank = jnp.int32(0)
        for n in range(m):
            rank += jnp.where(dest_ref[0, n] == dest_ref[0, m], 1, 0)
        bucket = jnp.bitwise_xor(dest_ref[0, m], me) * MCAP + rank
        pick = jnp.where((row == bucket) & (column == page_ref[0, m]), 1.0, pick)
    pick = pick.astype(bf16)
    step = 2048

    @pl.loop(0, width // step)
    def _(i):
        columns = pl.ds(pl.multiple_of(i * step, step), step)
        out = jnp.dot(pick, pool_ref[:, columns], preferred_element_type=f32)
        low_ref[:, columns] = out[: slots // 2].astype(bf16)
        high_ref[:, columns] = out[slots // 2 :].astype(bf16)


def pick_pages(moved_page, moved_dest, latent_pool, dp_count):
    width = latent_pool.shape[1]
    half = jax.ShapeDtypeStruct((dp_count * MCAP // 2, width), bf16)
    return pl.pallas_call(
        functools.partial(pages_kernel, dp_count),
        out_shape=(half, half),
        in_specs=[in_smem(), in_smem(), in_vmem()],
        out_specs=(in_vmem(), in_vmem()),
        cost_estimate=pl.CostEstimate(flops=0, bytes_accessed=4 * latent_pool.size, transcendentals=0),
    )(moved_page, moved_dest, latent_pool)


def exchange_pages(low, high, dp_count):
    blocks, senders = [low], [0]
    sent = high
    for bit in partner_bits(dp_count):
        got = swap(sent, "dp", dp_count, bit)
        size = got.shape[0] // len(blocks)
        blocks = blocks + [got[i * size : (i + 1) * size] for i in range(len(blocks))]
        senders = senders + [s ^ bit for s in senders]
        if size > MCAP:
            sent = jnp.concatenate([b[size // 2 :] for b in blocks], axis=0)
            blocks = [b[: size // 2] for b in blocks]
    return jnp.concatenate(blocks, axis=0), senders


def attend_kernel(senders, length_ref, table_ref, query_ref, pool_ref, arrived_ref, out_ref, query_rows):
    rows_dev = query_ref.shape[0]
    own, width = pool_ref.shape
    arrived = arrived_ref.shape[0]
    slots = -(-(own + arrived) // 16) * 16
    pair_width = 2 * LAT
    pairs = width // pair_width
    me = lax.axis_index("dp")

    for h in range(HEADS // 2):
        query_rows[h * rows_dev : (h + 1) * rows_dev, :] = query_ref[:, h * pair_width : (h + 1) * pair_width].astype(f32)
    straight = query_rows[...]
    turned = pltpu.roll(straight, LAT, 1)
    first = lax.broadcasted_iota(jnp.int32, straight.shape, 1) < LAT
    query_all = jnp.concatenate(
        [
            jnp.where(first, straight, 0.0),
            jnp.where(first, turned, 0.0),
            jnp.where(first, 0.0, turned),
            jnp.where(first, 0.0, straight),
        ],
        axis=0,
    ).astype(bf16)

    pieces = []
    for j in range(pairs):
        columns = slice(j * pair_width, (j + 1) * pair_width)
        parts = [pool_ref[:, columns].astype(f32), arrived_ref[:, columns].astype(f32)]
        if slots > own + arrived:
            parts.append(jnp.zeros((slots - own - arrived, pair_width), f32))
        pieces.append(jnp.concatenate(parts, axis=0).astype(bf16))
    keys = jnp.concatenate(pieces, axis=0)

    scores = lax.dot_general(query_all, keys, (((1,), (1,)), ((), ())), preferred_element_type=f32) * score_scale

    column = lax.broadcasted_iota(jnp.int32, (1, pairs * slots), 1)
    pair = column // slots
    place = column - pair * slots
    slot = place
    for i, s in enumerate(senders):
        source = jnp.bitwise_xor(me, s)
        for k in range(MCAP):
            slot = jnp.where(place == own + i * MCAP + k, own + source * MCAP + k, slot)
    limits = []
    for r in range(rows_dev):
        limit = jnp.full(column.shape, -1, jnp.int32)
        for p in range(table_ref.shape[1]):
            limit = jnp.where(slot == table_ref[r, p], length_ref[r] - p * PAGE, limit)
        limit = jnp.where(place < own + arrived, limit, -1)
        limits.append(limit - 2 * pair)
    half = scores.shape[0] // 2
    row = lax.broadcasted_iota(jnp.int32, (half, 1), 0) % rows_dev
    limit = limits[0]
    for r in range(1, rows_dev):
        limit = jnp.where(row == r, limits[r], limit)
    even = jnp.where(limit > 0, scores[:half], -jnp.inf)
    odd = jnp.where(limit > 1, scores[half:], -jnp.inf)
    peak = jnp.maximum(jnp.max(even, axis=1, keepdims=True), jnp.max(odd, axis=1, keepdims=True))
    even = jnp.exp(even - peak)
    odd = jnp.exp(odd - peak)
    total = jnp.sum(even, axis=1, keepdims=True) + jnp.sum(odd, axis=1, keepdims=True)
    even = (even / total).astype(bf16)
    odd = (odd / total).astype(bf16)
    from_even = jnp.dot(even, keys[:, :VL], preferred_element_type=f32)
    from_odd = jnp.dot(odd, keys[:, VL:], preferred_element_type=f32)
    shift = LAT - VL
    wide = pair_width - VL
    attended = from_even + pltpu.roll(from_odd, wide - shift, 1)[:, :VL]
    for h in range(HEADS):
        at = (h % 2) * (half // 2) + (h // 2) * rows_dev
        out_ref[:, h * VL : (h + 1) * VL] = attended[at : at + rows_dev].astype(bf16)


def attend(lengths, page_table, queries, latent_pool, arrived, senders):
    rows_dev = queries.shape[0]
    return pl.pallas_call(
        functools.partial(attend_kernel, senders),
        out_shape=jax.ShapeDtypeStruct((rows_dev, HEADS * VL), bf16),
        in_specs=[in_smem(), in_smem(), in_vmem(), in_vmem(), in_vmem()],
        out_specs=in_vmem(),
        scratch_shapes=[pltpu.VMEM((HEADS // 2 * rows_dev, 2 * LAT), f32)],
        compiler_params=pltpu.CompilerParams(vmem_limit_bytes=24 * MIB),
        cost_estimate=pl.CostEstimate(flops=1 << 30, bytes_accessed=4 << 20, transcendentals=1 << 17),
    )(lengths, page_table, queries, latent_pool, arrived)


def body(
    hidden,
    routes,
    route_weight,
    gate_weight,
    up_weight,
    down_weight,
    queries,
    latent_pool,
    lengths,
    page_table,
    moved_page,
    moved_dest,
):
    ep_count = lax.axis_size("ep")
    dp_count = lax.axis_size("dp")
    count = ep_count * dp_count
    bits = partner_bits(count)

    near = make_payload(hidden, routes, route_weight, ep_count)
    for bit in bits[:-1]:
        near = jnp.concatenate([near, swap(near, AXES, count, bit)], axis=0)
    far = swap(near, AXES, count, bits[-1])

    low, high = pick_pages(moved_page, moved_dest, latent_pool, dp_count)
    arrived, senders = exchange_pages(low, high, dp_count)
    attended = attend(lengths, page_table, queries, latent_pool, arrived, senders)

    keep, send = run_experts(near, far, gate_weight, up_weight, down_weight, ep_count)
    for bit in reversed(bits):
        keep = keep + swap(send, AXES, count, bit).astype(f32)
        half = keep.shape[0] // 2
        if bit != bits[0]:
            send = keep[half:].astype(bf16)
            keep = keep[:half]
    return keep.astype(bf16), attended


def solution(mesh):
    rows = P(("inst", "ep", "dp"), None)
    in_specs = (
        rows,
        rows,
        rows,
        P("ep", None, "dp"),
        P("ep", None, "dp"),
        P("ep", "dp", None),
        rows,
        rows,
        P(("inst", "ep", "dp")),
        rows,
        rows,
        rows,
    )
    return jax.shard_map(body, mesh=mesh, in_specs=in_specs, out_specs=(rows, rows), check_vma=False)
```

```python
import functools

import jax
import jax.numpy as jnp
from jax import lax
from jax.experimental import pallas as pl
from jax.experimental.pallas import tpu as pltpu
from jax.sharding import PartitionSpec as P

HEADS = 64
LAT = 576
VL = 512
MCAP = 2
PAGE = 32
LANES = 128
AXES = ("ep", "dp")
MIB = 1 << 20

score_scale = 192.0 ** (-0.5)
bf16 = jnp.bfloat16
f32 = jnp.float32


def in_vmem():
    return pl.BlockSpec(memory_space=pltpu.VMEM)


def in_smem():
    return pl.BlockSpec(memory_space=pltpu.SMEM)


def vmem(x):
    return pltpu.with_memory_space_constraint(x, pltpu.VMEM)


def hbm(x):
    return pltpu.with_memory_space_constraint(x, pltpu.HBM)


def anywhere():
    return pl.BlockSpec(memory_space=pl.ANY)


def in_hbm():
    return pl.BlockSpec(memory_space=pltpu.HBM)


def partner_bits(count):
    bits = []
    b = count // 2
    while b:
        bits.append(b)
        b //= 2
    return bits


def swap(x, axes, pairs):
    return lax.ppermute(x, axes, pairs)


def stage_pairs(count, stage):
    bits = partner_bits(count)[:-1]
    turned = bits[:-2] + [bits[-1], bits[-2]]
    return [(i, i ^ (turned if i & 1 else bits)[stage]) for i in range(count)]


def core_pairs(count):
    return [(i, i ^ 1) for i in range(count)]


def payload_kernel(ep_count, hidden_hbm, routes_hbm, weight_hbm, mine_ref, other_ref, hidden_ref, routes_ref, weight_ref, sems):
    copies = [
        pltpu.make_async_copy(source, target, sems.at[i])
        for i, (source, target) in enumerate(
            [(hidden_hbm, hidden_ref), (routes_hbm, routes_ref), (weight_hbm, weight_ref)]
        )
    ]
    for c in copies:
        c.start()
    for c in copies:
        c.wait()
    rows, width = hidden_ref.shape
    half = width // 2
    column = lax.broadcasted_iota(jnp.int32, (rows, LANES), 1)
    expert = jnp.where(column < ep_count, column, column - ep_count)
    total = jnp.zeros((rows, LANES), f32)
    for k in range(routes_ref.shape[1]):
        total += jnp.where(routes_ref[:, k : k + 1] == expert, weight_ref[:, k : k + 1], 0.0)
    high = total.astype(bf16).astype(f32)
    low = total - high
    value = jnp.where(column < ep_count, high, jnp.where(column < 2 * ep_count, low, 0.0)).astype(bf16)
    first = lax.rem(lax.axis_index("dp"), 2) == 0
    left, right = hidden_ref[:, :half].astype(f32), hidden_ref[:, half:].astype(f32)
    mine_ref[:, :half] = jnp.where(first, left, right).astype(bf16)
    other_ref[:, :half] = jnp.where(first, right, left).astype(bf16)
    mine_ref[:, half:] = value
    other_ref[:, half:] = value


def make_payload(hidden, routes, route_weight, ep_count):
    rows, width = hidden.shape
    half = pltpu.VMEM((rows, width // 2 + LANES), bf16)
    return pl.pallas_call(
        functools.partial(payload_kernel, ep_count),
        out_shape=(half, half),
        in_specs=[in_hbm()] * 3,
        out_specs=(in_vmem(), in_vmem()),
        scratch_shapes=[
            pltpu.VMEM(hidden.shape, bf16),
            pltpu.VMEM(routes.shape, jnp.int32),
            pltpu.VMEM(route_weight.shape, f32),
            pltpu.SemaphoreType.DMA((3,)),
        ],
        compiler_params=pltpu.CompilerParams(vmem_limit_bytes=4 * MIB),
        cost_estimate=pl.CostEstimate(flops=0, bytes_accessed=4 * rows * width, transcendentals=0),
    )(hbm(hidden), hbm(routes), hbm(route_weight))


def merge_kernel(by_core, near_ref, got_ref, *rest):
    out_ref = rest[-1]
    rows = near_ref.shape[0]
    if rows % 16:
        near, got = near_ref[...].astype(f32), got_ref[...].astype(f32)
        both = jnp.concatenate([near, got], axis=0)
        if by_core:
            first = lax.rem(lax.axis_index("dp"), 2) == 0
            both = jnp.where(first, both, jnp.concatenate([got, near], axis=0))
        out_ref[...] = both.astype(bf16)
    else:
        out_ref[:rows] = near_ref[...]
        out_ref[rows:] = got_ref[...]


def merge(near, got, *after, by_core=False):
    rows, width = near.shape
    return pl.pallas_call(
        functools.partial(merge_kernel, by_core),
        out_shape=pltpu.VMEM((2 * rows, width), bf16),
        in_specs=[in_vmem(), in_vmem()] + [anywhere()] * len(after),
        out_specs=in_vmem(),
        compiler_params=pltpu.CompilerParams(vmem_limit_bytes=4 * MIB),
        cost_estimate=pl.CostEstimate(flops=0, bytes_accessed=8 * rows * width, transcendentals=0),
    )(vmem(near), vmem(got), *after)


def half_start(width, near):
    core = lax.rem(lax.axis_index("dp"), 2)
    core = core if near else 1 - core
    return pl.multiple_of(core * (width // 2), width // 2)


def load_kernel(pieces, *refs):
    sources = refs[: len(pieces)]
    outs = refs[len(pieces) + 1 : -1]
    sems = refs[-1]
    copies = []
    for i, (near, source, out) in enumerate(zip(pieces, sources, outs)):
        rows = source.shape[1] // 2
        copies.append(
            pltpu.make_async_copy(source.at[0, pl.ds(half_start(source.shape[1], near), rows)], out, sems.at[i])
        )
    for c in copies:
        c.start()
    for c in copies:
        c.wait()


def load_halves(after, *requests):
    weights = [w for w, _ in requests]
    pieces = [near for _, near in requests]
    out = tuple(pltpu.VMEM((w.shape[1] // 2, w.shape[2]), bf16) for w in weights)
    return pl.pallas_call(
        functools.partial(load_kernel, pieces),
        out_shape=out,
        in_specs=[in_hbm()] * len(weights) + [anywhere()],
        out_specs=(in_vmem(),) * len(weights),
        scratch_shapes=[pltpu.SemaphoreType.DMA((len(weights),))],
        compiler_params=pltpu.CompilerParams(vmem_limit_bytes=4 * MIB),
        cost_estimate=pl.CostEstimate(flops=0, bytes_accessed=sum(w.size for w in weights), transcendentals=0),
    )(*[hbm(w) for w in weights], after)


def near_kernel(near_ref, gate_ref, up_ref, down_ref, gate_out, up_out, down_out, sem):
    width = down_ref.shape[2]
    copy = pltpu.make_async_copy(down_ref.at[0, :, pl.ds(half_start(width, False), width // 2)], down_out, sem)
    copy.start()
    x = near_ref[:, : width // 2]
    gate_out[...] = jnp.dot(x, gate_ref[...], preferred_element_type=f32)
    up_out[...] = jnp.dot(x, up_ref[...], preferred_element_type=f32)
    copy.wait()


def far_kernel(
    ep_count, near_ref, far_ref, gate_ref, up_ref, gate_in, up_in, down_far_ref, down_ref, inner_ref, send_ref, down_out, sem
):
    width = down_ref.shape[2]
    half = width // 2
    copy = pltpu.make_async_copy(down_ref.at[0, :, pl.ds(half_start(width, True), half)], down_out, sem)
    copy.start()
    rows = near_ref.shape[0]
    quarter = rows // 4

    def turn(x):
        return jnp.concatenate([x[:quarter], x[2 * quarter : 3 * quarter], x[quarter : 2 * quarter], x[3 * quarter :]], axis=0)

    ep = lax.axis_index("ep")
    table = near_ref[:, half:].astype(f32)
    column = lax.broadcasted_iota(jnp.int32, table.shape, 1)
    mine = (column == ep) | (column == ep + ep_count)
    row_weight = jnp.sum(jnp.where(mine, table, 0.0), axis=1, keepdims=True)
    x = turn(far_ref[:, :half])
    gate = gate_in[...] + jnp.dot(x, gate_ref[...], preferred_element_type=f32)
    up = up_in[...] + jnp.dot(x, up_ref[...], preferred_element_type=f32)
    inner = (gate / (1.0 + jnp.exp(-gate)) * up).astype(bf16)
    inner_ref[...] = inner
    step = half // 7

    @pl.loop(0, half // step)
    def _(i):
        columns = pl.ds(pl.multiple_of(i * step, step), step)
        out = jnp.dot(inner, down_far_ref[:, columns], preferred_element_type=f32) * row_weight
        send_ref[:, columns] = turn(out).astype(bf16)

    copy.wait()


def keep_kernel(ep_count, near_ref, inner_ref, down_ref, keep_ref):
    half = down_ref.shape[1]
    ep = lax.axis_index("ep")
    table = near_ref[:, half:].astype(f32)
    column = lax.broadcasted_iota(jnp.int32, table.shape, 1)
    mine = (column == ep) | (column == ep + ep_count)
    row_weight = jnp.sum(jnp.where(mine, table, 0.0), axis=1, keepdims=True)
    step = half // 7
    inner = inner_ref[...]

    @pl.loop(0, half // step)
    def _(i):
        columns = pl.ds(pl.multiple_of(i * step, step), step)
        keep_ref[:, columns] = jnp.dot(inner, down_ref[:, columns], preferred_element_type=f32) * row_weight


def estimate(rows, weights):
    return pl.CostEstimate(flops=2 * rows * weights, bytes_accessed=2 * weights, transcendentals=0)


def near_products(near, gate_near, up_near, down_weight):
    rows = near.shape[0]
    units, width = down_weight.shape[1:]
    acc = pltpu.VMEM((rows, units), f32)
    return pl.pallas_call(
        near_kernel,
        out_shape=(acc, acc, pltpu.VMEM((units, width // 2), bf16)),
        in_specs=[in_vmem()] * 3 + [in_hbm()],
        out_specs=(in_vmem(),) * 3,
        scratch_shapes=[pltpu.SemaphoreType.DMA],
        compiler_params=pltpu.CompilerParams(vmem_limit_bytes=12 * MIB),
        cost_estimate=estimate(rows, width * units),
    )(vmem(near), vmem(gate_near), vmem(up_near), hbm(down_weight))


def far_products(near, far, gate_far, up_far, gate_acc, up_acc, down_far, down_weight, ep_count):
    rows = near.shape[0]
    units, width = down_weight.shape[1:]
    half = width // 2
    return pl.pallas_call(
        functools.partial(far_kernel, ep_count),
        out_shape=(pltpu.VMEM((rows, units), bf16), pltpu.VMEM((rows, half), bf16), pltpu.VMEM((units, half), bf16)),
        in_specs=[in_vmem()] * 7 + [in_hbm()],
        out_specs=(in_vmem(),) * 3,
        scratch_shapes=[pltpu.SemaphoreType.DMA],
        compiler_params=pltpu.CompilerParams(vmem_limit_bytes=12 * MIB),
        cost_estimate=estimate(rows, 3 * half * units),
    )(
        vmem(near),
        vmem(far),
        vmem(gate_far),
        vmem(up_far),
        vmem(gate_acc),
        vmem(up_acc),
        vmem(down_far),
        hbm(down_weight),
    )


def keep_products(near, inner, down_near, ep_count):
    rows = near.shape[0]
    units, half = down_near.shape
    return pl.pallas_call(
        functools.partial(keep_kernel, ep_count),
        out_shape=pltpu.VMEM((rows, half), f32),
        in_specs=[in_vmem()] * 3,
        out_specs=in_vmem(),
        compiler_params=pltpu.CompilerParams(vmem_limit_bytes=8 * MIB),
        cost_estimate=estimate(rows, half * units),
    )(vmem(near), vmem(inner), vmem(down_near))


def fold_kernel(by_core, keep_ref, got_ref, *rest):
    keep_out, send_out = rest[-2:]
    half = keep_out.shape[0]
    upper = keep_ref[:half] + got_ref[:half].astype(f32)
    lower = keep_ref[half:] + got_ref[half:].astype(f32)
    if by_core:
        first = lax.rem(lax.axis_index("dp"), 2) == 0
        upper, lower = jnp.where(first, upper, lower), jnp.where(first, lower, upper)
    keep_out[...] = upper
    send_out[...] = lower.astype(bf16)


def fold(keep, got, *after, by_core=False):
    rows, width = keep.shape
    return pl.pallas_call(
        functools.partial(fold_kernel, by_core),
        out_shape=(pltpu.VMEM((rows // 2, width), f32), pltpu.VMEM((rows // 2, width), bf16)),
        in_specs=[in_vmem(), in_vmem()] + [anywhere()] * len(after),
        out_specs=(in_vmem(), in_vmem()),
        compiler_params=pltpu.CompilerParams(vmem_limit_bytes=4 * MIB),
        cost_estimate=pl.CostEstimate(flops=0, bytes_accessed=8 * rows * width, transcendentals=0),
    )(vmem(keep), vmem(got), *after)


def finish_kernel(keep_ref, got_ref, out_ref):
    half = keep_ref.shape[1]
    first = lax.rem(lax.axis_index("dp"), 2) == 0
    keep, got = keep_ref[...], got_ref[...].astype(f32)
    out_ref[:, :half] = jnp.where(first, keep, got).astype(bf16)
    out_ref[:, half:] = jnp.where(first, got, keep).astype(bf16)


def finish(keep, got):
    rows, half = keep.shape
    return pl.pallas_call(
        finish_kernel,
        out_shape=jax.ShapeDtypeStruct((rows, 2 * half), bf16),
        in_specs=[in_vmem(), in_vmem()],
        out_specs=in_vmem(),
        compiler_params=pltpu.CompilerParams(vmem_limit_bytes=4 * MIB),
        cost_estimate=pl.CostEstimate(flops=0, bytes_accessed=8 * rows * half, transcendentals=0),
    )(vmem(keep), vmem(got))


def pages_kernel(
    dp_count, page_hbm, dest_hbm, pool_ref, gate_ref, after_ref, low_ref, high_ref, copy_ref, gate_out, page_ref, dest_ref, sems
):
    own, width = pool_ref.shape
    depth = gate_ref.shape[1]
    pool_copy = pltpu.make_async_copy(pool_ref, copy_ref, sems.at[0])
    page_copy = pltpu.make_async_copy(page_hbm, page_ref, sems.at[2])
    dest_copy = pltpu.make_async_copy(dest_hbm, dest_ref, sems.at[3])
    page_copy.start()
    dest_copy.start()
    pool_copy.start()
    gate_copy = pltpu.make_async_copy(
        gate_ref.at[0, pl.ds(half_start(depth, True), depth // 2)], gate_out, sems.at[1]
    )
    gate_copy.start()
    page_copy.wait()
    dest_copy.wait()
    me = lax.axis_index("dp")
    slots = dp_count * MCAP
    row = lax.broadcasted_iota(jnp.int32, (slots, own), 0)
    column = lax.broadcasted_iota(jnp.int32, (slots, own), 1)
    pick = jnp.zeros((slots, own), f32)
    entries = page_ref.shape[1]
    for m in range(entries):
        rank = jnp.int32(0)
        for n in range(m):
            rank += jnp.where(dest_ref[0, n] == dest_ref[0, m], 1, 0)
        bucket = jnp.bitwise_xor(dest_ref[0, m], me) * MCAP + rank
        pick = jnp.where((row == bucket) & (column == page_ref[0, m]), 1.0, pick)
    pick = pick.astype(bf16)
    step = 2048
    pool_copy.wait()
    for i in range(width // step):
        columns = slice(i * step, (i + 1) * step)
        out = jnp.dot(pick, copy_ref[:, columns], preferred_element_type=f32)
        low_ref[:, columns] = out[: slots // 2].astype(bf16)
        high_ref[:, columns] = out[slots // 2 :].astype(bf16)
    gate_copy.wait()


def pick_pages(moved_page, moved_dest, latent_pool, gate_weight, after, dp_count):
    width = latent_pool.shape[1]
    half = pltpu.VMEM((dp_count * MCAP // 2, width), bf16)
    depth, units = gate_weight.shape[1:]
    return pl.pallas_call(
        functools.partial(pages_kernel, dp_count),
        out_shape=(half, half, pltpu.VMEM(latent_pool.shape, bf16), pltpu.VMEM((depth // 2, units), bf16)),
        in_specs=[in_hbm()] * 4 + [anywhere()],
        out_specs=(in_vmem(),) * 4,
        scratch_shapes=[
            pltpu.SMEM(moved_page.shape, jnp.int32),
            pltpu.SMEM(moved_dest.shape, jnp.int32),
            pltpu.SemaphoreType.DMA((4,)),
        ],
        compiler_params=pltpu.CompilerParams(vmem_limit_bytes=4 * MIB),
        cost_estimate=pl.CostEstimate(flops=0, bytes_accessed=4 * latent_pool.size + gate_weight.size, transcendentals=0),
    )(hbm(moved_page), hbm(moved_dest), hbm(latent_pool), hbm(gate_weight), after)


def exchange_pages(low, high, dp_count):
    blocks, senders = [low], [0]
    sent = high
    for bit in partner_bits(dp_count):
        got = swap(sent, "dp", [(i, i ^ bit) for i in range(dp_count)])
        size = got.shape[0] // len(blocks)
        blocks = blocks + [got[i * size : (i + 1) * size] for i in range(len(blocks))]
        senders = senders + [s ^ bit for s in senders]
        if size > MCAP:
            sent = jnp.concatenate([b[size // 2 :] for b in blocks], axis=0)
            blocks = [b[: size // 2] for b in blocks]
    return jnp.concatenate(blocks, axis=0), senders


def attend_kernel(senders, length_ref, table_ref, query_ref, pool_ref, arrived_ref, out_ref, query_rows):
    rows_dev = query_ref.shape[0]
    own, width = pool_ref.shape
    arrived = arrived_ref.shape[0]
    slots = -(-(own + arrived) // 16) * 16
    pair_width = 2 * LAT
    pairs = width // pair_width
    me = lax.axis_index("dp")

    for h in range(HEADS // 2):
        query_rows[h * rows_dev : (h + 1) * rows_dev, :] = query_ref[:, h * pair_width : (h + 1) * pair_width].astype(f32)
    straight = query_rows[...]
    turned = pltpu.roll(straight, LAT, 1)
    first = lax.broadcasted_iota(jnp.int32, straight.shape, 1) < LAT
    query_all = jnp.concatenate(
        [
            jnp.where(first, straight, 0.0),
            jnp.where(first, turned, 0.0),
            jnp.where(first, 0.0, turned),
            jnp.where(first, 0.0, straight),
        ],
        axis=0,
    ).astype(bf16)

    pieces = []
    for j in range(pairs):
        columns = slice(j * pair_width, (j + 1) * pair_width)
        parts = [pool_ref[:, columns].astype(f32), arrived_ref[:, columns].astype(f32)]
        if slots > own + arrived:
            parts.append(jnp.zeros((slots - own - arrived, pair_width), f32))
        pieces.append(jnp.concatenate(parts, axis=0).astype(bf16))
    keys = jnp.concatenate(pieces, axis=0)

    scores = lax.dot_general(query_all, keys, (((1,), (1,)), ((), ())), preferred_element_type=f32) * score_scale

    column = lax.broadcasted_iota(jnp.int32, (1, pairs * slots), 1)
    pair = column // slots
    place = column - pair * slots
    slot = place
    for i, s in enumerate(senders):
        source = jnp.bitwise_xor(me, s)
        for k in range(MCAP):
            slot = jnp.where(place == own + i * MCAP + k, own + source * MCAP + k, slot)
    limits = []
    for r in range(rows_dev):
        limit = jnp.full(column.shape, -1, jnp.int32)
        for p in range(table_ref.shape[1]):
            limit = jnp.where(slot == table_ref[r, p], length_ref[r] - p * PAGE, limit)
        limit = jnp.where(place < own + arrived, limit, -1)
        limits.append(limit - 2 * pair)
    half = scores.shape[0] // 2
    row = lax.broadcasted_iota(jnp.int32, (half, 1), 0) % rows_dev
    limit = limits[0]
    for r in range(1, rows_dev):
        limit = jnp.where(row == r, limits[r], limit)
    even = jnp.where(limit > 0, scores[:half], -jnp.inf)
    odd = jnp.where(limit > 1, scores[half:], -jnp.inf)
    peak = jnp.maximum(jnp.max(even, axis=1, keepdims=True), jnp.max(odd, axis=1, keepdims=True))
    even = jnp.exp(even - peak)
    odd = jnp.exp(odd - peak)
    total = jnp.sum(even, axis=1, keepdims=True) + jnp.sum(odd, axis=1, keepdims=True)
    even = (even / total).astype(bf16)
    odd = (odd / total).astype(bf16)
    from_even = jnp.dot(even, keys[:, :VL], preferred_element_type=f32)
    from_odd = jnp.dot(odd, keys[:, VL:], preferred_element_type=f32)
    shift = LAT - VL
    wide = pair_width - VL
    attended = from_even + pltpu.roll(from_odd, wide - shift, 1)[:, :VL]
    for h in range(HEADS):
        at = (h % 2) * (half // 2) + (h // 2) * rows_dev
        out_ref[:, h * VL : (h + 1) * VL] = attended[at : at + rows_dev].astype(bf16)


def attend(lengths, page_table, queries, latent_pool, arrived, senders):
    rows_dev = queries.shape[0]
    return pl.pallas_call(
        functools.partial(attend_kernel, senders),
        out_shape=jax.ShapeDtypeStruct((rows_dev, HEADS * VL), bf16),
        in_specs=[in_smem(), in_smem(), in_vmem(), in_vmem(), in_vmem()],
        out_specs=in_vmem(),
        scratch_shapes=[pltpu.VMEM((HEADS // 2 * rows_dev, 2 * LAT), f32)],
        compiler_params=pltpu.CompilerParams(vmem_limit_bytes=16 * MIB),
        cost_estimate=pl.CostEstimate(flops=1 << 30, bytes_accessed=4 << 20, transcendentals=1 << 17),
    )(lengths, page_table, queries, vmem(latent_pool), vmem(arrived))


def body(
    hidden,
    routes,
    route_weight,
    gate_weight,
    up_weight,
    down_weight,
    queries,
    latent_pool,
    lengths,
    page_table,
    moved_page,
    moved_dest,
):
    ep_count = lax.axis_size("ep")
    dp_count = lax.axis_size("dp")
    count = ep_count * dp_count
    stages = len(partner_bits(count)) - 1
    cores = core_pairs(count)

    mine, other = make_payload(hidden, routes, route_weight, ep_count)
    near = merge(mine, swap(other, AXES, cores), by_core=True)
    for stage in range(stages):
        got = swap(near, AXES, stage_pairs(count, stage))
        if stage == 0:
            low, high, pool, gate_near = pick_pages(moved_page, moved_dest, latent_pool, gate_weight, near, dp_count)
            loaded = [high]
        elif stage == 1:
            loaded = load_halves(near, (up_weight, True))
            (up_near,) = loaded
        elif stage == 2:
            loaded = load_halves(near, (gate_weight, False))
            (gate_far,) = loaded
        elif stage == 3:
            loaded = load_halves(near, (up_weight, False))
            (up_far,) = loaded
        else:
            loaded = []
        near = merge(near, got, *loaded)
    arrived, senders = exchange_pages(low, high, dp_count)
    far = swap(near, AXES, cores)
    gate_acc, up_acc, down_far = near_products(near, gate_near, up_near, down_weight)
    inner, send, down_near = far_products(
        near, far, gate_far, up_far, gate_acc, up_acc, down_far, down_weight, ep_count
    )
    got = swap(send, AXES, cores)
    keep = keep_products(near, inner, down_near, ep_count)
    keep, send = fold(keep, got)
    attended = attend(lengths, page_table, queries, pool, arrived, senders)
    for stage in reversed(range(stages)):
        got = swap(send, AXES, stage_pairs(count, stage))
        after = [hbm(attended)] if stage == stages - 1 else []
        keep, send = fold(keep, got, *after, by_core=stage == 0)
    return finish(keep, swap(send, AXES, cores)), attended


def solution(mesh):
    rows = P(("inst", "ep", "dp"), None)
    in_specs = (
        rows,
        rows,
        rows,
        P("ep", None, "dp"),
        P("ep", None, "dp"),
        P("ep", "dp", None),
        rows,
        rows,
        P(("inst", "ep", "dp")),
        rows,
        rows,
        rows,
    )
    return jax.shard_map(body, mesh=mesh, in_specs=in_specs, out_specs=(rows, rows), check_vma=False)
```

```python
import functools

import jax
import jax.numpy as jnp
from jax import lax
from jax.experimental import pallas as pl
from jax.experimental.pallas import tpu as pltpu
from jax.sharding import PartitionSpec as P

HEADS = 64
LAT = 576
VL = 512
MCAP = 2
PAGE = 32
LANES = 128
AXES = ("ep", "dp")
MIB = 1 << 20
MERGE_FLOPS = 20_000_000_000

score_scale = 192.0 ** (-0.5)
bf16 = jnp.bfloat16
f32 = jnp.float32


def in_vmem():
    return pl.BlockSpec(memory_space=pltpu.VMEM)


def in_smem():
    return pl.BlockSpec(memory_space=pltpu.SMEM)


def vmem(x):
    return pltpu.with_memory_space_constraint(x, pltpu.VMEM)


def hbm(x):
    return pltpu.with_memory_space_constraint(x, pltpu.HBM)


def anywhere():
    return pl.BlockSpec(memory_space=pl.ANY)


def in_hbm():
    return pl.BlockSpec(memory_space=pltpu.HBM)


def partner_bits(count):
    bits = []
    b = count // 2
    while b:
        bits.append(b)
        b //= 2
    return bits


def swap(x, axes, pairs):
    return lax.ppermute(x, axes, pairs)


def stage_partners(count):
    bits = partner_bits(count)[:-1]
    stages = [(bits[0],)] if len(bits) % 2 else []
    bits = bits[len(bits) % 2 :]
    for high, low in zip(bits[::2], bits[1::2]):
        stages.append((low, high, high ^ low))
    return stages


def pairs_of(count, bit):
    return [(i, i ^ bit) for i in range(count)]


def payload_kernel(ep_count, hidden_hbm, routes_hbm, weight_hbm, mine_ref, other_ref, hidden_ref, routes_ref, weight_ref, sems):
    copies = [
        pltpu.make_async_copy(source, target, sems.at[i])
        for i, (source, target) in enumerate(
            [(hidden_hbm, hidden_ref), (routes_hbm, routes_ref), (weight_hbm, weight_ref)]
        )
    ]
    for c in copies:
        c.start()
    for c in copies:
        c.wait()
    rows, width = hidden_ref.shape
    half = width // 2
    column = lax.broadcasted_iota(jnp.int32, (rows, LANES), 1)
    expert = jnp.where(column < ep_count, column, column - ep_count)
    total = jnp.zeros((rows, LANES), f32)
    for k in range(routes_ref.shape[1]):
        total += jnp.where(routes_ref[:, k : k + 1] == expert, weight_ref[:, k : k + 1], 0.0)
    high = total.astype(bf16).astype(f32)
    low = total - high
    value = jnp.where(column < ep_count, high, jnp.where(column < 2 * ep_count, low, 0.0)).astype(bf16)
    first = lax.rem(lax.axis_index("dp"), 2) == 0
    left, right = hidden_ref[:, :half].astype(f32), hidden_ref[:, half:].astype(f32)
    mine_ref[:, :half] = jnp.where(first, left, right).astype(bf16)
    other_ref[:, :half] = jnp.where(first, right, left).astype(bf16)
    mine_ref[:, half:] = value
    other_ref[:, half:] = value


def make_payload(hidden, routes, route_weight, ep_count):
    rows, width = hidden.shape
    half = pltpu.VMEM((rows, width // 2 + LANES), bf16)
    return pl.pallas_call(
        functools.partial(payload_kernel, ep_count),
        out_shape=(half, half),
        in_specs=[in_hbm()] * 3,
        out_specs=(in_vmem(), in_vmem()),
        scratch_shapes=[
            pltpu.VMEM(hidden.shape, bf16),
            pltpu.VMEM(routes.shape, jnp.int32),
            pltpu.VMEM(route_weight.shape, f32),
            pltpu.SemaphoreType.DMA((3,)),
        ],
        compiler_params=pltpu.CompilerParams(vmem_limit_bytes=4 * MIB),
        cost_estimate=pl.CostEstimate(flops=0, bytes_accessed=4 * rows * width, transcendentals=0),
    )(hbm(hidden), hbm(routes), hbm(route_weight))


def merge_kernel(by_core, parts, *refs):
    out_ref = refs[-1]
    rows = refs[0].shape[0]
    if rows % 16:
        pieces = [r[...].astype(f32) for r in refs[:parts]]
        both = jnp.concatenate(pieces, axis=0)
        if by_core:
            first = lax.rem(lax.axis_index("dp"), 2) == 0
            both = jnp.where(first, both, jnp.concatenate(pieces[::-1], axis=0))
        out_ref[...] = both.astype(bf16)
    else:
        for i in range(parts):
            out_ref[i * rows : (i + 1) * rows] = refs[i][...]


def merge(pieces, *after, by_core=False):
    rows, width = pieces[0].shape
    return pl.pallas_call(
        functools.partial(merge_kernel, by_core, len(pieces)),
        out_shape=pltpu.VMEM((len(pieces) * rows, width), bf16),
        in_specs=[in_vmem()] * len(pieces) + [anywhere()] * len(after),
        out_specs=in_vmem(),
        compiler_params=pltpu.CompilerParams(vmem_limit_bytes=4 * MIB),
        cost_estimate=pl.CostEstimate(flops=MERGE_FLOPS, bytes_accessed=8 * MIB, transcendentals=0),
    )(*[vmem(p) for p in pieces], *after)


def half_start(width, near):
    core = lax.rem(lax.axis_index("dp"), 2)
    core = core if near else 1 - core
    return pl.multiple_of(core * (width // 2), width // 2)


def near_kernel(near_ref, gate_ref, up_ref, gate_out, up_out):
    width = gate_ref.shape[1]
    at = pl.ds(half_start(width, True), width // 2)
    x = near_ref[:, : width // 2]
    gate_out[...] = jnp.dot(x, gate_ref[0, at, :], preferred_element_type=f32)
    up_out[...] = jnp.dot(x, up_ref[0, at, :], preferred_element_type=f32)


def row_weights(near_ref, half, ep_count):
    ep = lax.axis_index("ep")
    table = near_ref[:, half:].astype(f32)
    column = lax.broadcasted_iota(jnp.int32, table.shape, 1)
    mine = (column == ep) | (column == ep + ep_count)
    return jnp.sum(jnp.where(mine, table, 0.0), axis=1, keepdims=True)


STEPS = 7


def far_kernel(ep_count, near_ref, far_ref, gate_ref, up_ref, gate_in, up_in, down_ref, inner_ref, send_ref):
    width = gate_ref.shape[1]
    half = width // 2
    start = half_start(width, False)
    at = pl.ds(start, half)
    row_weight = row_weights(near_ref, half, ep_count)
    x = far_ref[:, :half]
    gate = gate_in[...] + jnp.dot(x, gate_ref[0, at, :], preferred_element_type=f32)
    up = up_in[...] + jnp.dot(x, up_ref[0, at, :], preferred_element_type=f32)
    inner = (gate / (1.0 + jnp.exp(-gate)) * up).astype(bf16)
    inner_ref[...] = inner
    step = half // STEPS
    for i in range(STEPS):
        columns = pl.ds(pl.multiple_of(start + i * step, step), step)
        out = jnp.dot(inner, down_ref[0, :, columns], preferred_element_type=f32) * row_weight
        send_ref[:, i * step : (i + 1) * step] = out.astype(bf16)


def keep_kernel(ep_count, near_ref, inner_ref, down_ref, keep_ref):
    half = keep_ref.shape[1]
    start = half_start(2 * half, True)
    row_weight = row_weights(near_ref, half, ep_count)
    step = half // STEPS
    inner = inner_ref[...]
    for i in range(STEPS):
        columns = pl.ds(pl.multiple_of(start + i * step, step), step)
        out = jnp.dot(inner, down_ref[0, :, columns], preferred_element_type=f32)
        keep_ref[:, i * step : (i + 1) * step] = out * row_weight


def estimate(rows, weights):
    return pl.CostEstimate(flops=2 * rows * weights, bytes_accessed=2 * weights, transcendentals=0)


def near_products(near, gate, up):
    rows = near.shape[0]
    width, units = gate.shape[1:]
    acc = pltpu.VMEM((rows, units), f32)
    return pl.pallas_call(
        near_kernel,
        out_shape=(acc, acc),
        in_specs=[in_vmem()] * 3,
        out_specs=(in_vmem(),) * 2,
        compiler_params=pltpu.CompilerParams(vmem_limit_bytes=8 * MIB),
        cost_estimate=estimate(rows, width * units),
    )(vmem(near), gate, up)


def far_products(near, far, gate, up, gate_acc, up_acc, down, ep_count):
    rows = near.shape[0]
    units, width = down.shape[1:]
    half = width // 2
    return pl.pallas_call(
        functools.partial(far_kernel, ep_count),
        out_shape=(pltpu.VMEM((rows, units), bf16), pltpu.VMEM((rows, half), bf16)),
        in_specs=[in_vmem()] * 7,
        out_specs=(in_vmem(),) * 2,
        compiler_params=pltpu.CompilerParams(vmem_limit_bytes=8 * MIB),
        cost_estimate=estimate(rows, 3 * half * units),
    )(vmem(near), vmem(far), gate, up, vmem(gate_acc), vmem(up_acc), down)


def keep_products(near, inner, down, ep_count):
    rows = near.shape[0]
    units, width = down.shape[1:]
    half = width // 2
    return pl.pallas_call(
        functools.partial(keep_kernel, ep_count),
        out_shape=pltpu.VMEM((rows, half), f32),
        in_specs=[in_vmem()] * 3,
        out_specs=in_vmem(),
        compiler_params=pltpu.CompilerParams(vmem_limit_bytes=8 * MIB),
        cost_estimate=estimate(rows, half * units),
    )(vmem(near), vmem(inner), down)


def fold_kernel(by_core, parts, arrived, *refs):
    keep_ref, got_refs = refs[0], refs[1 : 1 + arrived]
    outs = refs[-parts:]
    total = keep_ref[...]
    for g in got_refs:
        total += g[...].astype(f32)
    rows = outs[0].shape[0]
    pieces = [total[i * rows : (i + 1) * rows] for i in range(parts)]
    if by_core:
        first = lax.rem(lax.axis_index("dp"), 2) == 0
        pieces = [jnp.where(first, pieces[0], pieces[1]), jnp.where(first, pieces[1], pieces[0])]
    outs[0][...] = pieces[0]
    for out, piece in zip(outs[1:], pieces[1:]):
        out[...] = piece.astype(bf16)


def fold(keep, gots, parts, *after, by_core=False):
    rows, width = keep.shape
    part = (rows // parts, width)
    return pl.pallas_call(
        functools.partial(fold_kernel, by_core, parts, len(gots)),
        out_shape=(pltpu.VMEM(part, f32),) + (pltpu.VMEM(part, bf16),) * (parts - 1),
        in_specs=[in_vmem()] * (1 + len(gots)) + [anywhere()] * len(after),
        out_specs=(in_vmem(),) * parts,
        compiler_params=pltpu.CompilerParams(vmem_limit_bytes=4 * MIB),
        cost_estimate=pl.CostEstimate(flops=0, bytes_accessed=8 * rows * width, transcendentals=0),
    )(vmem(keep), *[vmem(g) for g in gots], *after)


def finish_kernel(keep_ref, got_ref, out_ref):
    half = keep_ref.shape[1]
    first = lax.rem(lax.axis_index("dp"), 2) == 0
    keep, got = keep_ref[...], got_ref[...].astype(f32)
    out_ref[:, :half] = jnp.where(first, keep, got).astype(bf16)
    out_ref[:, half:] = jnp.where(first, got, keep).astype(bf16)


def finish(keep, got):
    rows, half = keep.shape
    return pl.pallas_call(
        finish_kernel,
        out_shape=jax.ShapeDtypeStruct((rows, 2 * half), bf16),
        in_specs=[in_vmem(), in_vmem()],
        out_specs=in_vmem(),
        compiler_params=pltpu.CompilerParams(vmem_limit_bytes=4 * MIB),
        cost_estimate=pl.CostEstimate(flops=0, bytes_accessed=8 * rows * half, transcendentals=0),
    )(vmem(keep), vmem(got))


def pages_kernel(
    dp_count, page_hbm, dest_hbm, pool_ref, after_ref, low_ref, high_ref, copy_ref, page_ref, dest_ref, sems
):
    own, width = pool_ref.shape
    pool_copy = pltpu.make_async_copy(pool_ref, copy_ref, sems.at[0])
    page_copy = pltpu.make_async_copy(page_hbm, page_ref, sems.at[1])
    dest_copy = pltpu.make_async_copy(dest_hbm, dest_ref, sems.at[2])
    page_copy.start()
    dest_copy.start()
    pool_copy.start()
    page_copy.wait()
    dest_copy.wait()
    me = lax.axis_index("dp")
    slots = dp_count * MCAP
    row = lax.broadcasted_iota(jnp.int32, (slots, own), 0)
    column = lax.broadcasted_iota(jnp.int32, (slots, own), 1)
    pick = jnp.zeros((slots, own), f32)
    entries = page_ref.shape[1]
    for m in range(entries):
        rank = jnp.int32(0)
        for n in range(m):
            rank += jnp.where(dest_ref[0, n] == dest_ref[0, m], 1, 0)
        bucket = jnp.bitwise_xor(dest_ref[0, m], me) * MCAP + rank
        pick = jnp.where((row == bucket) & (column == page_ref[0, m]), 1.0, pick)
    pick = pick.astype(bf16)
    step = 2048
    pool_copy.wait()
    for i in range(width // step):
        columns = slice(i * step, (i + 1) * step)
        out = jnp.dot(pick, copy_ref[:, columns], preferred_element_type=f32)
        low_ref[:, columns] = out[: slots // 2].astype(bf16)
        high_ref[:, columns] = out[slots // 2 :].astype(bf16)


def pick_pages(moved_page, moved_dest, latent_pool, after, dp_count):
    width = latent_pool.shape[1]
    half = pltpu.VMEM((dp_count * MCAP // 2, width), bf16)
    return pl.pallas_call(
        functools.partial(pages_kernel, dp_count),
        out_shape=(half, half, pltpu.VMEM(latent_pool.shape, bf16)),
        in_specs=[in_hbm()] * 3 + [anywhere()],
        out_specs=(in_vmem(),) * 3,
        scratch_shapes=[
            pltpu.SMEM(moved_page.shape, jnp.int32),
            pltpu.SMEM(moved_dest.shape, jnp.int32),
            pltpu.SemaphoreType.DMA((3,)),
        ],
        compiler_params=pltpu.CompilerParams(vmem_limit_bytes=4 * MIB),
        cost_estimate=pl.CostEstimate(flops=0, bytes_accessed=4 * latent_pool.size, transcendentals=0),
    )(hbm(moved_page), hbm(moved_dest), hbm(latent_pool), after)


def exchange_pages(low, high, dp_count):
    blocks, senders = [low], [0]
    sent = high
    for bit in partner_bits(dp_count):
        got = swap(sent, "dp", pairs_of(dp_count, bit))
        size = got.shape[0] // len(blocks)
        blocks = blocks + [got[i * size : (i + 1) * size] for i in range(len(blocks))]
        senders = senders + [s ^ bit for s in senders]
        if size > MCAP:
            sent = jnp.concatenate([b[size // 2 :] for b in blocks], axis=0)
            blocks = [b[: size // 2] for b in blocks]
    return jnp.concatenate(blocks, axis=0), senders


def attend_kernel(senders, length_ref, table_ref, query_ref, pool_ref, arrived_ref, out_ref, query_rows):
    rows_dev = query_ref.shape[0]
    own, width = pool_ref.shape
    arrived = arrived_ref.shape[0]
    slots = -(-(own + arrived) // 16) * 16
    pair_width = 2 * LAT
    pairs = width // pair_width
    me = lax.axis_index("dp")

    for h in range(HEADS // 2):
        query_rows[h * rows_dev : (h + 1) * rows_dev, :] = query_ref[:, h * pair_width : (h + 1) * pair_width].astype(f32)
    straight = query_rows[...]
    turned = pltpu.roll(straight, LAT, 1)
    first = lax.broadcasted_iota(jnp.int32, straight.shape, 1) < LAT
    query_all = jnp.concatenate(
        [
            jnp.where(first, straight, 0.0),
            jnp.where(first, turned, 0.0),
            jnp.where(first, 0.0, turned),
            jnp.where(first, 0.0, straight),
        ],
        axis=0,
    ).astype(bf16)

    pieces = []
    for j in range(pairs):
        columns = slice(j * pair_width, (j + 1) * pair_width)
        parts = [pool_ref[:, columns].astype(f32), arrived_ref[:, columns].astype(f32)]
        if slots > own + arrived:
            parts.append(jnp.zeros((slots - own - arrived, pair_width), f32))
        pieces.append(jnp.concatenate(parts, axis=0).astype(bf16))
    keys = jnp.concatenate(pieces, axis=0)

    scores = lax.dot_general(query_all, keys, (((1,), (1,)), ((), ())), preferred_element_type=f32) * score_scale

    column = lax.broadcasted_iota(jnp.int32, (1, pairs * slots), 1)
    pair = column // slots
    place = column - pair * slots
    slot = place
    for i, s in enumerate(senders):
        source = jnp.bitwise_xor(me, s)
        for k in range(MCAP):
            slot = jnp.where(place == own + i * MCAP + k, own + source * MCAP + k, slot)
    limits = []
    for r in range(rows_dev):
        limit = jnp.full(column.shape, -1, jnp.int32)
        for p in range(table_ref.shape[1]):
            limit = jnp.where(slot == table_ref[r, p], length_ref[r] - p * PAGE, limit)
        limit = jnp.where(place < own + arrived, limit, -1)
        limits.append(limit - 2 * pair)
    half = scores.shape[0] // 2
    row = lax.broadcasted_iota(jnp.int32, (half, 1), 0) % rows_dev
    limit = limits[0]
    for r in range(1, rows_dev):
        limit = jnp.where(row == r, limits[r], limit)
    even = jnp.where(limit > 0, scores[:half], -jnp.inf)
    odd = jnp.where(limit > 1, scores[half:], -jnp.inf)
    peak = jnp.maximum(jnp.max(even, axis=1, keepdims=True), jnp.max(odd, axis=1, keepdims=True))
    even = jnp.exp(even - peak)
    odd = jnp.exp(odd - peak)
    total = jnp.sum(even, axis=1, keepdims=True) + jnp.sum(odd, axis=1, keepdims=True)
    even = (even / total).astype(bf16)
    odd = (odd / total).astype(bf16)
    from_even = jnp.dot(even, keys[:, :VL], preferred_element_type=f32)
    from_odd = jnp.dot(odd, keys[:, VL:], preferred_element_type=f32)
    shift = LAT - VL
    wide = pair_width - VL
    attended = from_even + pltpu.roll(from_odd, wide - shift, 1)[:, :VL]
    for h in range(HEADS):
        at = (h % 2) * (half // 2) + (h // 2) * rows_dev
        out_ref[:, h * VL : (h + 1) * VL] = attended[at : at + rows_dev].astype(bf16)


def attend(lengths, page_table, queries, latent_pool, arrived, senders):
    rows_dev = queries.shape[0]
    return pl.pallas_call(
        functools.partial(attend_kernel, senders),
        out_shape=jax.ShapeDtypeStruct((rows_dev, HEADS * VL), bf16),
        in_specs=[in_smem(), in_smem(), in_vmem(), in_vmem(), in_vmem()],
        out_specs=in_vmem(),
        scratch_shapes=[pltpu.VMEM((HEADS // 2 * rows_dev, 2 * LAT), f32)],
        compiler_params=pltpu.CompilerParams(vmem_limit_bytes=16 * MIB),
        cost_estimate=pl.CostEstimate(flops=1 << 30, bytes_accessed=4 << 20, transcendentals=1 << 17),
    )(lengths, page_table, queries, vmem(latent_pool), vmem(arrived))


def body(
    hidden,
    routes,
    route_weight,
    gate_weight,
    up_weight,
    down_weight,
    queries,
    latent_pool,
    lengths,
    page_table,
    moved_page,
    moved_dest,
):
    ep_count = lax.axis_size("ep")
    dp_count = lax.axis_size("dp")
    count = ep_count * dp_count
    stages = stage_partners(count)

    def trade(x, bit):
        return swap(x, AXES, pairs_of(count, bit))

    mine, other = make_payload(hidden, routes, route_weight, ep_count)
    near = merge([mine, trade(other, 1)], by_core=True)
    for number, partners in enumerate(stages):
        got = [trade(near, bit) for bit in partners]
        after = []
        if number == 0:
            low, high, pool = pick_pages(moved_page, moved_dest, latent_pool, near, dp_count)
            after = [high]
        near = merge([near] + got, *after)
    arrived, senders = exchange_pages(low, high, dp_count)
    far = trade(near, 1)
    gate_acc, up_acc = near_products(near, gate_weight, up_weight)
    inner, send = far_products(near, far, gate_weight, up_weight, gate_acc, up_acc, down_weight, ep_count)
    got = [trade(send, 1)]
    keep = keep_products(near, inner, down_weight, ep_count)
    attended = attend(lengths, page_table, queries, pool, arrived, senders)
    after = []
    for partners in reversed(stages):
        keep, *send = fold(keep, got, len(partners) + 1, *after)
        got = [trade(x, bit) for x, bit in zip(send, partners)]
        after = [] if after else [hbm(attended)]
    keep, send = fold(keep, got, 2, *(after if len(stages) == 1 else []), by_core=True)
    return finish(keep, trade(send, 1)), attended


def solution(mesh):
    rows = P(("inst", "ep", "dp"), None)
    in_specs = (
        rows,
        rows,
        rows,
        P("ep", None, "dp"),
        P("ep", None, "dp"),
        P("ep", "dp", None),
        rows,
        rows,
        P(("inst", "ep", "dp")),
        rows,
        rows,
        rows,
    )
    return jax.shard_map(body, mesh=mesh, in_specs=in_specs, out_specs=(rows, rows), check_vma=False)
```

```python
import functools

import jax
import jax.numpy as jnp
from jax import lax
from jax.experimental import pallas as pl
from jax.experimental.pallas import tpu as pltpu
from jax.sharding import PartitionSpec as P

HEADS = 64
LAT = 576
VL = 512
MCAP = 2
PAGE = 32
LANES = 128
AXES = ("ep", "dp")
MIB = 1 << 20
MERGE_FLOPS = 20_000_000_000

score_scale = 192.0 ** (-0.5)
bf16 = jnp.bfloat16
f32 = jnp.float32


def in_vmem():
    return pl.BlockSpec(memory_space=pltpu.VMEM)


def in_smem():
    return pl.BlockSpec(memory_space=pltpu.SMEM)


def vmem(x):
    return pltpu.with_memory_space_constraint(x, pltpu.VMEM)


def hbm(x):
    return pltpu.with_memory_space_constraint(x, pltpu.HBM)


def anywhere():
    return pl.BlockSpec(memory_space=pl.ANY)


def in_hbm():
    return pl.BlockSpec(memory_space=pltpu.HBM)


def partner_bits(count):
    bits = []
    b = count // 2
    while b:
        bits.append(b)
        b //= 2
    return bits


def swap(x, axes, pairs):
    return lax.ppermute(x, axes, pairs)


def stage_partners(count):
    bits = partner_bits(count)[:-1]
    stages = [(bits[0],)] if len(bits) % 2 else []
    bits = bits[len(bits) % 2 :]
    for high, low in zip(bits[::2], bits[1::2]):
        stages.append((low, high, high ^ low))
    return stages


def pairs_of(count, bit):
    return [(i, i ^ bit) for i in range(count)]


def fetch_kernel(*refs):
    count = (len(refs) - 1) // 2
    copies = [pltpu.make_async_copy(refs[i], refs[count + i], refs[-1].at[i]) for i in range(count)]
    for c in copies:
        c.start()
    for c in copies:
        c.wait()


def fetch(*arrays):
    return pl.pallas_call(
        fetch_kernel,
        out_shape=tuple(pltpu.VMEM(x.shape, x.dtype) for x in arrays),
        in_specs=[in_hbm()] * len(arrays),
        out_specs=(in_vmem(),) * len(arrays),
        scratch_shapes=[pltpu.SemaphoreType.DMA((len(arrays),))],
        compiler_params=pltpu.CompilerParams(vmem_limit_bytes=4 * MIB),
        cost_estimate=pl.CostEstimate(flops=MERGE_FLOPS // 16, bytes_accessed=MIB, transcendentals=0),
    )(*[hbm(x) for x in arrays])


def payload_kernel(ep_count, mine_hidden, mine_routes, mine_weight, got_hidden, got_routes, got_weight, out_ref):
    first = lax.rem(lax.axis_index("dp"), 2) == 0
    rows, width = mine_hidden.shape
    half = width // 2

    def in_order(mine, got):
        return jnp.where(first, jnp.concatenate([mine, got], axis=0), jnp.concatenate([got, mine], axis=0))

    def my_half(ref):
        return jnp.where(first, ref[:, :half].astype(f32), ref[:, half:].astype(f32))

    out_ref[:, :half] = in_order(my_half(mine_hidden), my_half(got_hidden)).astype(bf16)
    routes = in_order(mine_routes[...], got_routes[...])
    weight = in_order(mine_weight[...], got_weight[...])
    column = lax.broadcasted_iota(jnp.int32, (2 * rows, LANES), 1)
    expert = jnp.where(column < ep_count, column, column - ep_count)
    total = jnp.zeros((2 * rows, LANES), f32)
    for k in range(routes.shape[1]):
        total += jnp.where(routes[:, k : k + 1] == expert, weight[:, k : k + 1], 0.0)
    high = total.astype(bf16).astype(f32)
    low = total - high
    out_ref[:, half:] = jnp.where(column < ep_count, high, jnp.where(column < 2 * ep_count, low, 0.0)).astype(bf16)


def make_payload(mine, got, ep_count):
    rows, width = mine[0].shape
    return pl.pallas_call(
        functools.partial(payload_kernel, ep_count),
        out_shape=pltpu.VMEM((2 * rows, width // 2 + LANES), bf16),
        in_specs=[in_vmem()] * 6,
        out_specs=in_vmem(),
        compiler_params=pltpu.CompilerParams(vmem_limit_bytes=4 * MIB),
        cost_estimate=pl.CostEstimate(flops=0, bytes_accessed=4 * rows * width, transcendentals=0),
    )(*[vmem(x) for x in mine], *[vmem(x) for x in got])


def merge_kernel(parts, *refs):
    out_ref = refs[-1]
    rows = refs[0].shape[0]
    if rows % 16:
        out_ref[...] = jnp.concatenate([r[...].astype(f32) for r in refs[:parts]], axis=0).astype(bf16)
    else:
        for i in range(parts):
            out_ref[i * rows : (i + 1) * rows] = refs[i][...]


def merge(pieces, flops, *after):
    rows, width = pieces[0].shape
    return pl.pallas_call(
        functools.partial(merge_kernel, len(pieces)),
        out_shape=pltpu.VMEM((len(pieces) * rows, width), bf16),
        in_specs=[in_vmem()] * len(pieces) + [anywhere()] * len(after),
        out_specs=in_vmem(),
        compiler_params=pltpu.CompilerParams(vmem_limit_bytes=4 * MIB),
        cost_estimate=pl.CostEstimate(flops=flops, bytes_accessed=8 * rows * width, transcendentals=0),
    )(*[vmem(p) for p in pieces], *after)


def half_start(width, near):
    core = lax.rem(lax.axis_index("dp"), 2)
    core = core if near else 1 - core
    return pl.multiple_of(core * (width // 2), width // 2)


def near_kernel(near_ref, gate_ref, up_ref, gate_out, up_out):
    width = gate_ref.shape[1]
    at = pl.ds(half_start(width, True), width // 2)
    x = near_ref[:, : width // 2]
    gate_out[...] = jnp.dot(x, gate_ref[0, at, :], preferred_element_type=f32)
    up_out[...] = jnp.dot(x, up_ref[0, at, :], preferred_element_type=f32)


def row_weights(near_ref, half, ep_count):
    ep = lax.axis_index("ep")
    table = near_ref[:, half:].astype(f32)
    column = lax.broadcasted_iota(jnp.int32, table.shape, 1)
    mine = (column == ep) | (column == ep + ep_count)
    return jnp.sum(jnp.where(mine, table, 0.0), axis=1, keepdims=True)


STEPS = 7


def far_kernel(ep_count, near_ref, far_ref, gate_ref, up_ref, gate_in, up_in, down_ref, inner_ref, send_ref):
    width = gate_ref.shape[1]
    half = width // 2
    start = half_start(width, False)
    at = pl.ds(start, half)
    row_weight = row_weights(near_ref, half, ep_count)
    x = far_ref[:, :half]
    gate = gate_in[...] + jnp.dot(x, gate_ref[0, at, :], preferred_element_type=f32)
    up = up_in[...] + jnp.dot(x, up_ref[0, at, :], preferred_element_type=f32)
    inner = (gate / (1.0 + jnp.exp(-gate)) * up).astype(bf16)
    inner_ref[...] = inner
    step = half // STEPS
    for i in range(STEPS):
        columns = pl.ds(pl.multiple_of(start + i * step, step), step)
        out = jnp.dot(inner, down_ref[0, :, columns], preferred_element_type=f32) * row_weight
        send_ref[:, i * step : (i + 1) * step] = out.astype(bf16)


def keep_kernel(ep_count, near_ref, inner_ref, down_ref, keep_ref):
    half = keep_ref.shape[1]
    start = half_start(2 * half, True)
    row_weight = row_weights(near_ref, half, ep_count)
    step = half // STEPS
    inner = inner_ref[...]
    for i in range(STEPS):
        columns = pl.ds(pl.multiple_of(start + i * step, step), step)
        out = jnp.dot(inner, down_ref[0, :, columns], preferred_element_type=f32)
        keep_ref[:, i * step : (i + 1) * step] = out * row_weight


def estimate(rows, weights):
    return pl.CostEstimate(flops=2 * rows * weights, bytes_accessed=2 * weights, transcendentals=0)


def near_products(near, gate, up):
    rows = near.shape[0]
    width, units = gate.shape[1:]
    acc = pltpu.VMEM((rows, units), f32)
    return pl.pallas_call(
        near_kernel,
        out_shape=(acc, acc),
        in_specs=[in_vmem()] * 3,
        out_specs=(in_vmem(),) * 2,
        compiler_params=pltpu.CompilerParams(vmem_limit_bytes=8 * MIB),
        cost_estimate=estimate(rows, width * units),
    )(vmem(near), gate, up)


def far_products(near, far, gate, up, gate_acc, up_acc, down, ep_count):
    rows = near.shape[0]
    units, width = down.shape[1:]
    half = width // 2
    return pl.pallas_call(
        functools.partial(far_kernel, ep_count),
        out_shape=(pltpu.VMEM((rows, units), bf16), pltpu.VMEM((rows, half), bf16)),
        in_specs=[in_vmem()] * 7,
        out_specs=(in_vmem(),) * 2,
        compiler_params=pltpu.CompilerParams(vmem_limit_bytes=8 * MIB),
        cost_estimate=estimate(rows, 3 * half * units),
    )(vmem(near), vmem(far), gate, up, vmem(gate_acc), vmem(up_acc), down)


def keep_products(near, inner, down, ep_count):
    rows = near.shape[0]
    units, width = down.shape[1:]
    half = width // 2
    return pl.pallas_call(
        functools.partial(keep_kernel, ep_count),
        out_shape=pltpu.VMEM((rows, half), f32),
        in_specs=[in_vmem()] * 3,
        out_specs=in_vmem(),
        compiler_params=pltpu.CompilerParams(vmem_limit_bytes=8 * MIB),
        cost_estimate=estimate(rows, half * units),
    )(vmem(near), vmem(inner), down)


def fold_kernel(by_core, parts, arrived, *refs):
    keep_ref, got_refs = refs[0], refs[1 : 1 + arrived]
    outs = refs[-parts:]
    total = keep_ref[...]
    for g in got_refs:
        total += g[...].astype(f32)
    rows = outs[0].shape[0]
    pieces = [total[i * rows : (i + 1) * rows] for i in range(parts)]
    if by_core:
        first = lax.rem(lax.axis_index("dp"), 2) == 0
        pieces = [jnp.where(first, pieces[0], pieces[1]), jnp.where(first, pieces[1], pieces[0])]
    outs[0][...] = pieces[0]
    for out, piece in zip(outs[1:], pieces[1:]):
        out[...] = piece.astype(bf16)


def fold(keep, gots, parts, *after, by_core=False):
    rows, width = keep.shape
    part = (rows // parts, width)
    return pl.pallas_call(
        functools.partial(fold_kernel, by_core, parts, len(gots)),
        out_shape=(pltpu.VMEM(part, f32),) + (pltpu.VMEM(part, bf16),) * (parts - 1),
        in_specs=[in_vmem()] * (1 + len(gots)) + [anywhere()] * len(after),
        out_specs=(in_vmem(),) * parts,
        compiler_params=pltpu.CompilerParams(vmem_limit_bytes=4 * MIB),
        cost_estimate=pl.CostEstimate(flops=0, bytes_accessed=8 * rows * width, transcendentals=0),
    )(vmem(keep), *[vmem(g) for g in gots], *after)


def finish_kernel(keep_ref, got_ref, out_ref):
    half = keep_ref.shape[1]
    first = lax.rem(lax.axis_index("dp"), 2) == 0
    keep, got = keep_ref[...], got_ref[...].astype(f32)
    out_ref[:, :half] = jnp.where(first, keep, got).astype(bf16)
    out_ref[:, half:] = jnp.where(first, got, keep).astype(bf16)


def finish(keep, got):
    rows, half = keep.shape
    return pl.pallas_call(
        finish_kernel,
        out_shape=jax.ShapeDtypeStruct((rows, 2 * half), bf16),
        in_specs=[in_vmem(), in_vmem()],
        out_specs=in_vmem(),
        compiler_params=pltpu.CompilerParams(vmem_limit_bytes=4 * MIB),
        cost_estimate=pl.CostEstimate(flops=0, bytes_accessed=8 * rows * half, transcendentals=0),
    )(vmem(keep), vmem(got))


def pages_kernel(
    dp_count, page_hbm, dest_hbm, pool_ref, after_ref, low_ref, high_ref, copy_ref, page_ref, dest_ref, sems
):
    own, width = pool_ref.shape
    pool_copy = pltpu.make_async_copy(pool_ref, copy_ref, sems.at[0])
    page_copy = pltpu.make_async_copy(page_hbm, page_ref, sems.at[1])
    dest_copy = pltpu.make_async_copy(dest_hbm, dest_ref, sems.at[2])
    page_copy.start()
    dest_copy.start()
    pool_copy.start()
    page_copy.wait()
    dest_copy.wait()
    me = lax.axis_index("dp")
    slots = dp_count * MCAP
    row = lax.broadcasted_iota(jnp.int32, (slots, own), 0)
    column = lax.broadcasted_iota(jnp.int32, (slots, own), 1)
    pick = jnp.zeros((slots, own), f32)
    entries = page_ref.shape[1]
    for m in range(entries):
        rank = jnp.int32(0)
        for n in range(m):
            rank += jnp.where(dest_ref[0, n] == dest_ref[0, m], 1, 0)
        bucket = jnp.bitwise_xor(dest_ref[0, m], me) * MCAP + rank
        pick = jnp.where((row == bucket) & (column == page_ref[0, m]), 1.0, pick)
    pick = pick.astype(bf16)
    step = 2048
    pool_copy.wait()
    for i in range(width // step):
        columns = slice(i * step, (i + 1) * step)
        out = jnp.dot(pick, copy_ref[:, columns], preferred_element_type=f32)
        low_ref[:, columns] = out[: slots // 2].astype(bf16)
        high_ref[:, columns] = out[slots // 2 :].astype(bf16)


def pick_pages(moved_page, moved_dest, latent_pool, after, dp_count):
    width = latent_pool.shape[1]
    half = pltpu.VMEM((dp_count * MCAP // 2, width), bf16)
    return pl.pallas_call(
        functools.partial(pages_kernel, dp_count),
        out_shape=(half, half, pltpu.VMEM(latent_pool.shape, bf16)),
        in_specs=[in_hbm()] * 3 + [anywhere()],
        out_specs=(in_vmem(),) * 3,
        scratch_shapes=[
            pltpu.SMEM(moved_page.shape, jnp.int32),
            pltpu.SMEM(moved_dest.shape, jnp.int32),
            pltpu.SemaphoreType.DMA((3,)),
        ],
        compiler_params=pltpu.CompilerParams(vmem_limit_bytes=4 * MIB),
        cost_estimate=pl.CostEstimate(flops=0, bytes_accessed=4 * latent_pool.size, transcendentals=0),
    )(hbm(moved_page), hbm(moved_dest), hbm(latent_pool), after)


def exchange_pages(low, high, dp_count):
    blocks, senders = [low], [0]
    sent = high
    for bit in partner_bits(dp_count):
        got = swap(sent, "dp", pairs_of(dp_count, bit))
        size = got.shape[0] // len(blocks)
        blocks = blocks + [got[i * size : (i + 1) * size] for i in range(len(blocks))]
        senders = senders + [s ^ bit for s in senders]
        if size > MCAP:
            sent = jnp.concatenate([b[size // 2 :] for b in blocks], axis=0)
            blocks = [b[: size // 2] for b in blocks]
    return jnp.concatenate(blocks, axis=0), senders


def attend_kernel(senders, length_ref, table_ref, query_ref, pool_ref, arrived_ref, out_ref, query_rows):
    rows_dev = query_ref.shape[0]
    own, width = pool_ref.shape
    arrived = arrived_ref.shape[0]
    slots = -(-(own + arrived) // 16) * 16
    pair_width = 2 * LAT
    pairs = width // pair_width
    me = lax.axis_index("dp")

    for h in range(HEADS // 2):
        query_rows[h * rows_dev : (h + 1) * rows_dev, :] = query_ref[:, h * pair_width : (h + 1) * pair_width].astype(f32)
    straight = query_rows[...]
    turned = pltpu.roll(straight, LAT, 1)
    first = lax.broadcasted_iota(jnp.int32, straight.shape, 1) < LAT
    query_all = jnp.concatenate(
        [
            jnp.where(first, straight, 0.0),
            jnp.where(first, turned, 0.0),
            jnp.where(first, 0.0, turned),
            jnp.where(first, 0.0, straight),
        ],
        axis=0,
    ).astype(bf16)

    pieces = []
    for j in range(pairs):
        columns = slice(j * pair_width, (j + 1) * pair_width)
        parts = [pool_ref[:, columns].astype(f32), arrived_ref[:, columns].astype(f32)]
        if slots > own + arrived:
            parts.append(jnp.zeros((slots - own - arrived, pair_width), f32))
        pieces.append(jnp.concatenate(parts, axis=0).astype(bf16))
    keys = jnp.concatenate(pieces, axis=0)

    scores = lax.dot_general(query_all, keys, (((1,), (1,)), ((), ())), preferred_element_type=f32) * score_scale

    column = lax.broadcasted_iota(jnp.int32, (1, pairs * slots), 1)
    pair = column // slots
    place = column - pair * slots
    slot = place
    for i, s in enumerate(senders):
        source = jnp.bitwise_xor(me, s)
        for k in range(MCAP):
            slot = jnp.where(place == own + i * MCAP + k, own + source * MCAP + k, slot)
    limits = []
    for r in range(rows_dev):
        limit = jnp.full(column.shape, -1, jnp.int32)
        for p in range(table_ref.shape[1]):
            limit = jnp.where(slot == table_ref[r, p], length_ref[r] - p * PAGE, limit)
        limit = jnp.where(place < own + arrived, limit, -1)
        limits.append(limit - 2 * pair)
    half = scores.shape[0] // 2
    row = lax.broadcasted_iota(jnp.int32, (half, 1), 0) % rows_dev
    limit = limits[0]
    for r in range(1, rows_dev):
        limit = jnp.where(row == r, limits[r], limit)
    even = jnp.where(limit > 0, scores[:half], -jnp.inf)
    odd = jnp.where(limit > 1, scores[half:], -jnp.inf)
    peak = jnp.maximum(jnp.max(even, axis=1, keepdims=True), jnp.max(odd, axis=1, keepdims=True))
    even = jnp.exp(even - peak)
    odd = jnp.exp(odd - peak)
    total = jnp.sum(even, axis=1, keepdims=True) + jnp.sum(odd, axis=1, keepdims=True)
    even = (even / total).astype(bf16)
    odd = (odd / total).astype(bf16)
    from_even = jnp.dot(even, keys[:, :VL], preferred_element_type=f32)
    from_odd = jnp.dot(odd, keys[:, VL:], preferred_element_type=f32)
    shift = LAT - VL
    wide = pair_width - VL
    attended = from_even + pltpu.roll(from_odd, wide - shift, 1)[:, :VL]
    for h in range(HEADS):
        at = (h % 2) * (half // 2) + (h // 2) * rows_dev
        out_ref[:, h * VL : (h + 1) * VL] = attended[at : at + rows_dev].astype(bf16)


def attend(lengths, page_table, queries, latent_pool, arrived, senders):
    rows_dev = queries.shape[0]
    return pl.pallas_call(
        functools.partial(attend_kernel, senders),
        out_shape=jax.ShapeDtypeStruct((rows_dev, HEADS * VL), bf16),
        in_specs=[in_smem(), in_smem(), in_vmem(), in_vmem(), in_vmem()],
        out_specs=in_vmem(),
        scratch_shapes=[pltpu.VMEM((HEADS // 2 * rows_dev, 2 * LAT), f32)],
        compiler_params=pltpu.CompilerParams(vmem_limit_bytes=16 * MIB),
        cost_estimate=pl.CostEstimate(flops=1 << 30, bytes_accessed=4 << 20, transcendentals=1 << 17),
    )(lengths, page_table, queries, vmem(latent_pool), vmem(arrived))


def body(
    hidden,
    routes,
    route_weight,
    gate_weight,
    up_weight,
    down_weight,
    queries,
    latent_pool,
    lengths,
    page_table,
    moved_page,
    moved_dest,
):
    ep_count = lax.axis_size("ep")
    dp_count = lax.axis_size("dp")
    count = ep_count * dp_count
    stages = stage_partners(count)

    def trade(x, bit):
        return swap(x, AXES, pairs_of(count, bit))

    mine = (hidden, routes, route_weight)
    got = [trade(x, 1) for x in mine]
    near = make_payload(fetch(*mine), got, ep_count)
    for number, partners in enumerate(stages):
        got = [trade(near, bit) for bit in partners]
        after = []
        if number == 0:
            low, high, pool = pick_pages(moved_page, moved_dest, latent_pool, near, dp_count)
            after = [high]
        near = merge([near] + got, MERGE_FLOPS if number < len(stages) - 1 else MERGE_FLOPS // 4, *after)
    arrived, senders = exchange_pages(low, high, dp_count)
    far = trade(near, 1)
    gate_acc, up_acc = near_products(near, gate_weight, up_weight)
    inner, send = far_products(near, far, gate_weight, up_weight, gate_acc, up_acc, down_weight, ep_count)
    got = [trade(send, 1)]
    keep = keep_products(near, inner, down_weight, ep_count)
    attended = attend(lengths, page_table, queries, pool, arrived, senders)
    after = []
    for partners in reversed(stages):
        keep, *send = fold(keep, got, len(partners) + 1, *after)
        got = [trade(x, bit) for x, bit in list(zip(send, partners))[::-1]]
        after = [] if after else [hbm(attended)]
    keep, send = fold(keep, got, 2, *(after if len(stages) == 1 else []), by_core=True)
    return finish(keep, trade(send, 1)), attended


def solution(mesh):
    rows = P(("inst", "ep", "dp"), None)
    in_specs = (
        rows,
        rows,
        rows,
        P("ep", None, "dp"),
        P("ep", None, "dp"),
        P("ep", "dp", None),
        rows,
        rows,
        P(("inst", "ep", "dp")),
        rows,
        rows,
        rows,
    )
    return jax.shard_map(body, mesh=mesh, in_specs=in_specs, out_specs=(rows, rows), check_vma=False)
```

```python
import functools

import jax
import jax.numpy as jnp
from jax import lax
from jax.experimental import pallas as pl
from jax.experimental.pallas import tpu as pltpu
from jax.sharding import PartitionSpec as P

HEADS = 64
LAT = 576
VL = 512
MCAP = 2
PAGE = 32
LANES = 128
AXES = ("ep", "dp")
MIB = 1 << 20
MERGE_FLOPS = 20_000_000_000

score_scale = 192.0 ** (-0.5)
bf16 = jnp.bfloat16
f32 = jnp.float32


def in_vmem():
    return pl.BlockSpec(memory_space=pltpu.VMEM)


def in_smem():
    return pl.BlockSpec(memory_space=pltpu.SMEM)


def vmem(x):
    return pltpu.with_memory_space_constraint(x, pltpu.VMEM)


def hbm(x):
    return pltpu.with_memory_space_constraint(x, pltpu.HBM)


def anywhere():
    return pl.BlockSpec(memory_space=pl.ANY)


def in_hbm():
    return pl.BlockSpec(memory_space=pltpu.HBM)


def partner_bits(count):
    bits = []
    b = count // 2
    while b:
        bits.append(b)
        b //= 2
    return bits


def swap(x, axes, pairs):
    return lax.ppermute(x, axes, pairs)


def stage_partners(count):
    bits = partner_bits(count)[:-1]
    stages = [(bits[0],)] if len(bits) % 2 else []
    bits = bits[len(bits) % 2 :]
    for high, low in zip(bits[::2], bits[1::2]):
        stages.append((low, high, high ^ low))
    return stages


def pairs_of(count, bit):
    return [(i, i ^ bit) for i in range(count)]


def fetch_kernel(*refs):
    count = (len(refs) - 1) // 2
    copies = [pltpu.make_async_copy(refs[i], refs[count + i], refs[-1].at[i]) for i in range(count)]
    for c in copies:
        c.start()
    for c in copies:
        c.wait()


def fetch(*arrays):
    return pl.pallas_call(
        fetch_kernel,
        out_shape=tuple(pltpu.VMEM(x.shape, x.dtype) for x in arrays),
        in_specs=[in_hbm()] * len(arrays),
        out_specs=(in_vmem(),) * len(arrays),
        scratch_shapes=[pltpu.SemaphoreType.DMA((len(arrays),))],
        compiler_params=pltpu.CompilerParams(vmem_limit_bytes=4 * MIB),
        cost_estimate=pl.CostEstimate(flops=MERGE_FLOPS // 16, bytes_accessed=MIB, transcendentals=0),
    )(*[hbm(x) for x in arrays])


def payload_kernel(ep_count, mine_hidden, mine_routes, mine_weight, got_hidden, got_routes, got_weight, out_ref):
    first = lax.rem(lax.axis_index("dp"), 2) == 0
    rows, width = mine_hidden.shape
    half = width // 2

    def in_order(mine, got):
        return jnp.where(first, jnp.concatenate([mine, got], axis=0), jnp.concatenate([got, mine], axis=0))

    def my_half(ref):
        return jnp.where(first, ref[:, :half].astype(f32), ref[:, half:].astype(f32))

    out_ref[:, :half] = in_order(my_half(mine_hidden), my_half(got_hidden)).astype(bf16)
    routes = in_order(mine_routes[...], got_routes[...])
    weight = in_order(mine_weight[...], got_weight[...])
    column = lax.broadcasted_iota(jnp.int32, (2 * rows, LANES), 1)
    expert = jnp.where(column < ep_count, column, column - ep_count)
    total = jnp.zeros((2 * rows, LANES), f32)
    for k in range(routes.shape[1]):
        total += jnp.where(routes[:, k : k + 1] == expert, weight[:, k : k + 1], 0.0)
    high = total.astype(bf16).astype(f32)
    low = total - high
    out_ref[:, half:] = jnp.where(column < ep_count, high, jnp.where(column < 2 * ep_count, low, 0.0)).astype(bf16)


def make_payload(mine, got, ep_count):
    rows, width = mine[0].shape
    return pl.pallas_call(
        functools.partial(payload_kernel, ep_count),
        out_shape=pltpu.VMEM((2 * rows, width // 2 + LANES), bf16),
        in_specs=[in_vmem()] * 6,
        out_specs=in_vmem(),
        compiler_params=pltpu.CompilerParams(vmem_limit_bytes=4 * MIB),
        cost_estimate=pl.CostEstimate(flops=0, bytes_accessed=4 * rows * width, transcendentals=0),
    )(*[vmem(x) for x in mine], *[vmem(x) for x in got])


def merge_kernel(parts, *refs):
    out_ref = refs[-1]
    half = refs[0].shape[0] // 2
    pieces = [r[...].astype(f32) for r in refs[:parts]]
    cores = [p[:half] for p in pieces] + [p[half:] for p in pieces]
    out_ref[...] = jnp.concatenate(cores, axis=0).astype(bf16)


def merge(pieces, flops, *after):
    rows, width = pieces[0].shape
    return pl.pallas_call(
        functools.partial(merge_kernel, len(pieces)),
        out_shape=pltpu.VMEM((len(pieces) * rows, width), bf16),
        in_specs=[in_vmem()] * len(pieces) + [anywhere()] * len(after),
        out_specs=in_vmem(),
        compiler_params=pltpu.CompilerParams(vmem_limit_bytes=4 * MIB),
        cost_estimate=pl.CostEstimate(flops=flops, bytes_accessed=8 * rows * width, transcendentals=0),
    )(*[vmem(p) for p in pieces], *after)


def half_start(width, near):
    core = lax.rem(lax.axis_index("dp"), 2)
    core = core if near else 1 - core
    return pl.multiple_of(core * (width // 2), width // 2)


def padded(x):
    rows = x.shape[0]
    return x if rows >= 128 else jnp.concatenate([x] * (128 // rows), axis=0)


def near_kernel(near_ref, gate_ref, up_ref, gate_out, up_out):
    rows, width = near_ref.shape[0], gate_ref.shape[1]
    at = pl.ds(half_start(width, True), width // 2)
    x = padded(near_ref[:, : width // 2])
    gate_out[...] = jnp.dot(x, gate_ref[0, at, :], preferred_element_type=f32)[:rows]
    up_out[...] = jnp.dot(x, up_ref[0, at, :], preferred_element_type=f32)[:rows]


def row_weights(near_ref, half, ep_count):
    ep = lax.axis_index("ep")
    table = near_ref[:, half:].astype(f32)
    column = lax.broadcasted_iota(jnp.int32, table.shape, 1)
    mine = (column == ep) | (column == ep + ep_count)
    return jnp.sum(jnp.where(mine, table, 0.0), axis=1, keepdims=True)


STEPS = 7


def down_half(inner, row_weight, down_ref, start, keep_ref, send_ref):
    first = lax.rem(lax.axis_index("dp"), 2) == 0
    rows, half = keep_ref.shape
    step = half // STEPS
    x = padded(inner)
    for i in range(STEPS):
        columns = slice(i * step, (i + 1) * step)
        out = jnp.dot(x, down_ref[0, :, start + i * step : start + (i + 1) * step], preferred_element_type=f32)
        out = out[: 2 * rows] * row_weight
        keep_ref[:, columns] = jnp.where(first, out[:rows], out[rows:])
        send_ref[:, columns] = jnp.where(first, out[rows:], out[:rows]).astype(bf16)


def far_kernel(ep_count, near_ref, far_ref, gate_ref, up_ref, gate_in, up_in, down_ref, inner_ref, keep_ref, send_ref):
    rows, width = near_ref.shape[0], gate_ref.shape[1]
    half = width // 2
    at = pl.ds(half_start(width, False), half)
    row_weight = row_weights(near_ref, half, ep_count)
    x = padded(far_ref[:, :half])
    gate = gate_in[...] + jnp.dot(x, gate_ref[0, at, :], preferred_element_type=f32)[:rows]
    up = up_in[...] + jnp.dot(x, up_ref[0, at, :], preferred_element_type=f32)[:rows]
    inner = (gate / (1.0 + jnp.exp(-gate)) * up).astype(bf16)
    inner_ref[...] = inner
    down_half(inner, row_weight, down_ref, 0, keep_ref, send_ref)


def rest_kernel(ep_count, near_ref, inner_ref, down_ref, keep_ref, send_ref):
    half = keep_ref.shape[1]
    down_half(inner_ref[...], row_weights(near_ref, half, ep_count), down_ref, half, keep_ref, send_ref)


def estimate(rows, weights):
    return pl.CostEstimate(flops=2 * rows * weights, bytes_accessed=2 * weights, transcendentals=0)


def near_products(near, gate, up):
    rows = near.shape[0]
    width, units = gate.shape[1:]
    acc = pltpu.VMEM((rows, units), f32)
    return pl.pallas_call(
        near_kernel,
        out_shape=(acc, acc),
        in_specs=[in_vmem()] * 3,
        out_specs=(in_vmem(),) * 2,
        compiler_params=pltpu.CompilerParams(vmem_limit_bytes=8 * MIB),
        cost_estimate=estimate(rows, width * units),
    )(vmem(near), gate, up)


def far_products(near, far, gate, up, gate_acc, up_acc, down, ep_count):
    rows = near.shape[0]
    units, width = down.shape[1:]
    half = width // 2
    return pl.pallas_call(
        functools.partial(far_kernel, ep_count),
        out_shape=(
            pltpu.VMEM((rows, units), bf16),
            pltpu.VMEM((rows // 2, half), f32),
            pltpu.VMEM((rows // 2, half), bf16),
        ),
        in_specs=[in_vmem()] * 7,
        out_specs=(in_vmem(),) * 3,
        compiler_params=pltpu.CompilerParams(vmem_limit_bytes=8 * MIB),
        cost_estimate=estimate(rows, 3 * half * units),
    )(vmem(near), vmem(far), gate, up, vmem(gate_acc), vmem(up_acc), down)


def rest_products(near, inner, down, ep_count):
    rows = near.shape[0]
    units, width = down.shape[1:]
    half = width // 2
    return pl.pallas_call(
        functools.partial(rest_kernel, ep_count),
        out_shape=(pltpu.VMEM((rows // 2, half), f32), pltpu.VMEM((rows // 2, half), bf16)),
        in_specs=[in_vmem()] * 3,
        out_specs=(in_vmem(),) * 2,
        compiler_params=pltpu.CompilerParams(vmem_limit_bytes=8 * MIB),
        cost_estimate=estimate(rows, half * units),
    )(vmem(near), vmem(inner), down)


def fold_kernel(arrived, parts, *refs):
    outs = refs[-parts:]
    rows = outs[0].shape[0]
    start = at = 0
    for number in arrived:
        ours = refs[at : at + 1 + number]
        at += 1 + number
        total = ours[0][...]
        for g in ours[1:]:
            total += g[...].astype(f32)
        columns = slice(start, start + total.shape[1])
        start += total.shape[1]
        for i, out in enumerate(outs):
            out[:, columns] = total[i * rows : (i + 1) * rows].astype(out.dtype)


def fold(held, parts, *after, out=None, flops=0):
    rows = held[0][0].shape[0]
    width = sum(keep.shape[1] for keep, _ in held)
    part = (rows // parts, width)
    operands = [vmem(x) for keep, gots in held for x in [keep] + gots]
    shapes = (pltpu.VMEM(part, f32),) + (pltpu.VMEM(part, bf16),) * (parts - 1)
    return pl.pallas_call(
        functools.partial(fold_kernel, [len(gots) for _, gots in held], parts),
        out_shape=shapes if out is None else (out,),
        in_specs=[in_vmem()] * len(operands) + [anywhere()] * len(after),
        out_specs=(in_vmem(),) * parts,
        compiler_params=pltpu.CompilerParams(vmem_limit_bytes=4 * MIB),
        cost_estimate=pl.CostEstimate(flops=flops, bytes_accessed=8 * rows * width, transcendentals=0),
    )(*operands, *after)


def pages_kernel(
    dp_count, page_hbm, dest_hbm, pool_ref, after_ref, low_ref, high_ref, copy_ref, page_ref, dest_ref, sems
):
    own, width = pool_ref.shape
    pool_copy = pltpu.make_async_copy(pool_ref, copy_ref, sems.at[0])
    page_copy = pltpu.make_async_copy(page_hbm, page_ref, sems.at[1])
    dest_copy = pltpu.make_async_copy(dest_hbm, dest_ref, sems.at[2])
    page_copy.start()
    dest_copy.start()
    pool_copy.start()
    page_copy.wait()
    dest_copy.wait()
    me = lax.axis_index("dp")
    slots = dp_count * MCAP
    row = lax.broadcasted_iota(jnp.int32, (slots, own), 0)
    column = lax.broadcasted_iota(jnp.int32, (slots, own), 1)
    pick = jnp.zeros((slots, own), f32)
    entries = page_ref.shape[1]
    for m in range(entries):
        rank = jnp.int32(0)
        for n in range(m):
            rank += jnp.where(dest_ref[0, n] == dest_ref[0, m], 1, 0)
        bucket = jnp.bitwise_xor(dest_ref[0, m], me) * MCAP + rank
        pick = jnp.where((row == bucket) & (column == page_ref[0, m]), 1.0, pick)
    pick = pick.astype(bf16)
    step = 2048
    pool_copy.wait()
    for i in range(width // step):
        columns = slice(i * step, (i + 1) * step)
        out = jnp.dot(pick, copy_ref[:, columns], preferred_element_type=f32)
        low_ref[:, columns] = out[: slots // 2].astype(bf16)
        high_ref[:, columns] = out[slots // 2 :].astype(bf16)


def pick_pages(moved_page, moved_dest, latent_pool, after, dp_count):
    width = latent_pool.shape[1]
    half = pltpu.VMEM((dp_count * MCAP // 2, width), bf16)
    return pl.pallas_call(
        functools.partial(pages_kernel, dp_count),
        out_shape=(half, half, pltpu.VMEM(latent_pool.shape, bf16)),
        in_specs=[in_hbm()] * 3 + [anywhere()],
        out_specs=(in_vmem(),) * 3,
        scratch_shapes=[
            pltpu.SMEM(moved_page.shape, jnp.int32),
            pltpu.SMEM(moved_dest.shape, jnp.int32),
            pltpu.SemaphoreType.DMA((3,)),
        ],
        compiler_params=pltpu.CompilerParams(vmem_limit_bytes=4 * MIB),
        cost_estimate=pl.CostEstimate(flops=0, bytes_accessed=4 * latent_pool.size, transcendentals=0),
    )(hbm(moved_page), hbm(moved_dest), hbm(latent_pool), after)


def exchange_pages(low, high, dp_count):
    blocks, senders = [low], [0]
    sent = high
    for bit in partner_bits(dp_count):
        got = swap(sent, "dp", pairs_of(dp_count, bit))
        size = got.shape[0] // len(blocks)
        blocks = blocks + [got[i * size : (i + 1) * size] for i in range(len(blocks))]
        senders = senders + [s ^ bit for s in senders]
        if size > MCAP:
            sent = jnp.concatenate([b[size // 2 :] for b in blocks], axis=0)
            blocks = [b[: size // 2] for b in blocks]
    return jnp.concatenate(blocks, axis=0), senders


def attend_kernel(senders, length_ref, table_ref, query_ref, pool_ref, arrived_ref, out_ref, query_rows):
    rows_dev = query_ref.shape[0]
    own, width = pool_ref.shape
    arrived = arrived_ref.shape[0]
    slots = -(-(own + arrived) // 16) * 16
    pair_width = 2 * LAT
    pairs = width // pair_width
    me = lax.axis_index("dp")

    for h in range(HEADS // 2):
        query_rows[h * rows_dev : (h + 1) * rows_dev, :] = query_ref[:, h * pair_width : (h + 1) * pair_width].astype(f32)
    straight = query_rows[...]
    turned = pltpu.roll(straight, LAT, 1)
    first = lax.broadcasted_iota(jnp.int32, straight.shape, 1) < LAT
    query_all = jnp.concatenate(
        [
            jnp.where(first, straight, 0.0),
            jnp.where(first, turned, 0.0),
            jnp.where(first, 0.0, turned),
            jnp.where(first, 0.0, straight),
        ],
        axis=0,
    ).astype(bf16)

    pieces = []
    for j in range(pairs):
        columns = slice(j * pair_width, (j + 1) * pair_width)
        parts = [pool_ref[:, columns].astype(f32), arrived_ref[:, columns].astype(f32)]
        if slots > own + arrived:
            parts.append(jnp.zeros((slots - own - arrived, pair_width), f32))
        pieces.append(jnp.concatenate(parts, axis=0).astype(bf16))
    keys = jnp.concatenate(pieces, axis=0)

    scores = lax.dot_general(query_all, keys, (((1,), (1,)), ((), ())), preferred_element_type=f32) * score_scale

    column = lax.broadcasted_iota(jnp.int32, (1, pairs * slots), 1)
    pair = column // slots
    place = column - pair * slots
    slot = place
    for i, s in enumerate(senders):
        source = jnp.bitwise_xor(me, s)
        for k in range(MCAP):
            slot = jnp.where(place == own + i * MCAP + k, own + source * MCAP + k, slot)
    limits = []
    for r in range(rows_dev):
        limit = jnp.full(column.shape, -1, jnp.int32)
        for p in range(table_ref.shape[1]):
            limit = jnp.where(slot == table_ref[r, p], length_ref[r] - p * PAGE, limit)
        limit = jnp.where(place < own + arrived, limit, -1)
        limits.append(limit - 2 * pair)
    half = scores.shape[0] // 2
    row = lax.broadcasted_iota(jnp.int32, (half, 1), 0) % rows_dev
    limit = limits[0]
    for r in range(1, rows_dev):
        limit = jnp.where(row == r, limits[r], limit)
    even = jnp.where(limit > 0, scores[:half], -jnp.inf)
    odd = jnp.where(limit > 1, scores[half:], -jnp.inf)
    peak = jnp.maximum(jnp.max(even, axis=1, keepdims=True), jnp.max(odd, axis=1, keepdims=True))
    even = jnp.exp(even - peak)
    odd = jnp.exp(odd - peak)
    total = jnp.sum(even, axis=1, keepdims=True) + jnp.sum(odd, axis=1, keepdims=True)
    even = (even / total).astype(bf16)
    odd = (odd / total).astype(bf16)
    from_even = jnp.dot(even, keys[:, :VL], preferred_element_type=f32)
    from_odd = jnp.dot(odd, keys[:, VL:], preferred_element_type=f32)
    shift = LAT - VL
    wide = pair_width - VL
    attended = from_even + pltpu.roll(from_odd, wide - shift, 1)[:, :VL]
    for h in range(HEADS):
        at = (h % 2) * (half // 2) + (h // 2) * rows_dev
        out_ref[:, h * VL : (h + 1) * VL] = attended[at : at + rows_dev].astype(bf16)


def attend(lengths, page_table, queries, latent_pool, arrived, senders):
    rows_dev = queries.shape[0]
    return pl.pallas_call(
        functools.partial(attend_kernel, senders),
        out_shape=jax.ShapeDtypeStruct((rows_dev, HEADS * VL), bf16),
        in_specs=[in_smem(), in_smem(), in_vmem(), in_vmem(), in_vmem()],
        out_specs=in_vmem(),
        scratch_shapes=[pltpu.VMEM((HEADS // 2 * rows_dev, 2 * LAT), f32)],
        compiler_params=pltpu.CompilerParams(vmem_limit_bytes=16 * MIB),
        cost_estimate=pl.CostEstimate(flops=1 << 30, bytes_accessed=4 << 20, transcendentals=1 << 17),
    )(lengths, page_table, queries, vmem(latent_pool), vmem(arrived))


def body(
    hidden,
    routes,
    route_weight,
    gate_weight,
    up_weight,
    down_weight,
    queries,
    latent_pool,
    lengths,
    page_table,
    moved_page,
    moved_dest,
):
    ep_count = lax.axis_size("ep")
    dp_count = lax.axis_size("dp")
    count = ep_count * dp_count
    stages = stage_partners(count)

    def trade(x, bit):
        return swap(x, AXES, pairs_of(count, bit))

    mine = (hidden, routes, route_weight)
    got = [trade(x, 1) for x in mine]
    near = make_payload(fetch(*mine), got, ep_count)
    for number, partners in enumerate(stages):
        got = [trade(near, bit) for bit in partners]
        after = []
        if number == 0:
            low, high, pool = pick_pages(moved_page, moved_dest, latent_pool, near, dp_count)
            after = [high]
        near = merge([near] + got, MERGE_FLOPS if number < len(stages) - 1 else MERGE_FLOPS // 4, *after)
    arrived, senders = exchange_pages(low, high, dp_count)
    far = trade(near, 1)
    gate_acc, up_acc = near_products(near, gate_weight, up_weight)
    inner, keep_a, send_a = far_products(
        near, far, gate_weight, up_weight, gate_acc, up_acc, down_weight, ep_count
    )
    got_a = trade(send_a, 1)
    keep_b, send_b = rest_products(near, inner, down_weight, ep_count)
    got_b = trade(send_b, 1)
    (sum_a,) = fold([(keep_a, [got_a])], 1, out=pltpu.VMEM(keep_a.shape, f32), flops=MERGE_FLOPS // 4)
    held = [(sum_a, []), (keep_b, [got_b])]
    attended = attend(lengths, page_table, queries, pool, arrived, senders)
    after = []
    for number, partners in enumerate(reversed(stages)):
        keep, *send = fold(held, len(partners) + 1, *(after if number == 1 else []))
        held = [(keep, [trade(x, bit) for x, bit in list(zip(send, partners))[::-1]])]
        after = [hbm(attended)]
    (expert_mix,) = fold(held, 1, out=jax.ShapeDtypeStruct(hidden.shape, bf16))
    return expert_mix, attended


def solution(mesh):
    rows = P(("inst", "ep", "dp"), None)
    in_specs = (
        rows,
        rows,
        rows,
        P("ep", None, "dp"),
        P("ep", None, "dp"),
        P("ep", "dp", None),
        rows,
        rows,
        P(("inst", "ep", "dp")),
        rows,
        rows,
        rows,
    )
    return jax.shard_map(body, mesh=mesh, in_specs=in_specs, out_specs=(rows, rows), check_vma=False)
```

```python
import functools

import jax
import jax.numpy as jnp
from jax import lax
from jax.experimental import pallas as pl
from jax.experimental.pallas import tpu as pltpu
from jax.sharding import PartitionSpec as P

HEADS = 64
LAT = 576
VL = 512
MCAP = 2
PAGE = 32
LANES = 128
AXES = ("ep", "dp")
MIB = 1 << 20
MERGE_FLOPS = 20_000_000_000

score_scale = 192.0 ** (-0.5)
bf16 = jnp.bfloat16
f32 = jnp.float32


def in_vmem():
    return pl.BlockSpec(memory_space=pltpu.VMEM)


def in_smem():
    return pl.BlockSpec(memory_space=pltpu.SMEM)


def vmem(x):
    return pltpu.with_memory_space_constraint(x, pltpu.VMEM)


def hbm(x):
    return pltpu.with_memory_space_constraint(x, pltpu.HBM)


def anywhere():
    return pl.BlockSpec(memory_space=pl.ANY)


def in_hbm():
    return pl.BlockSpec(memory_space=pltpu.HBM)


def partner_bits(count):
    bits = []
    b = count // 2
    while b:
        bits.append(b)
        b //= 2
    return bits


def swap(x, axes, pairs):
    return lax.ppermute(x, axes, pairs)


def stage_partners(count):
    bits = partner_bits(count)[:-1]
    stages = [(bits[0],)] if len(bits) % 2 else []
    bits = bits[len(bits) % 2 :]
    for high, low in zip(bits[::2], bits[1::2]):
        stages.append((high, high ^ low, low))
    high, far, low = stages[-1]
    return stages[:-1] + [(far, high, low)]


def pairs_of(count, bit):
    return [(i, i ^ bit) for i in range(count)]


def fetch_kernel(*refs):
    count = (len(refs) - 1) // 2
    copies = [pltpu.make_async_copy(refs[i], refs[count + i], refs[-1].at[i]) for i in range(count)]
    for c in copies:
        c.start()
    for c in copies:
        c.wait()


def fetch(*arrays):
    return pl.pallas_call(
        fetch_kernel,
        out_shape=tuple(pltpu.VMEM(x.shape, x.dtype) for x in arrays),
        in_specs=[in_hbm()] * len(arrays),
        out_specs=(in_vmem(),) * len(arrays),
        scratch_shapes=[pltpu.SemaphoreType.DMA((len(arrays),))],
        compiler_params=pltpu.CompilerParams(vmem_limit_bytes=4 * MIB),
        cost_estimate=pl.CostEstimate(flops=MERGE_FLOPS // 16, bytes_accessed=MIB, transcendentals=0),
    )(*[hbm(x) for x in arrays])


def payload_kernel(ep_count, mine_hidden, mine_routes, mine_weight, got_hidden, got_routes, got_weight, out_ref):
    first = lax.rem(lax.axis_index("dp"), 2) == 0
    rows, width = mine_hidden.shape
    half = width // 2

    def in_order(mine, got):
        return jnp.where(first, jnp.concatenate([mine, got], axis=0), jnp.concatenate([got, mine], axis=0))

    def my_half(ref):
        return jnp.where(first, ref[:, :half].astype(f32), ref[:, half:].astype(f32))

    out_ref[:, :half] = in_order(my_half(mine_hidden), my_half(got_hidden)).astype(bf16)
    routes = in_order(mine_routes[...], got_routes[...])
    weight = in_order(mine_weight[...], got_weight[...])
    column = lax.broadcasted_iota(jnp.int32, (2 * rows, LANES), 1)
    expert = jnp.where(column < ep_count, column, column - ep_count)
    total = jnp.zeros((2 * rows, LANES), f32)
    for k in range(routes.shape[1]):
        total += jnp.where(routes[:, k : k + 1] == expert, weight[:, k : k + 1], 0.0)
    high = total.astype(bf16).astype(f32)
    low = total - high
    out_ref[:, half:] = jnp.where(column < ep_count, high, jnp.where(column < 2 * ep_count, low, 0.0)).astype(bf16)


def make_payload(mine, got, ep_count):
    rows, width = mine[0].shape
    return pl.pallas_call(
        functools.partial(payload_kernel, ep_count),
        out_shape=pltpu.VMEM((2 * rows, width // 2 + LANES), bf16),
        in_specs=[in_vmem()] * 6,
        out_specs=in_vmem(),
        compiler_params=pltpu.CompilerParams(vmem_limit_bytes=4 * MIB),
        cost_estimate=pl.CostEstimate(flops=0, bytes_accessed=4 * rows * width, transcendentals=0),
    )(*[vmem(x) for x in mine], *[vmem(x) for x in got])


def merge_kernel(parts, *refs):
    out_ref = refs[-1]
    half = refs[0].shape[0] // 2
    pieces = [r[...].astype(f32) for r in refs[:parts]]
    cores = [p[:half] for p in pieces] + [p[half:] for p in pieces]
    out_ref[...] = jnp.concatenate(cores, axis=0).astype(bf16)


def merge(pieces, flops, *after):
    rows, width = pieces[0].shape
    return pl.pallas_call(
        functools.partial(merge_kernel, len(pieces)),
        out_shape=pltpu.VMEM((len(pieces) * rows, width), bf16),
        in_specs=[in_vmem()] * len(pieces) + [anywhere()] * len(after),
        out_specs=in_vmem(),
        compiler_params=pltpu.CompilerParams(vmem_limit_bytes=4 * MIB),
        cost_estimate=pl.CostEstimate(flops=flops, bytes_accessed=8 * rows * width, transcendentals=0),
    )(*[vmem(p) for p in pieces], *after)


def half_start(width, near):
    core = lax.rem(lax.axis_index("dp"), 2)
    core = core if near else 1 - core
    return pl.multiple_of(core * (width // 2), width // 2)


def padded(x):
    rows = x.shape[0]
    return x if rows >= 128 else jnp.concatenate([x] * (128 // rows), axis=0)


def near_kernel(near_ref, gate_ref, up_ref, gate_out, up_out):
    rows, width = near_ref.shape[0], gate_ref.shape[1]
    at = pl.ds(half_start(width, True), width // 2)
    x = padded(near_ref[:, : width // 2])
    gate_out[...] = jnp.dot(x, gate_ref[0, at, :], preferred_element_type=f32)[:rows]
    up_out[...] = jnp.dot(x, up_ref[0, at, :], preferred_element_type=f32)[:rows]


def row_weights(near_ref, half, ep_count):
    ep = lax.axis_index("ep")
    table = near_ref[:, half:].astype(f32)
    column = lax.broadcasted_iota(jnp.int32, table.shape, 1)
    mine = (column == ep) | (column == ep + ep_count)
    return jnp.sum(jnp.where(mine, table, 0.0), axis=1, keepdims=True)


STEPS = 7


def down_half(inner, row_weight, down_ref, start, keep_ref, send_ref):
    first = lax.rem(lax.axis_index("dp"), 2) == 0
    rows, half = keep_ref.shape
    step = half // STEPS
    x = padded(inner)
    for i in range(STEPS):
        columns = slice(i * step, (i + 1) * step)
        out = jnp.dot(x, down_ref[0, :, start + i * step : start + (i + 1) * step], preferred_element_type=f32)
        out = out[: 2 * rows] * row_weight
        keep_ref[:, columns] = jnp.where(first, out[:rows], out[rows:])
        send_ref[:, columns] = jnp.where(first, out[rows:], out[:rows]).astype(bf16)


def far_kernel(ep_count, near_ref, far_ref, gate_ref, up_ref, gate_in, up_in, down_ref, inner_ref, keep_ref, send_ref):
    rows, width = near_ref.shape[0], gate_ref.shape[1]
    half = width // 2
    at = pl.ds(half_start(width, False), half)
    row_weight = row_weights(near_ref, half, ep_count)
    x = padded(far_ref[:, :half])
    gate = gate_in[...] + jnp.dot(x, gate_ref[0, at, :], preferred_element_type=f32)[:rows]
    up = up_in[...] + jnp.dot(x, up_ref[0, at, :], preferred_element_type=f32)[:rows]
    inner = (gate / (1.0 + jnp.exp(-gate)) * up).astype(bf16)
    inner_ref[...] = inner
    down_half(inner, row_weight, down_ref, 0, keep_ref, send_ref)


def rest_kernel(ep_count, near_ref, inner_ref, down_ref, keep_ref, send_ref):
    half = keep_ref.shape[1]
    down_half(inner_ref[...], row_weights(near_ref, half, ep_count), down_ref, half, keep_ref, send_ref)


def estimate(rows, weights):
    return pl.CostEstimate(flops=2 * rows * weights, bytes_accessed=2 * weights, transcendentals=0)


def near_products(near, gate, up):
    rows = near.shape[0]
    width, units = gate.shape[1:]
    acc = pltpu.VMEM((rows, units), f32)
    return pl.pallas_call(
        near_kernel,
        out_shape=(acc, acc),
        in_specs=[in_vmem()] * 3,
        out_specs=(in_vmem(),) * 2,
        compiler_params=pltpu.CompilerParams(vmem_limit_bytes=8 * MIB),
        cost_estimate=estimate(rows, width * units),
    )(vmem(near), gate, up)


def far_products(near, far, gate, up, gate_acc, up_acc, down, ep_count):
    rows = near.shape[0]
    units, width = down.shape[1:]
    half = width // 2
    return pl.pallas_call(
        functools.partial(far_kernel, ep_count),
        out_shape=(
            pltpu.VMEM((rows, units), bf16),
            pltpu.VMEM((rows // 2, half), f32),
            pltpu.VMEM((rows // 2, half), bf16),
        ),
        in_specs=[in_vmem()] * 7,
        out_specs=(in_vmem(),) * 3,
        compiler_params=pltpu.CompilerParams(vmem_limit_bytes=8 * MIB),
        cost_estimate=estimate(rows, 3 * half * units),
    )(vmem(near), vmem(far), gate, up, vmem(gate_acc), vmem(up_acc), down)


def rest_products(near, inner, down, ep_count):
    rows = near.shape[0]
    units, width = down.shape[1:]
    half = width // 2
    return pl.pallas_call(
        functools.partial(rest_kernel, ep_count),
        out_shape=(pltpu.VMEM((rows // 2, half), f32), pltpu.VMEM((rows // 2, half), bf16)),
        in_specs=[in_vmem()] * 3,
        out_specs=(in_vmem(),) * 2,
        compiler_params=pltpu.CompilerParams(vmem_limit_bytes=8 * MIB),
        cost_estimate=estimate(rows, half * units),
    )(vmem(near), vmem(inner), down)


def fold_kernel(arrived, parts, *refs):
    outs = refs[-parts:]
    rows = outs[0].shape[0]
    start = at = 0
    for number in arrived:
        ours = refs[at : at + 1 + number]
        at += 1 + number
        total = ours[0][...]
        for g in ours[1:]:
            total += g[...].astype(f32)
        columns = slice(start, start + total.shape[1])
        start += total.shape[1]
        for i, out in enumerate(outs):
            out[:, columns] = total[i * rows : (i + 1) * rows].astype(out.dtype)


def fold(held, parts, *after, out=None, flops=0):
    rows = held[0][0].shape[0]
    width = sum(keep.shape[1] for keep, _ in held)
    part = (rows // parts, width)
    operands = [vmem(x) for keep, gots in held for x in [keep] + gots]
    shapes = (pltpu.VMEM(part, f32),) + (pltpu.VMEM(part, bf16),) * (parts - 1)
    return pl.pallas_call(
        functools.partial(fold_kernel, [len(gots) for _, gots in held], parts),
        out_shape=shapes if out is None else (out,),
        in_specs=[in_vmem()] * len(operands) + [anywhere()] * len(after),
        out_specs=(in_vmem(),) * parts,
        compiler_params=pltpu.CompilerParams(vmem_limit_bytes=4 * MIB),
        cost_estimate=pl.CostEstimate(flops=flops, bytes_accessed=8 * rows * width, transcendentals=0),
    )(*operands, *after)


def pages_kernel(
    dp_count, page_hbm, dest_hbm, pool_ref, after_ref, low_ref, high_ref, copy_ref, page_ref, dest_ref, sems
):
    own, width = pool_ref.shape
    pool_copy = pltpu.make_async_copy(pool_ref, copy_ref, sems.at[0])
    page_copy = pltpu.make_async_copy(page_hbm, page_ref, sems.at[1])
    dest_copy = pltpu.make_async_copy(dest_hbm, dest_ref, sems.at[2])
    page_copy.start()
    dest_copy.start()
    pool_copy.start()
    page_copy.wait()
    dest_copy.wait()
    me = lax.axis_index("dp")
    slots = dp_count * MCAP
    row = lax.broadcasted_iota(jnp.int32, (slots, own), 0)
    column = lax.broadcasted_iota(jnp.int32, (slots, own), 1)
    pick = jnp.zeros((slots, own), f32)
    entries = page_ref.shape[1]
    for m in range(entries):
        rank = jnp.int32(0)
        for n in range(m):
            rank += jnp.where(dest_ref[0, n] == dest_ref[0, m], 1, 0)
        bucket = jnp.bitwise_xor(dest_ref[0, m], me) * MCAP + rank
        pick = jnp.where((row == bucket) & (column == page_ref[0, m]), 1.0, pick)
    pick = pick.astype(bf16)
    step = 2048
    pool_copy.wait()
    for i in range(width // step):
        columns = slice(i * step, (i + 1) * step)
        out = jnp.dot(pick, copy_ref[:, columns], preferred_element_type=f32)
        low_ref[:, columns] = out[: slots // 2].astype(bf16)
        high_ref[:, columns] = out[slots // 2 :].astype(bf16)


def pick_pages(moved_page, moved_dest, latent_pool, after, dp_count):
    width = latent_pool.shape[1]
    half = pltpu.VMEM((dp_count * MCAP // 2, width), bf16)
    return pl.pallas_call(
        functools.partial(pages_kernel, dp_count),
        out_shape=(half, half, pltpu.VMEM(latent_pool.shape, bf16)),
        in_specs=[in_hbm()] * 3 + [anywhere()],
        out_specs=(in_vmem(),) * 3,
        scratch_shapes=[
            pltpu.SMEM(moved_page.shape, jnp.int32),
            pltpu.SMEM(moved_dest.shape, jnp.int32),
            pltpu.SemaphoreType.DMA((3,)),
        ],
        compiler_params=pltpu.CompilerParams(vmem_limit_bytes=4 * MIB),
        cost_estimate=pl.CostEstimate(flops=0, bytes_accessed=4 * latent_pool.size, transcendentals=0),
    )(hbm(moved_page), hbm(moved_dest), hbm(latent_pool), after)


def rows_kernel(places, *refs):
    out_ref = refs[-1]
    width = out_ref.shape[1]
    step = 2048
    for i in range(width // step):
        columns = slice(i * step, (i + 1) * step)
        pieces = [ref[:, columns].astype(f32)[low:high] for ref, (low, high) in zip(refs, places)]
        out_ref[:, columns] = jnp.concatenate(pieces, axis=0).astype(bf16)


def rows_of(pieces, *after):
    rows = sum(high - low for _, low, high in pieces)
    width = pieces[0][0].shape[1]
    return pl.pallas_call(
        functools.partial(rows_kernel, [(low, high) for _, low, high in pieces]),
        out_shape=pltpu.VMEM((rows, width), bf16),
        in_specs=[in_vmem()] * len(pieces) + [anywhere()] * len(after),
        out_specs=in_vmem(),
        compiler_params=pltpu.CompilerParams(vmem_limit_bytes=4 * MIB),
        cost_estimate=pl.CostEstimate(flops=0, bytes_accessed=4 * rows * width, transcendentals=0),
    )(*[vmem(x) for x, _, _ in pieces], *after)


def exchange_pages(low, high, dp_count, after):
    blocks, senders = [(low, 0, low.shape[0])], [0]
    sent = high
    for bit in partner_bits(dp_count):
        got = swap(sent, "dp", pairs_of(dp_count, bit))
        size = got.shape[0] // len(blocks)
        blocks = blocks + [(got, i * size, (i + 1) * size) for i in range(len(blocks))]
        senders = senders + [s ^ bit for s in senders]
        if size > MCAP:
            sent = rows_of([(x, start + size // 2, end) for x, start, end in blocks], after)
            after = sent
            blocks = [(x, start, start + size // 2) for x, start, _ in blocks]
    return rows_of(blocks), senders, after


def attend_kernel(senders, length_ref, table_ref, query_ref, pool_ref, arrived_ref, out_ref, query_rows):
    rows_dev = query_ref.shape[0]
    own, width = pool_ref.shape
    arrived = arrived_ref.shape[0]
    slots = -(-(own + arrived) // 16) * 16
    pair_width = 2 * LAT
    pairs = width // pair_width
    me = lax.axis_index("dp")

    for h in range(HEADS // 2):
        query_rows[h * rows_dev : (h + 1) * rows_dev, :] = query_ref[:, h * pair_width : (h + 1) * pair_width].astype(f32)
    straight = query_rows[...]
    turned = pltpu.roll(straight, LAT, 1)
    first = lax.broadcasted_iota(jnp.int32, straight.shape, 1) < LAT
    query_all = jnp.concatenate(
        [
            jnp.where(first, straight, 0.0),
            jnp.where(first, turned, 0.0),
            jnp.where(first, 0.0, turned),
            jnp.where(first, 0.0, straight),
        ],
        axis=0,
    ).astype(bf16)

    pieces = []
    for j in range(pairs):
        columns = slice(j * pair_width, (j + 1) * pair_width)
        parts = [pool_ref[:, columns].astype(f32), arrived_ref[:, columns].astype(f32)]
        if slots > own + arrived:
            parts.append(jnp.zeros((slots - own - arrived, pair_width), f32))
        pieces.append(jnp.concatenate(parts, axis=0).astype(bf16))
    keys = jnp.concatenate(pieces, axis=0)

    scores = lax.dot_general(query_all, keys, (((1,), (1,)), ((), ())), preferred_element_type=f32) * score_scale

    column = lax.broadcasted_iota(jnp.int32, (1, pairs * slots), 1)
    pair = column // slots
    place = column - pair * slots
    slot = place
    for i, s in enumerate(senders):
        source = jnp.bitwise_xor(me, s)
        for k in range(MCAP):
            slot = jnp.where(place == own + i * MCAP + k, own + source * MCAP + k, slot)
    limits = []
    for r in range(rows_dev):
        limit = jnp.full(column.shape, -1, jnp.int32)
        for p in range(table_ref.shape[1]):
            limit = jnp.where(slot == table_ref[r, p], length_ref[r] - p * PAGE, limit)
        limit = jnp.where(place < own + arrived, limit, -1)
        limits.append(limit - 2 * pair)
    half = scores.shape[0] // 2
    row = lax.broadcasted_iota(jnp.int32, (half, 1), 0) % rows_dev
    limit = limits[0]
    for r in range(1, rows_dev):
        limit = jnp.where(row == r, limits[r], limit)
    even = jnp.where(limit > 0, scores[:half], -jnp.inf)
    odd = jnp.where(limit > 1, scores[half:], -jnp.inf)
    peak = jnp.maximum(jnp.max(even, axis=1, keepdims=True), jnp.max(odd, axis=1, keepdims=True))
    even = jnp.exp(even - peak)
    odd = jnp.exp(odd - peak)
    total = jnp.sum(even, axis=1, keepdims=True) + jnp.sum(odd, axis=1, keepdims=True)
    even = (even / total).astype(bf16)
    odd = (odd / total).astype(bf16)
    from_even = jnp.dot(even, keys[:, :VL], preferred_element_type=f32)
    from_odd = jnp.dot(odd, keys[:, VL:], preferred_element_type=f32)
    shift = LAT - VL
    wide = pair_width - VL
    attended = from_even + pltpu.roll(from_odd, wide - shift, 1)[:, :VL]
    for h in range(HEADS):
        at = (h % 2) * (half // 2) + (h // 2) * rows_dev
        out_ref[:, h * VL : (h + 1) * VL] = attended[at : at + rows_dev].astype(bf16)


def attend(lengths, page_table, queries, latent_pool, arrived, senders):
    rows_dev = queries.shape[0]
    return pl.pallas_call(
        functools.partial(attend_kernel, senders),
        out_shape=jax.ShapeDtypeStruct((rows_dev, HEADS * VL), bf16),
        in_specs=[in_smem(), in_smem(), in_vmem(), in_vmem(), in_vmem()],
        out_specs=in_vmem(),
        scratch_shapes=[pltpu.VMEM((HEADS // 2 * rows_dev, 2 * LAT), f32)],
        compiler_params=pltpu.CompilerParams(vmem_limit_bytes=16 * MIB),
        cost_estimate=pl.CostEstimate(flops=1 << 30, bytes_accessed=4 << 20, transcendentals=1 << 17),
    )(lengths, page_table, queries, vmem(latent_pool), vmem(arrived))


def body(
    hidden,
    routes,
    route_weight,
    gate_weight,
    up_weight,
    down_weight,
    queries,
    latent_pool,
    lengths,
    page_table,
    moved_page,
    moved_dest,
):
    ep_count = lax.axis_size("ep")
    dp_count = lax.axis_size("dp")
    count = ep_count * dp_count
    stages = stage_partners(count)

    def trade(x, bit):
        return swap(x, AXES, pairs_of(count, bit))

    mine = (hidden, routes, route_weight)
    got = [trade(x, 1) for x in mine]
    near = make_payload(fetch(*mine), got, ep_count)
    for number, partners in enumerate(stages):
        got = [trade(near, bit) for bit in partners]
        after = []
        if number == 0:
            low, high, pool = pick_pages(moved_page, moved_dest, latent_pool, near, dp_count)
            after = [high]
        if number == len(stages) - 1:
            arrived, senders, sent = exchange_pages(low, high, dp_count, got[0])
            after = [sent]
        near = merge([near] + got, MERGE_FLOPS if number < len(stages) - 1 else MERGE_FLOPS // 4, *after)
    far = trade(near, 1)
    gate_acc, up_acc = near_products(near, gate_weight, up_weight)
    inner, keep_a, send_a = far_products(
        near, far, gate_weight, up_weight, gate_acc, up_acc, down_weight, ep_count
    )
    got_a = trade(send_a, 1)
    keep_b, send_b = rest_products(near, inner, down_weight, ep_count)
    got_b = trade(send_b, 1)
    (sum_a,) = fold([(keep_a, [got_a])], 1, out=pltpu.VMEM(keep_a.shape, f32), flops=MERGE_FLOPS // 4)
    held = [(sum_a, []), (keep_b, [got_b])]
    attended = attend(lengths, page_table, queries, pool, arrived, senders)
    after = []
    for number, partners in enumerate(reversed(stages)):
        keep, *send = fold(held, len(partners) + 1, *(after if number == 1 else []))
        held = [(keep, [trade(x, bit) for x, bit in zip(send, partners)])]
        after = [hbm(attended)]
    (expert_mix,) = fold(held, 1, out=jax.ShapeDtypeStruct(hidden.shape, bf16))
    return expert_mix, attended


def solution(mesh):
    rows = P(("inst", "ep", "dp"), None)
    in_specs = (
        rows,
        rows,
        rows,
        P("ep", None, "dp"),
        P("ep", None, "dp"),
        P("ep", "dp", None),
        rows,
        rows,
        P(("inst", "ep", "dp")),
        rows,
        rows,
        rows,
    )
    return jax.shard_map(body, mesh=mesh, in_specs=in_specs, out_specs=(rows, rows), check_vma=False)
```

```python
import functools

import jax
import jax.numpy as jnp
from jax import lax
from jax.experimental import pallas as pl
from jax.experimental.pallas import tpu as pltpu
from jax.sharding import PartitionSpec as P

HEADS = 64
LAT = 576
VL = 512
MCAP = 2
PAGE = 32
LANES = 128
AXES = ("ep", "dp")
MIB = 1 << 20
MERGE_FLOPS = 20_000_000_000

score_scale = 192.0 ** (-0.5)
bf16 = jnp.bfloat16
f32 = jnp.float32


def in_vmem():
    return pl.BlockSpec(memory_space=pltpu.VMEM)


def in_smem():
    return pl.BlockSpec(memory_space=pltpu.SMEM)


def vmem(x):
    return pltpu.with_memory_space_constraint(x, pltpu.VMEM)


def hbm(x):
    return pltpu.with_memory_space_constraint(x, pltpu.HBM)


def anywhere():
    return pl.BlockSpec(memory_space=pl.ANY)


def in_hbm():
    return pl.BlockSpec(memory_space=pltpu.HBM)


def partner_bits(count):
    bits = []
    b = count // 2
    while b:
        bits.append(b)
        b //= 2
    return bits


def swap(x, axes, pairs):
    return lax.ppermute(x, axes, pairs)


def stage_partners(count):
    bits = partner_bits(count)[:-1]
    stages = [(bits[0],)] if len(bits) % 2 else []
    bits = bits[len(bits) % 2 :]
    for high, low in zip(bits[::2], bits[1::2]):
        stages.append((high, high ^ low, low))
    high, far, low = stages[-1]
    return stages[:-1] + [(far, high, low)]


def pairs_of(count, bit):
    return [(i, i ^ bit) for i in range(count)]


def fetch_kernel(*refs):
    count = (len(refs) - 1) // 2
    copies = [pltpu.make_async_copy(refs[i], refs[count + i], refs[-1].at[i]) for i in range(count)]
    for c in copies:
        c.start()
    for c in copies:
        c.wait()


def fetch(*arrays):
    return pl.pallas_call(
        fetch_kernel,
        out_shape=tuple(pltpu.VMEM(x.shape, x.dtype) for x in arrays),
        in_specs=[in_hbm()] * len(arrays),
        out_specs=(in_vmem(),) * len(arrays),
        scratch_shapes=[pltpu.SemaphoreType.DMA((len(arrays),))],
        compiler_params=pltpu.CompilerParams(vmem_limit_bytes=4 * MIB),
        cost_estimate=pl.CostEstimate(flops=MERGE_FLOPS // 16, bytes_accessed=MIB, transcendentals=0),
    )(*[hbm(x) for x in arrays])


def payload_kernel(ep_count, mine_hidden, mine_routes, mine_weight, got_hidden, got_routes, got_weight, out_ref):
    first = lax.rem(lax.axis_index("dp"), 2) == 0
    rows, width = mine_hidden.shape
    half = width // 2

    def in_order(mine, got):
        return jnp.where(first, jnp.concatenate([mine, got], axis=0), jnp.concatenate([got, mine], axis=0))

    def my_half(ref):
        return jnp.where(first, ref[:, :half].astype(f32), ref[:, half:].astype(f32))

    out_ref[:, :half] = in_order(my_half(mine_hidden), my_half(got_hidden)).astype(bf16)
    routes = in_order(mine_routes[...], got_routes[...])
    weight = in_order(mine_weight[...], got_weight[...])
    column = lax.broadcasted_iota(jnp.int32, (2 * rows, LANES), 1)
    expert = jnp.where(column < ep_count, column, column - ep_count)
    total = jnp.zeros((2 * rows, LANES), f32)
    for k in range(routes.shape[1]):
        total += jnp.where(routes[:, k : k + 1] == expert, weight[:, k : k + 1], 0.0)
    high = total.astype(bf16).astype(f32)
    low = total - high
    out_ref[:, half:] = jnp.where(column < ep_count, high, jnp.where(column < 2 * ep_count, low, 0.0)).astype(bf16)


def make_payload(mine, got, ep_count):
    rows, width = mine[0].shape
    return pl.pallas_call(
        functools.partial(payload_kernel, ep_count),
        out_shape=pltpu.VMEM((2 * rows, width // 2 + LANES), bf16),
        in_specs=[in_vmem()] * 6,
        out_specs=in_vmem(),
        compiler_params=pltpu.CompilerParams(vmem_limit_bytes=4 * MIB),
        cost_estimate=pl.CostEstimate(flops=0, bytes_accessed=4 * rows * width, transcendentals=0),
    )(*[vmem(x) for x in mine], *[vmem(x) for x in got])


def merge_kernel(parts, *refs):
    out_ref = refs[-1]
    half = refs[0].shape[0] // 2
    pieces = [r[...].astype(f32) for r in [refs[0], *refs[1:parts][::-1]]]
    cores = [p[:half] for p in pieces] + [p[half:] for p in pieces]
    out_ref[...] = jnp.concatenate(cores, axis=0).astype(bf16)


def merge(pieces, flops, *after):
    rows, width = pieces[0].shape
    return pl.pallas_call(
        functools.partial(merge_kernel, len(pieces)),
        out_shape=pltpu.VMEM((len(pieces) * rows, width), bf16),
        in_specs=[in_vmem()] * len(pieces) + [anywhere()] * len(after),
        out_specs=in_vmem(),
        compiler_params=pltpu.CompilerParams(vmem_limit_bytes=4 * MIB),
        cost_estimate=pl.CostEstimate(flops=flops, bytes_accessed=8 * rows * width, transcendentals=0),
    )(*[vmem(p) for p in pieces[:1] + pieces[:0:-1]], *after)


def half_start(width, near):
    core = lax.rem(lax.axis_index("dp"), 2)
    core = core if near else 1 - core
    return pl.multiple_of(core * (width // 2), width // 2)


def padded(x):
    rows = x.shape[0]
    return x if rows >= 128 else jnp.concatenate([x] * (128 // rows), axis=0)


def near_kernel(near_ref, gate_ref, up_ref, gate_out, up_out):
    rows, width = near_ref.shape[0], gate_ref.shape[1]
    at = pl.ds(half_start(width, True), width // 2)
    x = padded(near_ref[:, : width // 2])
    gate_out[...] = jnp.dot(x, gate_ref[0, at, :], preferred_element_type=f32)[:rows]
    up_out[...] = jnp.dot(x, up_ref[0, at, :], preferred_element_type=f32)[:rows]


def row_weights(near_ref, half, ep_count):
    ep = lax.axis_index("ep")
    table = near_ref[:, half:].astype(f32)
    column = lax.broadcasted_iota(jnp.int32, table.shape, 1)
    mine = (column == ep) | (column == ep + ep_count)
    return jnp.sum(jnp.where(mine, table, 0.0), axis=1, keepdims=True)


STEPS = 7


def down_half(inner, row_weight, down_ref, start, keep_ref, send_ref):
    first = lax.rem(lax.axis_index("dp"), 2) == 0
    rows, half = keep_ref.shape
    step = half // STEPS
    x = padded(inner)
    for i in range(STEPS):
        columns = slice(i * step, (i + 1) * step)
        out = jnp.dot(x, down_ref[0, :, start + i * step : start + (i + 1) * step], preferred_element_type=f32)
        out = out[: 2 * rows] * row_weight
        keep_ref[:, columns] = jnp.where(first, out[:rows], out[rows:])
        send_ref[:, columns] = jnp.where(first, out[rows:], out[:rows]).astype(bf16)


def far_kernel(ep_count, near_ref, far_ref, gate_ref, up_ref, gate_in, up_in, down_ref, inner_ref, keep_ref, send_ref):
    rows, width = near_ref.shape[0], gate_ref.shape[1]
    half = width // 2
    at = pl.ds(half_start(width, False), half)
    row_weight = row_weights(near_ref, half, ep_count)
    x = padded(far_ref[:, :half])
    gate = gate_in[...] + jnp.dot(x, gate_ref[0, at, :], preferred_element_type=f32)[:rows]
    up = up_in[...] + jnp.dot(x, up_ref[0, at, :], preferred_element_type=f32)[:rows]
    inner = (gate / (1.0 + jnp.exp(-gate)) * up).astype(bf16)
    inner_ref[...] = inner
    down_half(inner, row_weight, down_ref, 0, keep_ref, send_ref)


def rest_kernel(ep_count, near_ref, inner_ref, down_ref, keep_ref, send_ref):
    half = keep_ref.shape[1]
    down_half(inner_ref[...], row_weights(near_ref, half, ep_count), down_ref, half, keep_ref, send_ref)


def estimate(rows, weights):
    return pl.CostEstimate(flops=2 * rows * weights, bytes_accessed=2 * weights, transcendentals=0)


def near_products(near, gate, up):
    rows = near.shape[0]
    width, units = gate.shape[1:]
    acc = pltpu.VMEM((rows, units), f32)
    return pl.pallas_call(
        near_kernel,
        out_shape=(acc, acc),
        in_specs=[in_vmem()] * 3,
        out_specs=(in_vmem(),) * 2,
        compiler_params=pltpu.CompilerParams(vmem_limit_bytes=8 * MIB),
        cost_estimate=estimate(rows, width * units),
    )(vmem(near), gate, up)


def far_products(near, far, gate, up, gate_acc, up_acc, down, ep_count):
    rows = near.shape[0]
    units, width = down.shape[1:]
    half = width // 2
    return pl.pallas_call(
        functools.partial(far_kernel, ep_count),
        out_shape=(
            pltpu.VMEM((rows, units), bf16),
            pltpu.VMEM((rows // 2, half), f32),
            pltpu.VMEM((rows // 2, half), bf16),
        ),
        in_specs=[in_vmem()] * 7,
        out_specs=(in_vmem(),) * 3,
        compiler_params=pltpu.CompilerParams(vmem_limit_bytes=8 * MIB),
        cost_estimate=estimate(rows, 3 * half * units),
    )(vmem(near), vmem(far), gate, up, vmem(gate_acc), vmem(up_acc), down)


def rest_products(near, inner, down, ep_count):
    rows = near.shape[0]
    units, width = down.shape[1:]
    half = width // 2
    return pl.pallas_call(
        functools.partial(rest_kernel, ep_count),
        out_shape=(pltpu.VMEM((rows // 2, half), f32), pltpu.VMEM((rows // 2, half), bf16)),
        in_specs=[in_vmem()] * 3,
        out_specs=(in_vmem(),) * 2,
        compiler_params=pltpu.CompilerParams(vmem_limit_bytes=8 * MIB),
        cost_estimate=estimate(rows, half * units),
    )(vmem(near), vmem(inner), down)


def fold_kernel(arrived, parts, *refs):
    outs = refs[-parts:]
    rows = outs[0].shape[0]
    start = at = 0
    for number in arrived:
        ours = refs[at : at + 1 + number]
        at += 1 + number
        total = ours[0][...]
        for g in ours[1:]:
            total += g[...].astype(f32)
        columns = slice(start, start + total.shape[1])
        start += total.shape[1]
        for i, out in enumerate(outs):
            out[:, columns] = total[i * rows : (i + 1) * rows].astype(out.dtype)


def fold(held, parts, *after, out=None, flops=0):
    rows = held[0][0].shape[0]
    width = sum(keep.shape[1] for keep, _ in held)
    part = (rows // parts, width)
    operands = [vmem(x) for keep, gots in held for x in [keep] + gots]
    shapes = (pltpu.VMEM(part, f32),) + (pltpu.VMEM(part, bf16),) * (parts - 1)
    return pl.pallas_call(
        functools.partial(fold_kernel, [len(gots) for _, gots in held], parts),
        out_shape=shapes if out is None else (out,),
        in_specs=[in_vmem()] * len(operands) + [anywhere()] * len(after),
        out_specs=(in_vmem(),) * parts,
        compiler_params=pltpu.CompilerParams(vmem_limit_bytes=4 * MIB),
        cost_estimate=pl.CostEstimate(flops=flops, bytes_accessed=8 * rows * width, transcendentals=0),
    )(*operands, *after)


def pages_kernel(
    dp_count, page_hbm, dest_hbm, pool_ref, after_ref, low_ref, high_ref, copy_ref, page_ref, dest_ref, sems
):
    own, width = pool_ref.shape
    pool_copy = pltpu.make_async_copy(pool_ref, copy_ref, sems.at[0])
    page_copy = pltpu.make_async_copy(page_hbm, page_ref, sems.at[1])
    dest_copy = pltpu.make_async_copy(dest_hbm, dest_ref, sems.at[2])
    page_copy.start()
    dest_copy.start()
    pool_copy.start()
    page_copy.wait()
    dest_copy.wait()
    me = lax.axis_index("dp")
    slots = dp_count * MCAP
    row = lax.broadcasted_iota(jnp.int32, (slots, own), 0)
    column = lax.broadcasted_iota(jnp.int32, (slots, own), 1)
    pick = jnp.zeros((slots, own), f32)
    entries = page_ref.shape[1]
    for m in range(entries):
        rank = jnp.int32(0)
        for n in range(m):
            rank += jnp.where(dest_ref[0, n] == dest_ref[0, m], 1, 0)
        bucket = jnp.bitwise_xor(dest_ref[0, m], me) * MCAP + rank
        pick = jnp.where((row == bucket) & (column == page_ref[0, m]), 1.0, pick)
    pick = pick.astype(bf16)
    step = 2048
    pool_copy.wait()
    for i in range(width // step):
        columns = slice(i * step, (i + 1) * step)
        out = jnp.dot(pick, copy_ref[:, columns], preferred_element_type=f32)
        low_ref[:, columns] = out[: slots // 2].astype(bf16)
        high_ref[:, columns] = out[slots // 2 :].astype(bf16)


def pick_pages(moved_page, moved_dest, latent_pool, after, dp_count):
    width = latent_pool.shape[1]
    half = pltpu.VMEM((dp_count * MCAP // 2, width), bf16)
    return pl.pallas_call(
        functools.partial(pages_kernel, dp_count),
        out_shape=(half, half, pltpu.VMEM(latent_pool.shape, bf16)),
        in_specs=[in_hbm()] * 3 + [anywhere()],
        out_specs=(in_vmem(),) * 3,
        scratch_shapes=[
            pltpu.SMEM(moved_page.shape, jnp.int32),
            pltpu.SMEM(moved_dest.shape, jnp.int32),
            pltpu.SemaphoreType.DMA((3,)),
        ],
        compiler_params=pltpu.CompilerParams(vmem_limit_bytes=4 * MIB),
        cost_estimate=pl.CostEstimate(flops=0, bytes_accessed=4 * latent_pool.size, transcendentals=0),
    )(hbm(moved_page), hbm(moved_dest), hbm(latent_pool), after)


def rows_kernel(places, *refs):
    out_ref = refs[-1]
    width = out_ref.shape[1]
    step = 2048
    for i in range(width // step):
        columns = slice(i * step, (i + 1) * step)
        pieces = [ref[:, columns].astype(f32)[low:high] for ref, (low, high) in zip(refs, places)]
        out_ref[:, columns] = jnp.concatenate(pieces, axis=0).astype(bf16)


def rows_of(pieces, *after):
    rows = sum(high - low for _, low, high in pieces)
    width = pieces[0][0].shape[1]
    return pl.pallas_call(
        functools.partial(rows_kernel, [(low, high) for _, low, high in pieces]),
        out_shape=pltpu.VMEM((rows, width), bf16),
        in_specs=[in_vmem()] * len(pieces) + [anywhere()] * len(after),
        out_specs=in_vmem(),
        compiler_params=pltpu.CompilerParams(vmem_limit_bytes=4 * MIB),
        cost_estimate=pl.CostEstimate(flops=0, bytes_accessed=4 * rows * width, transcendentals=0),
    )(*[vmem(x) for x, _, _ in pieces], *after)


def exchange_pages(low, first, dp_count, after):
    blocks, senders = [(low, 0, low.shape[0])], [0]
    got = first
    for number, bit in enumerate(partner_bits(dp_count)):
        if number:
            got = swap(sent, "dp", pairs_of(dp_count, bit))
        size = got.shape[0] // len(blocks)
        blocks = blocks + [(got, i * size, (i + 1) * size) for i in range(len(blocks))]
        senders = senders + [s ^ bit for s in senders]
        if size > MCAP:
            sent = rows_of([(x, start + size // 2, end) for x, start, end in blocks], after)
            blocks = [(x, start, start + size // 2) for x, start, _ in blocks]
    return rows_of(blocks), senders


def attend_kernel(senders, length_ref, table_ref, query_ref, pool_ref, arrived_ref, out_ref, query_rows):
    rows_dev = query_ref.shape[0]
    own, width = pool_ref.shape
    arrived = arrived_ref.shape[0]
    slots = -(-(own + arrived) // 16) * 16
    pair_width = 2 * LAT
    pairs = width // pair_width
    me = lax.axis_index("dp")

    for h in range(HEADS // 2):
        query_rows[h * rows_dev : (h + 1) * rows_dev, :] = query_ref[:, h * pair_width : (h + 1) * pair_width].astype(f32)
    straight = query_rows[...]
    turned = pltpu.roll(straight, LAT, 1)
    first = lax.broadcasted_iota(jnp.int32, straight.shape, 1) < LAT
    query_all = jnp.concatenate(
        [
            jnp.where(first, straight, 0.0),
            jnp.where(first, turned, 0.0),
            jnp.where(first, 0.0, turned),
            jnp.where(first, 0.0, straight),
        ],
        axis=0,
    ).astype(bf16)

    pieces = []
    for j in range(pairs):
        columns = slice(j * pair_width, (j + 1) * pair_width)
        parts = [pool_ref[:, columns].astype(f32), arrived_ref[:, columns].astype(f32)]
        if slots > own + arrived:
            parts.append(jnp.zeros((slots - own - arrived, pair_width), f32))
        pieces.append(jnp.concatenate(parts, axis=0).astype(bf16))
    keys = jnp.concatenate(pieces, axis=0)

    scores = lax.dot_general(query_all, keys, (((1,), (1,)), ((), ())), preferred_element_type=f32) * score_scale

    column = lax.broadcasted_iota(jnp.int32, (1, pairs * slots), 1)
    pair = column // slots
    place = column - pair * slots
    slot = place
    for i, s in enumerate(senders):
        source = jnp.bitwise_xor(me, s)
        for k in range(MCAP):
            slot = jnp.where(place == own + i * MCAP + k, own + source * MCAP + k, slot)
    limits = []
    for r in range(rows_dev):
        limit = jnp.full(column.shape, -1, jnp.int32)
        for p in range(table_ref.shape[1]):
            limit = jnp.where(slot == table_ref[r, p], length_ref[r] - p * PAGE, limit)
        limit = jnp.where(place < own + arrived, limit, -1)
        limits.append(limit - 2 * pair)
    half = scores.shape[0] // 2
    row = lax.broadcasted_iota(jnp.int32, (half, 1), 0) % rows_dev
    limit = limits[0]
    for r in range(1, rows_dev):
        limit = jnp.where(row == r, limits[r], limit)
    even = jnp.where(limit > 0, scores[:half], -jnp.inf)
    odd = jnp.where(limit > 1, scores[half:], -jnp.inf)
    peak = jnp.maximum(jnp.max(even, axis=1, keepdims=True), jnp.max(odd, axis=1, keepdims=True))
    even = jnp.exp(even - peak)
    odd = jnp.exp(odd - peak)
    total = jnp.sum(even, axis=1, keepdims=True) + jnp.sum(odd, axis=1, keepdims=True)
    even = (even / total).astype(bf16)
    odd = (odd / total).astype(bf16)
    from_even = jnp.dot(even, keys[:, :VL], preferred_element_type=f32)
    from_odd = jnp.dot(odd, keys[:, VL:], preferred_element_type=f32)
    shift = LAT - VL
    wide = pair_width - VL
    attended = from_even + pltpu.roll(from_odd, wide - shift, 1)[:, :VL]
    for h in range(HEADS):
        at = (h % 2) * (half // 2) + (h // 2) * rows_dev
        out_ref[:, h * VL : (h + 1) * VL] = attended[at : at + rows_dev].astype(bf16)


def attend(lengths, page_table, queries, latent_pool, arrived, senders):
    rows_dev = queries.shape[0]
    return pl.pallas_call(
        functools.partial(attend_kernel, senders),
        out_shape=jax.ShapeDtypeStruct((rows_dev, HEADS * VL), bf16),
        in_specs=[in_smem(), in_smem(), in_vmem(), in_vmem(), in_vmem()],
        out_specs=in_vmem(),
        scratch_shapes=[pltpu.VMEM((HEADS // 2 * rows_dev, 2 * LAT), f32)],
        compiler_params=pltpu.CompilerParams(vmem_limit_bytes=16 * MIB),
        cost_estimate=pl.CostEstimate(flops=1 << 30, bytes_accessed=4 << 20, transcendentals=1 << 17),
    )(lengths, page_table, queries, vmem(latent_pool), vmem(arrived))


def body(
    hidden,
    routes,
    route_weight,
    gate_weight,
    up_weight,
    down_weight,
    queries,
    latent_pool,
    lengths,
    page_table,
    moved_page,
    moved_dest,
):
    ep_count = lax.axis_size("ep")
    dp_count = lax.axis_size("dp")
    count = ep_count * dp_count
    stages = stage_partners(count)

    def trade(x, bit):
        return swap(x, AXES, pairs_of(count, bit))

    mine = (hidden, routes, route_weight)
    got = [trade(x, 1) for x in mine]
    near = make_payload(fetch(*mine), got, ep_count)
    for number, partners in enumerate(stages):
        got = [trade(near, bit) for bit in partners]
        after = []
        if number == 0:
            low, high, pool = pick_pages(moved_page, moved_dest, latent_pool, near, dp_count)
            after = [high]
            bit = partner_bits(dp_count)[0]
            first = swap(high, "dp", pairs_of(dp_count, bit))
        if number == len(stages) - 1:
            after = [first]
        near = merge([near] + got, MERGE_FLOPS if number < len(stages) - 1 else MERGE_FLOPS // 4, *after)
    far = trade(near, 1)
    gate_acc, up_acc = near_products(near, gate_weight, up_weight)
    inner, keep_a, send_a = far_products(
        near, far, gate_weight, up_weight, gate_acc, up_acc, down_weight, ep_count
    )
    got_a = trade(send_a, 1)
    keep_b, send_b = rest_products(near, inner, down_weight, ep_count)
    got_b = trade(send_b, 1)
    (sum_a,) = fold([(keep_a, [got_a])], 1, out=pltpu.VMEM(keep_a.shape, f32), flops=MERGE_FLOPS // 4)
    held = [(sum_a, []), (keep_b, [got_b])]
    after = []
    for number, partners in enumerate(reversed(stages)):
        keep, *send = fold(held, len(partners) + 1, *(after if number == 1 else []))
        held = [(keep, [trade(x, bit) for x, bit in zip(send, partners)])]
        if number == 0:
            arrived, senders = exchange_pages(low, first, dp_count, keep)
            attended = attend(lengths, page_table, queries, pool, arrived, senders)
            after = [hbm(attended)]
    (expert_mix,) = fold(held, 1, out=jax.ShapeDtypeStruct(hidden.shape, bf16))
    return expert_mix, attended


def solution(mesh):
    rows = P(("inst", "ep", "dp"), None)
    in_specs = (
        rows,
        rows,
        rows,
        P("ep", None, "dp"),
        P("ep", None, "dp"),
        P("ep", "dp", None),
        rows,
        rows,
        P(("inst", "ep", "dp")),
        rows,
        rows,
        rows,
    )
    return jax.shard_map(body, mesh=mesh, in_specs=in_specs, out_specs=(rows, rows), check_vma=False)
```

```python
import functools

import jax
import jax.numpy as jnp
from jax import lax
from jax.experimental import pallas as pl
from jax.experimental.pallas import tpu as pltpu
from jax.sharding import PartitionSpec as P

HEADS = 64
LAT = 576
VL = 512
MCAP = 2
PAGE = 32
LANES = 128
AXES = ("ep", "dp")
MIB = 1 << 20
MERGE_FLOPS = 20_000_000_000

score_scale = 192.0 ** (-0.5)
bf16 = jnp.bfloat16
f32 = jnp.float32


def in_vmem():
    return pl.BlockSpec(memory_space=pltpu.VMEM)


def in_smem():
    return pl.BlockSpec(memory_space=pltpu.SMEM)


def vmem(x):
    return pltpu.with_memory_space_constraint(x, pltpu.VMEM)


def hbm(x):
    return pltpu.with_memory_space_constraint(x, pltpu.HBM)


def anywhere():
    return pl.BlockSpec(memory_space=pl.ANY)


def in_hbm():
    return pl.BlockSpec(memory_space=pltpu.HBM)


def partner_bits(count):
    bits = []
    b = count // 2
    while b:
        bits.append(b)
        b //= 2
    return bits


def swap(x, axes, pairs):
    return lax.ppermute(x, axes, pairs)


def stage_partners(count):
    bits = partner_bits(count)[:-1]
    stages = [(bits[0],)] if len(bits) % 2 else []
    bits = bits[len(bits) % 2 :]
    for high, low in zip(bits[::2], bits[1::2]):
        stages.append((high, high ^ low, low))
    high, far, low = stages[-1]
    return stages[:-1] + [(far, high, low)]


def pairs_of(count, bit):
    return [(i, i ^ bit) for i in range(count)]


def fetch_kernel(*refs):
    count = (len(refs) - 1) // 2
    copies = [pltpu.make_async_copy(refs[i], refs[count + i], refs[-1].at[i]) for i in range(count)]
    for c in copies:
        c.start()
    for c in copies:
        c.wait()


def fetch(*arrays):
    return pl.pallas_call(
        fetch_kernel,
        out_shape=tuple(pltpu.VMEM(x.shape, x.dtype) for x in arrays),
        in_specs=[in_hbm()] * len(arrays),
        out_specs=(in_vmem(),) * len(arrays),
        scratch_shapes=[pltpu.SemaphoreType.DMA((len(arrays),))],
        compiler_params=pltpu.CompilerParams(vmem_limit_bytes=4 * MIB),
        cost_estimate=pl.CostEstimate(flops=MERGE_FLOPS // 16, bytes_accessed=MIB, transcendentals=0),
    )(*[hbm(x) for x in arrays])


def payload_kernel(ep_count, mine_hidden, mine_routes, mine_weight, got_hidden, got_routes, got_weight, out_ref):
    first = lax.rem(lax.axis_index("dp"), 2) == 0
    rows, width = mine_hidden.shape
    half = width // 2

    def in_order(mine, got):
        return jnp.where(first, jnp.concatenate([mine, got], axis=0), jnp.concatenate([got, mine], axis=0))

    def my_half(ref):
        return jnp.where(first, ref[:, :half].astype(f32), ref[:, half:].astype(f32))

    out_ref[:, :half] = in_order(my_half(mine_hidden), my_half(got_hidden)).astype(bf16)
    routes = in_order(mine_routes[...], got_routes[...])
    weight = in_order(mine_weight[...], got_weight[...])
    column = lax.broadcasted_iota(jnp.int32, (2 * rows, LANES), 1)
    expert = jnp.where(column < ep_count, column, column - ep_count)
    total = jnp.zeros((2 * rows, LANES), f32)
    for k in range(routes.shape[1]):
        total += jnp.where(routes[:, k : k + 1] == expert, weight[:, k : k + 1], 0.0)
    high = total.astype(bf16).astype(f32)
    low = total - high
    out_ref[:, half:] = jnp.where(column < ep_count, high, jnp.where(column < 2 * ep_count, low, 0.0)).astype(bf16)


def make_payload(mine, got, ep_count):
    rows, width = mine[0].shape
    return pl.pallas_call(
        functools.partial(payload_kernel, ep_count),
        out_shape=pltpu.VMEM((2 * rows, width // 2 + LANES), bf16),
        in_specs=[in_vmem()] * 6,
        out_specs=in_vmem(),
        compiler_params=pltpu.CompilerParams(vmem_limit_bytes=4 * MIB),
        cost_estimate=pl.CostEstimate(flops=0, bytes_accessed=4 * rows * width, transcendentals=0),
    )(*[vmem(x) for x in mine], *[vmem(x) for x in got])


def merge_kernel(parts, *refs):
    out_ref = refs[-1]
    half = refs[0].shape[0] // 2
    pieces = [r[...].astype(f32) for r in [refs[0], *refs[1:parts][::-1]]]
    cores = [p[:half] for p in pieces] + [p[half:] for p in pieces]
    out_ref[...] = jnp.concatenate(cores, axis=0).astype(bf16)


def merge(pieces, flops, *after):
    rows, width = pieces[0].shape
    return pl.pallas_call(
        functools.partial(merge_kernel, len(pieces)),
        out_shape=pltpu.VMEM((len(pieces) * rows, width), bf16),
        in_specs=[in_vmem()] * len(pieces) + [anywhere()] * len(after),
        out_specs=in_vmem(),
        compiler_params=pltpu.CompilerParams(vmem_limit_bytes=4 * MIB),
        cost_estimate=pl.CostEstimate(flops=flops, bytes_accessed=8 * rows * width, transcendentals=0),
    )(*[vmem(p) for p in pieces[:1] + pieces[:0:-1]], *after)


def half_start(width, near):
    core = lax.rem(lax.axis_index("dp"), 2)
    core = core if near else 1 - core
    return pl.multiple_of(core * (width // 2), width // 2)


def padded(x):
    rows = x.shape[0]
    return x if rows >= 128 else jnp.concatenate([x] * (128 // rows), axis=0)


def near_kernel(near_ref, gate_ref, up_ref, *refs):
    gate_out, up_out = refs[-2:]
    rows, width = near_ref.shape[0], gate_ref.shape[1]
    at = pl.ds(half_start(width, True), width // 2)
    x = padded(near_ref[:, : width // 2])
    gate_out[...] = jnp.dot(x, gate_ref[0, at, :], preferred_element_type=f32)[:rows]
    up_out[...] = jnp.dot(x, up_ref[0, at, :], preferred_element_type=f32)[:rows]


def row_weights(near_ref, half, ep_count):
    ep = lax.axis_index("ep")
    table = near_ref[:, half:].astype(f32)
    column = lax.broadcasted_iota(jnp.int32, table.shape, 1)
    mine = (column == ep) | (column == ep + ep_count)
    return jnp.sum(jnp.where(mine, table, 0.0), axis=1, keepdims=True)


STEPS = 7


def down_half(inner, row_weight, down_ref, start, keep_ref, send_ref):
    first = lax.rem(lax.axis_index("dp"), 2) == 0
    rows, half = keep_ref.shape
    step = half // STEPS
    x = padded(inner)
    for i in range(STEPS):
        columns = slice(i * step, (i + 1) * step)
        out = jnp.dot(x, down_ref[0, :, start + i * step : start + (i + 1) * step], preferred_element_type=f32)
        out = out[: 2 * rows] * row_weight
        keep_ref[:, columns] = jnp.where(first, out[:rows], out[rows:])
        send_ref[:, columns] = jnp.where(first, out[rows:], out[:rows]).astype(bf16)


def far_kernel(ep_count, near_ref, far_ref, gate_ref, up_ref, gate_in, up_in, down_ref, *refs):
    inner_ref, keep_ref, send_ref = refs[-3:]
    rows, width = near_ref.shape[0], gate_ref.shape[1]
    half = width // 2
    at = pl.ds(half_start(width, False), half)
    row_weight = row_weights(near_ref, half, ep_count)
    x = padded(far_ref[:, :half])
    gate = gate_in[...] + jnp.dot(x, gate_ref[0, at, :], preferred_element_type=f32)[:rows]
    up = up_in[...] + jnp.dot(x, up_ref[0, at, :], preferred_element_type=f32)[:rows]
    inner = (gate / (1.0 + jnp.exp(-gate)) * up).astype(bf16)
    inner_ref[...] = inner
    down_half(inner, row_weight, down_ref, 0, keep_ref, send_ref)


def rest_kernel(ep_count, near_ref, inner_ref, down_ref, keep_ref, send_ref):
    half = keep_ref.shape[1]
    down_half(inner_ref[...], row_weights(near_ref, half, ep_count), down_ref, half, keep_ref, send_ref)


def estimate(rows, weights):
    return pl.CostEstimate(flops=2 * rows * weights, bytes_accessed=2 * weights, transcendentals=0)


def near_products(near, gate, up, down, *after):
    rows = near.shape[0]
    width, units = gate.shape[1:]
    acc = pltpu.VMEM((rows, units), f32)
    return pl.pallas_call(
        near_kernel,
        out_shape=(acc, acc),
        in_specs=[in_vmem()] * 4 + [anywhere()] * len(after),
        out_specs=(in_vmem(),) * 2,
        compiler_params=pltpu.CompilerParams(vmem_limit_bytes=8 * MIB),
        cost_estimate=estimate(rows, width * units),
    )(vmem(near), gate, up, down, *after)


def far_products(near, far, gate, up, gate_acc, up_acc, down, ep_count, *after):
    rows = near.shape[0]
    units, width = down.shape[1:]
    half = width // 2
    return pl.pallas_call(
        functools.partial(far_kernel, ep_count),
        out_shape=(
            pltpu.VMEM((rows, units), bf16),
            pltpu.VMEM((rows // 2, half), f32),
            pltpu.VMEM((rows // 2, half), bf16),
        ),
        in_specs=[in_vmem()] * 7 + [anywhere()] * len(after),
        out_specs=(in_vmem(),) * 3,
        compiler_params=pltpu.CompilerParams(vmem_limit_bytes=8 * MIB),
        cost_estimate=estimate(rows, 3 * half * units),
    )(vmem(near), vmem(far), gate, up, vmem(gate_acc), vmem(up_acc), down, *after)


def rest_products(near, inner, down, ep_count):
    rows = near.shape[0]
    units, width = down.shape[1:]
    half = width // 2
    return pl.pallas_call(
        functools.partial(rest_kernel, ep_count),
        out_shape=(pltpu.VMEM((rows // 2, half), f32), pltpu.VMEM((rows // 2, half), bf16)),
        in_specs=[in_vmem()] * 3,
        out_specs=(in_vmem(),) * 2,
        compiler_params=pltpu.CompilerParams(vmem_limit_bytes=8 * MIB),
        cost_estimate=estimate(rows, half * units),
    )(vmem(near), vmem(inner), down)


def fold_kernel(arrived, parts, *refs):
    outs = refs[-parts:]
    rows = outs[0].shape[0]
    start = at = 0
    for number in arrived:
        ours = refs[at : at + 1 + number]
        at += 1 + number
        total = ours[0][...]
        for g in ours[1:]:
            total += g[...].astype(f32)
        columns = slice(start, start + total.shape[1])
        start += total.shape[1]
        for i, out in enumerate(outs):
            out[:, columns] = total[i * rows : (i + 1) * rows].astype(out.dtype)


def fold(held, parts, *after, out=None, flops=0):
    rows = held[0][0].shape[0]
    width = sum(keep.shape[1] for keep, _ in held)
    part = (rows // parts, width)
    operands = [vmem(x) for keep, gots in held for x in [keep] + gots]
    shapes = (pltpu.VMEM(part, f32),) + (pltpu.VMEM(part, bf16),) * (parts - 1)
    return pl.pallas_call(
        functools.partial(fold_kernel, [len(gots) for _, gots in held], parts),
        out_shape=shapes if out is None else (out,),
        in_specs=[in_vmem()] * len(operands) + [anywhere()] * len(after),
        out_specs=(in_vmem(),) * parts,
        compiler_params=pltpu.CompilerParams(vmem_limit_bytes=4 * MIB),
        cost_estimate=pl.CostEstimate(flops=flops, bytes_accessed=8 * rows * width, transcendentals=0),
    )(*operands, *after)


def pages_kernel(
    dp_count, page_hbm, dest_hbm, pool_ref, after_ref, low_ref, high_ref, copy_ref, page_ref, dest_ref, sems
):
    own, width = pool_ref.shape
    pool_copy = pltpu.make_async_copy(pool_ref, copy_ref, sems.at[0])
    page_copy = pltpu.make_async_copy(page_hbm, page_ref, sems.at[1])
    dest_copy = pltpu.make_async_copy(dest_hbm, dest_ref, sems.at[2])
    page_copy.start()
    dest_copy.start()
    pool_copy.start()
    page_copy.wait()
    dest_copy.wait()
    me = lax.axis_index("dp")
    slots = dp_count * MCAP
    row = lax.broadcasted_iota(jnp.int32, (slots, own), 0)
    column = lax.broadcasted_iota(jnp.int32, (slots, own), 1)
    pick = jnp.zeros((slots, own), f32)
    entries = page_ref.shape[1]
    for m in range(entries):
        rank = jnp.int32(0)
        for n in range(m):
            rank += jnp.where(dest_ref[0, n] == dest_ref[0, m], 1, 0)
        bucket = jnp.bitwise_xor(dest_ref[0, m], me) * MCAP + rank
        pick = jnp.where((row == bucket) & (column == page_ref[0, m]), 1.0, pick)
    pick = pick.astype(bf16)
    step = 2048
    pool_copy.wait()
    for i in range(width // step):
        columns = slice(i * step, (i + 1) * step)
        out = jnp.dot(pick, copy_ref[:, columns], preferred_element_type=f32)
        low_ref[:, columns] = out[: slots // 2].astype(bf16)
        high_ref[:, columns] = out[slots // 2 :].astype(bf16)


def pick_pages(moved_page, moved_dest, latent_pool, after, dp_count):
    width = latent_pool.shape[1]
    half = pltpu.VMEM((dp_count * MCAP // 2, width), bf16)
    return pl.pallas_call(
        functools.partial(pages_kernel, dp_count),
        out_shape=(half, half, pltpu.VMEM(latent_pool.shape, bf16)),
        in_specs=[in_hbm()] * 3 + [anywhere()],
        out_specs=(in_vmem(),) * 3,
        scratch_shapes=[
            pltpu.SMEM(moved_page.shape, jnp.int32),
            pltpu.SMEM(moved_dest.shape, jnp.int32),
            pltpu.SemaphoreType.DMA((3,)),
        ],
        compiler_params=pltpu.CompilerParams(vmem_limit_bytes=4 * MIB),
        cost_estimate=pl.CostEstimate(flops=0, bytes_accessed=4 * latent_pool.size, transcendentals=0),
    )(hbm(moved_page), hbm(moved_dest), hbm(latent_pool), after)


def rows_kernel(places, *refs):
    out_ref = refs[-1]
    width = out_ref.shape[1]
    step = 2048
    for i in range(width // step):
        columns = slice(i * step, (i + 1) * step)
        pieces = [ref[:, columns].astype(f32)[low:high] for ref, (low, high) in zip(refs, places)]
        out_ref[:, columns] = jnp.concatenate(pieces, axis=0).astype(bf16)


def rows_of(pieces, *after):
    rows = sum(high - low for _, low, high in pieces)
    width = pieces[0][0].shape[1]
    return pl.pallas_call(
        functools.partial(rows_kernel, [(low, high) for _, low, high in pieces]),
        out_shape=pltpu.VMEM((rows, width), bf16),
        in_specs=[in_vmem()] * len(pieces) + [anywhere()] * len(after),
        out_specs=in_vmem(),
        compiler_params=pltpu.CompilerParams(vmem_limit_bytes=4 * MIB),
        cost_estimate=pl.CostEstimate(flops=0, bytes_accessed=4 * rows * width, transcendentals=0),
    )(*[vmem(x) for x, _, _ in pieces], *after)


def exchange_pages(low, first, dp_count, after):
    blocks, senders = [(low, 0, low.shape[0])], [0]
    got = first
    moves = []
    for number, bit in enumerate(partner_bits(dp_count)):
        if number:
            got = swap(sent, "dp", pairs_of(dp_count, bit))
            moves.append((sent, got))
        size = got.shape[0] // len(blocks)
        blocks = blocks + [(got, i * size, (i + 1) * size) for i in range(len(blocks))]
        senders = senders + [s ^ bit for s in senders]
        if size > MCAP:
            sent = rows_of([(x, start + size // 2, end) for x, start, end in blocks], after)
            blocks = [(x, start, start + size // 2) for x, start, _ in blocks]
    return rows_of(blocks), senders, moves


def attend_kernel(senders, length_ref, table_ref, query_ref, pool_ref, arrived_ref, out_ref, query_rows):
    rows_dev = query_ref.shape[0]
    own, width = pool_ref.shape
    arrived = arrived_ref.shape[0]
    slots = -(-(own + arrived) // 16) * 16
    pair_width = 2 * LAT
    pairs = width // pair_width
    me = lax.axis_index("dp")

    for h in range(HEADS // 2):
        query_rows[h * rows_dev : (h + 1) * rows_dev, :] = query_ref[:, h * pair_width : (h + 1) * pair_width].astype(f32)
    straight = query_rows[...]
    turned = pltpu.roll(straight, LAT, 1)
    first = lax.broadcasted_iota(jnp.int32, straight.shape, 1) < LAT
    query_all = jnp.concatenate(
        [
            jnp.where(first, straight, 0.0),
            jnp.where(first, turned, 0.0),
            jnp.where(first, 0.0, turned),
            jnp.where(first, 0.0, straight),
        ],
        axis=0,
    ).astype(bf16)

    pieces = []
    for j in range(pairs):
        columns = slice(j * pair_width, (j + 1) * pair_width)
        parts = [pool_ref[:, columns].astype(f32), arrived_ref[:, columns].astype(f32)]
        if slots > own + arrived:
            parts.append(jnp.zeros((slots - own - arrived, pair_width), f32))
        pieces.append(jnp.concatenate(parts, axis=0).astype(bf16))
    keys = jnp.concatenate(pieces, axis=0)

    scores = lax.dot_general(query_all, keys, (((1,), (1,)), ((), ())), preferred_element_type=f32) * score_scale

    column = lax.broadcasted_iota(jnp.int32, (1, pairs * slots), 1)
    pair = column // slots
    place = column - pair * slots
    slot = place
    for i, s in enumerate(senders):
        source = jnp.bitwise_xor(me, s)
        for k in range(MCAP):
            slot = jnp.where(place == own + i * MCAP + k, own + source * MCAP + k, slot)
    limits = []
    for r in range(rows_dev):
        limit = jnp.full(column.shape, -1, jnp.int32)
        for p in range(table_ref.shape[1]):
            limit = jnp.where(slot == table_ref[r, p], length_ref[r] - p * PAGE, limit)
        limit = jnp.where(place < own + arrived, limit, -1)
        limits.append(limit - 2 * pair)
    half = scores.shape[0] // 2
    row = lax.broadcasted_iota(jnp.int32, (half, 1), 0) % rows_dev
    limit = limits[0]
    for r in range(1, rows_dev):
        limit = jnp.where(row == r, limits[r], limit)
    even = jnp.where(limit > 0, scores[:half], -jnp.inf)
    odd = jnp.where(limit > 1, scores[half:], -jnp.inf)
    peak = jnp.maximum(jnp.max(even, axis=1, keepdims=True), jnp.max(odd, axis=1, keepdims=True))
    even = jnp.exp(even - peak)
    odd = jnp.exp(odd - peak)
    total = jnp.sum(even, axis=1, keepdims=True) + jnp.sum(odd, axis=1, keepdims=True)
    even = (even / total).astype(bf16)
    odd = (odd / total).astype(bf16)
    from_even = jnp.dot(even, keys[:, :VL], preferred_element_type=f32)
    from_odd = jnp.dot(odd, keys[:, VL:], preferred_element_type=f32)
    shift = LAT - VL
    wide = pair_width - VL
    attended = from_even + pltpu.roll(from_odd, wide - shift, 1)[:, :VL]
    for h in range(HEADS):
        at = (h % 2) * (half // 2) + (h // 2) * rows_dev
        out_ref[:, h * VL : (h + 1) * VL] = attended[at : at + rows_dev].astype(bf16)


def attend(lengths, page_table, queries, latent_pool, arrived, senders):
    rows_dev = queries.shape[0]
    return pl.pallas_call(
        functools.partial(attend_kernel, senders),
        out_shape=jax.ShapeDtypeStruct((rows_dev, HEADS * VL), bf16),
        in_specs=[in_smem(), in_smem(), in_vmem(), in_vmem(), in_vmem()],
        out_specs=in_vmem(),
        scratch_shapes=[pltpu.VMEM((HEADS // 2 * rows_dev, 2 * LAT), f32)],
        compiler_params=pltpu.CompilerParams(vmem_limit_bytes=16 * MIB),
        cost_estimate=pl.CostEstimate(flops=1 << 30, bytes_accessed=4 << 20, transcendentals=1 << 17),
    )(lengths, page_table, queries, vmem(latent_pool), vmem(arrived))


def body(
    hidden,
    routes,
    route_weight,
    gate_weight,
    up_weight,
    down_weight,
    queries,
    latent_pool,
    lengths,
    page_table,
    moved_page,
    moved_dest,
):
    ep_count = lax.axis_size("ep")
    dp_count = lax.axis_size("dp")
    count = ep_count * dp_count
    stages = stage_partners(count)

    def trade(x, bit):
        return swap(x, AXES, pairs_of(count, bit))

    mine = (hidden, routes, route_weight)
    got = [trade(x, 1) for x in mine]
    near = make_payload(fetch(*mine), got, ep_count)
    for number, partners in enumerate(stages):
        got = [trade(near, bit) for bit in partners]
        after = []
        if number == 0:
            low, high, pool = pick_pages(moved_page, moved_dest, latent_pool, near, dp_count)
            after = [high]
            bit = partner_bits(dp_count)[0]
            first = swap(high, "dp", pairs_of(dp_count, bit))
        if number == len(stages) - 1:
            after = [first]
        near = merge([near] + got, MERGE_FLOPS if number < len(stages) - 1 else MERGE_FLOPS // 4, *after)
    far = trade(near, 1)
    arrived, senders, moves = exchange_pages(low, first, dp_count, near)
    gate_acc, up_acc = near_products(near, gate_weight, up_weight, down_weight, *[sent for sent, _ in moves])
    inner, keep_a, send_a = far_products(
        near, far, gate_weight, up_weight, gate_acc, up_acc, down_weight, ep_count, *[got for _, got in moves]
    )
    got_a = trade(send_a, 1)
    keep_b, send_b = rest_products(near, inner, down_weight, ep_count)
    got_b = trade(send_b, 1)
    (sum_a,) = fold([(keep_a, [got_a])], 1, out=pltpu.VMEM(keep_a.shape, f32), flops=MERGE_FLOPS // 4)
    held = [(sum_a, []), (keep_b, [got_b])]
    after = []
    for number, partners in enumerate(reversed(stages)):
        keep, *send = fold(held, len(partners) + 1, *(after if number == 1 else []))
        held = [(keep, [trade(x, bit) for x, bit in zip(send, partners)])]
        if number == 0:
            attended = attend(lengths, page_table, queries, pool, arrived, senders)
            after = [hbm(attended)]
    (expert_mix,) = fold(held, 1, out=jax.ShapeDtypeStruct(hidden.shape, bf16))
    return expert_mix, attended


def solution(mesh):
    rows = P(("inst", "ep", "dp"), None)
    in_specs = (
        rows,
        rows,
        rows,
        P("ep", None, "dp"),
        P("ep", None, "dp"),
        P("ep", "dp", None),
        rows,
        rows,
        P(("inst", "ep", "dp")),
        rows,
        rows,
        rows,
    )
    return jax.shard_map(body, mesh=mesh, in_specs=in_specs, out_specs=(rows, rows), check_vma=False)
```

```python
import functools

import jax
import jax.numpy as jnp
from jax import lax
from jax.experimental import pallas as pl
from jax.experimental.pallas import tpu as pltpu
from jax.sharding import PartitionSpec as P

HEADS = 64
LAT = 576
VL = 512
MCAP = 2
PAGE = 32
LANES = 128
AXES = ("ep", "dp")
MIB = 1 << 20
MERGE_FLOPS = 20_000_000_000

score_scale = 192.0 ** (-0.5)
bf16 = jnp.bfloat16
f32 = jnp.float32


def in_vmem():
    return pl.BlockSpec(memory_space=pltpu.VMEM)


def in_smem():
    return pl.BlockSpec(memory_space=pltpu.SMEM)


def vmem(x):
    return pltpu.with_memory_space_constraint(x, pltpu.VMEM)


def hbm(x):
    return pltpu.with_memory_space_constraint(x, pltpu.HBM)


def anywhere():
    return pl.BlockSpec(memory_space=pl.ANY)


def in_hbm():
    return pl.BlockSpec(memory_space=pltpu.HBM)


def partner_bits(count):
    bits = []
    b = count // 2
    while b:
        bits.append(b)
        b //= 2
    return bits


def swap(x, axes, pairs):
    return lax.ppermute(x, axes, pairs)


def stage_partners(count):
    bits = partner_bits(count)[:-1]
    stages = [(bits[0],)] if len(bits) % 2 else []
    bits = bits[len(bits) % 2 :]
    for high, low in zip(bits[::2], bits[1::2]):
        stages.append((high, high ^ low, low))
    high, far, low = stages[-1]
    return stages[:-1] + [(far, high, low)]


def pairs_of(count, bit):
    return [(i, i ^ bit) for i in range(count)]


def fetch_kernel(*refs):
    count = (len(refs) - 1) // 2
    copies = [pltpu.make_async_copy(refs[i], refs[count + i], refs[-1].at[i]) for i in range(count)]
    for c in copies:
        c.start()
    for c in copies:
        c.wait()


def fetch(*arrays):
    return pl.pallas_call(
        fetch_kernel,
        out_shape=tuple(pltpu.VMEM(x.shape, x.dtype) for x in arrays),
        in_specs=[in_hbm()] * len(arrays),
        out_specs=(in_vmem(),) * len(arrays),
        scratch_shapes=[pltpu.SemaphoreType.DMA((len(arrays),))],
        compiler_params=pltpu.CompilerParams(vmem_limit_bytes=4 * MIB),
        cost_estimate=pl.CostEstimate(flops=MERGE_FLOPS // 16, bytes_accessed=MIB, transcendentals=0),
    )(*[hbm(x) for x in arrays])


def payload_kernel(ep_count, mine_hidden, mine_routes, mine_weight, got_hidden, got_routes, got_weight, out_ref):
    first = lax.rem(lax.axis_index("dp"), 2) == 0
    rows, width = mine_hidden.shape
    half = width // 2

    def in_order(mine, got):
        return jnp.where(first, jnp.concatenate([mine, got], axis=0), jnp.concatenate([got, mine], axis=0))

    def my_half(ref):
        return jnp.where(first, ref[:, :half].astype(f32), ref[:, half:].astype(f32))

    out_ref[:, :half] = in_order(my_half(mine_hidden), my_half(got_hidden)).astype(bf16)
    routes = in_order(mine_routes[...], got_routes[...])
    weight = in_order(mine_weight[...], got_weight[...])
    column = lax.broadcasted_iota(jnp.int32, (2 * rows, LANES), 1)
    expert = jnp.where(column < ep_count, column, column - ep_count)
    total = jnp.zeros((2 * rows, LANES), f32)
    for k in range(routes.shape[1]):
        total += jnp.where(routes[:, k : k + 1] == expert, weight[:, k : k + 1], 0.0)
    high = total.astype(bf16).astype(f32)
    low = total - high
    out_ref[:, half:] = jnp.where(column < ep_count, high, jnp.where(column < 2 * ep_count, low, 0.0)).astype(bf16)


def make_payload(mine, got, ep_count):
    rows, width = mine[0].shape
    return pl.pallas_call(
        functools.partial(payload_kernel, ep_count),
        out_shape=pltpu.VMEM((2 * rows, width // 2 + LANES), bf16),
        in_specs=[in_vmem()] * 6,
        out_specs=in_vmem(),
        compiler_params=pltpu.CompilerParams(vmem_limit_bytes=4 * MIB),
        cost_estimate=pl.CostEstimate(flops=0, bytes_accessed=4 * rows * width, transcendentals=0),
    )(*[vmem(x) for x in mine], *[vmem(x) for x in got])


def merge_kernel(parts, *refs):
    out_ref = refs[-1]
    half = refs[0].shape[0] // 2
    pieces = [r[...].astype(f32) for r in [refs[0], *refs[1:parts][::-1]]]
    cores = [p[:half] for p in pieces] + [p[half:] for p in pieces]
    out_ref[...] = jnp.concatenate(cores, axis=0).astype(bf16)


def merge(pieces, flops, *after):
    rows, width = pieces[0].shape
    return pl.pallas_call(
        functools.partial(merge_kernel, len(pieces)),
        out_shape=pltpu.VMEM((len(pieces) * rows, width), bf16),
        in_specs=[in_vmem()] * len(pieces) + [anywhere()] * len(after),
        out_specs=in_vmem(),
        compiler_params=pltpu.CompilerParams(vmem_limit_bytes=4 * MIB),
        cost_estimate=pl.CostEstimate(flops=flops, bytes_accessed=8 * rows * width, transcendentals=0),
    )(*[vmem(p) for p in pieces[:1] + pieces[:0:-1]], *after)


def half_start(width, near):
    core = lax.rem(lax.axis_index("dp"), 2)
    core = core if near else 1 - core
    return pl.multiple_of(core * (width // 2), width // 2)


def padded(x):
    rows = x.shape[0]
    return x if rows >= 128 else jnp.concatenate([x] * (128 // rows), axis=0)


def near_kernel(near_ref, gate_ref, up_ref, *refs):
    gate_out, up_out = refs[-2:]
    rows, width = near_ref.shape[0], gate_ref.shape[1]
    at = pl.ds(half_start(width, True), width // 2)
    x = padded(near_ref[:, : width // 2])
    gate_out[...] = jnp.dot(x, gate_ref[0, at, :], preferred_element_type=f32)[:rows]
    up_out[...] = jnp.dot(x, up_ref[0, at, :], preferred_element_type=f32)[:rows]


def row_weights(near_ref, half, ep_count):
    ep = lax.axis_index("ep")
    table = near_ref[:, half:].astype(f32)
    column = lax.broadcasted_iota(jnp.int32, table.shape, 1)
    mine = (column == ep) | (column == ep + ep_count)
    return jnp.sum(jnp.where(mine, table, 0.0), axis=1, keepdims=True)


STEPS = 7


def down_half(inner, row_weight, down_ref, start, keep_ref, send_ref):
    first = lax.rem(lax.axis_index("dp"), 2) == 0
    rows, half = keep_ref.shape
    step = half // STEPS
    x = padded(inner)
    for i in range(STEPS):
        columns = slice(i * step, (i + 1) * step)
        out = jnp.dot(x, down_ref[0, :, start + i * step : start + (i + 1) * step], preferred_element_type=f32)
        out = out[: 2 * rows] * row_weight
        keep_ref[:, columns] = jnp.where(first, out[:rows], out[rows:])
        send_ref[:, columns] = jnp.where(first, out[rows:], out[:rows]).astype(bf16)


def far_kernel(ep_count, near_ref, far_ref, gate_ref, up_ref, gate_in, up_in, down_ref, *refs):
    inner_ref, keep_ref, send_ref = refs[-3:]
    rows, width = near_ref.shape[0], gate_ref.shape[1]
    half = width // 2
    at = pl.ds(half_start(width, False), half)
    row_weight = row_weights(near_ref, half, ep_count)
    x = padded(far_ref[:, :half])
    gate = gate_in[...] + jnp.dot(x, gate_ref[0, at, :], preferred_element_type=f32)[:rows]
    up = up_in[...] + jnp.dot(x, up_ref[0, at, :], preferred_element_type=f32)[:rows]
    inner = (gate / (1.0 + jnp.exp(-gate)) * up).astype(bf16)
    inner_ref[...] = inner
    down_half(inner, row_weight, down_ref, 0, keep_ref, send_ref)


def rest_kernel(ep_count, near_ref, inner_ref, down_ref, keep_ref, send_ref):
    half = keep_ref.shape[1]
    down_half(inner_ref[...], row_weights(near_ref, half, ep_count), down_ref, half, keep_ref, send_ref)


def estimate(rows, weights):
    return pl.CostEstimate(flops=2 * rows * weights, bytes_accessed=2 * weights, transcendentals=0)


def near_products(near, gate, up, down, *after):
    rows = near.shape[0]
    width, units = gate.shape[1:]
    acc = pltpu.VMEM((rows, units), f32)
    return pl.pallas_call(
        near_kernel,
        out_shape=(acc, acc),
        in_specs=[in_vmem()] * 4 + [anywhere()] * len(after),
        out_specs=(in_vmem(),) * 2,
        compiler_params=pltpu.CompilerParams(vmem_limit_bytes=8 * MIB),
        cost_estimate=estimate(rows, width * units),
    )(vmem(near), gate, up, down, *after)


def far_products(near, far, gate, up, gate_acc, up_acc, down, ep_count, *after):
    rows = near.shape[0]
    units, width = down.shape[1:]
    half = width // 2
    return pl.pallas_call(
        functools.partial(far_kernel, ep_count),
        out_shape=(
            pltpu.VMEM((rows, units), bf16),
            pltpu.VMEM((rows // 2, half), f32),
            pltpu.VMEM((rows // 2, half), bf16),
        ),
        in_specs=[in_vmem()] * 7 + [anywhere()] * len(after),
        out_specs=(in_vmem(),) * 3,
        compiler_params=pltpu.CompilerParams(vmem_limit_bytes=8 * MIB),
        cost_estimate=estimate(rows, 3 * half * units),
    )(vmem(near), vmem(far), gate, up, vmem(gate_acc), vmem(up_acc), down, *after)


def rest_products(near, inner, down, ep_count):
    rows = near.shape[0]
    units, width = down.shape[1:]
    half = width // 2
    return pl.pallas_call(
        functools.partial(rest_kernel, ep_count),
        out_shape=(pltpu.VMEM((rows // 2, half), f32), pltpu.VMEM((rows // 2, half), bf16)),
        in_specs=[in_vmem()] * 3,
        out_specs=(in_vmem(),) * 2,
        compiler_params=pltpu.CompilerParams(vmem_limit_bytes=8 * MIB),
        cost_estimate=estimate(rows, half * units),
    )(vmem(near), vmem(inner), down)


def fold_kernel(arrived, parts, *refs):
    outs = refs[-parts:]
    rows = outs[0].shape[0]
    start = at = 0
    for number in arrived:
        ours = refs[at : at + 1 + number]
        at += 1 + number
        total = ours[0][...]
        for g in ours[1:]:
            total += g[...].astype(f32)
        columns = slice(start, start + total.shape[1])
        start += total.shape[1]
        for i, out in enumerate(outs):
            out[:, columns] = total[i * rows : (i + 1) * rows].astype(out.dtype)


def fold(held, parts, *after, out=None, flops=0):
    rows = held[0][0].shape[0]
    width = sum(keep.shape[1] for keep, _ in held)
    part = (rows // parts, width)
    operands = [vmem(x) for keep, gots in held for x in [keep] + gots]
    shapes = (pltpu.VMEM(part, f32),) + (pltpu.VMEM(part, bf16),) * (parts - 1)
    return pl.pallas_call(
        functools.partial(fold_kernel, [len(gots) for _, gots in held], parts),
        out_shape=shapes if out is None else (out,),
        in_specs=[in_vmem()] * len(operands) + [anywhere()] * len(after),
        out_specs=(in_vmem(),) * parts,
        compiler_params=pltpu.CompilerParams(vmem_limit_bytes=4 * MIB),
        cost_estimate=pl.CostEstimate(flops=flops, bytes_accessed=8 * rows * width, transcendentals=0),
    )(*operands, *after)


def pages_kernel(
    dp_count, page_hbm, dest_hbm, pool_ref, after_ref, low_ref, high_ref, page_ref, dest_ref, sems
):
    own, width = pool_ref.shape
    page_copy = pltpu.make_async_copy(page_hbm, page_ref, sems.at[0])
    dest_copy = pltpu.make_async_copy(dest_hbm, dest_ref, sems.at[1])
    page_copy.start()
    dest_copy.start()
    page_copy.wait()
    dest_copy.wait()
    me = lax.axis_index("dp")
    slots = dp_count * MCAP
    row = lax.broadcasted_iota(jnp.int32, (slots, own), 0)
    column = lax.broadcasted_iota(jnp.int32, (slots, own), 1)
    pick = jnp.zeros((slots, own), f32)
    entries = page_ref.shape[1]
    for m in range(entries):
        rank = jnp.int32(0)
        for n in range(m):
            rank += jnp.where(dest_ref[0, n] == dest_ref[0, m], 1, 0)
        bucket = jnp.bitwise_xor(dest_ref[0, m], me) * MCAP + rank
        pick = jnp.where((row == bucket) & (column == page_ref[0, m]), 1.0, pick)
    pick = pick.astype(bf16)
    step = 2048
    for i in range(width // step):
        columns = slice(i * step, (i + 1) * step)
        out = jnp.dot(pick, pool_ref[:, columns], preferred_element_type=f32)
        low_ref[:, columns] = out[: slots // 2].astype(bf16)
        high_ref[:, columns] = out[slots // 2 :].astype(bf16)


def pick_pages(moved_page, moved_dest, latent_pool, after, dp_count):
    width = latent_pool.shape[1]
    half = pltpu.VMEM((dp_count * MCAP // 2, width), bf16)
    return pl.pallas_call(
        functools.partial(pages_kernel, dp_count),
        out_shape=(half, half),
        in_specs=[in_hbm()] * 2 + [in_vmem(), anywhere()],
        out_specs=(in_vmem(),) * 2,
        scratch_shapes=[
            pltpu.SMEM(moved_page.shape, jnp.int32),
            pltpu.SMEM(moved_dest.shape, jnp.int32),
            pltpu.SemaphoreType.DMA((2,)),
        ],
        compiler_params=pltpu.CompilerParams(vmem_limit_bytes=4 * MIB),
        cost_estimate=pl.CostEstimate(flops=0, bytes_accessed=4 * latent_pool.size, transcendentals=0),
    )(hbm(moved_page), hbm(moved_dest), vmem(latent_pool), after)


def rows_kernel(places, *refs):
    out_ref = refs[-1]
    width = out_ref.shape[1]
    step = 2048
    for i in range(width // step):
        columns = slice(i * step, (i + 1) * step)
        pieces = [ref[:, columns].astype(f32)[low:high] for ref, (low, high) in zip(refs, places)]
        out_ref[:, columns] = jnp.concatenate(pieces, axis=0).astype(bf16)


def rows_of(pieces, *after):
    rows = sum(high - low for _, low, high in pieces)
    width = pieces[0][0].shape[1]
    return pl.pallas_call(
        functools.partial(rows_kernel, [(low, high) for _, low, high in pieces]),
        out_shape=pltpu.VMEM((rows, width), bf16),
        in_specs=[in_vmem()] * len(pieces) + [anywhere()] * len(after),
        out_specs=in_vmem(),
        compiler_params=pltpu.CompilerParams(vmem_limit_bytes=4 * MIB),
        cost_estimate=pl.CostEstimate(flops=0, bytes_accessed=4 * rows * width, transcendentals=0),
    )(*[vmem(x) for x, _, _ in pieces], *after)


def exchange_pages(low, first, dp_count, after):
    blocks, senders = [(low, 0, low.shape[0])], [0]
    got = first
    moves = []
    for number, bit in enumerate(partner_bits(dp_count)):
        if number:
            got = swap(sent, "dp", pairs_of(dp_count, bit))
            moves.append((sent, got))
        size = got.shape[0] // len(blocks)
        blocks = blocks + [(got, i * size, (i + 1) * size) for i in range(len(blocks))]
        senders = senders + [s ^ bit for s in senders]
        if size > MCAP:
            sent = rows_of([(x, start + size // 2, end) for x, start, end in blocks], after)
            blocks = [(x, start, start + size // 2) for x, start, _ in blocks]
    return rows_of(blocks), senders, moves


def attend_kernel(senders, length_ref, table_ref, query_ref, pool_ref, arrived_ref, out_ref, query_rows):
    rows_dev = query_ref.shape[0]
    own, width = pool_ref.shape
    arrived = arrived_ref.shape[0]
    slots = -(-(own + arrived) // 16) * 16
    pair_width = 2 * LAT
    pairs = width // pair_width
    me = lax.axis_index("dp")

    for h in range(HEADS // 2):
        query_rows[h * rows_dev : (h + 1) * rows_dev, :] = query_ref[:, h * pair_width : (h + 1) * pair_width].astype(f32)
    straight = query_rows[...]
    turned = pltpu.roll(straight, LAT, 1)
    first = lax.broadcasted_iota(jnp.int32, straight.shape, 1) < LAT
    query_all = jnp.concatenate(
        [
            jnp.where(first, straight, 0.0),
            jnp.where(first, turned, 0.0),
            jnp.where(first, 0.0, turned),
            jnp.where(first, 0.0, straight),
        ],
        axis=0,
    ).astype(bf16)

    pieces = []
    for j in range(pairs):
        columns = slice(j * pair_width, (j + 1) * pair_width)
        parts = [pool_ref[:, columns].astype(f32), arrived_ref[:, columns].astype(f32)]
        if slots > own + arrived:
            parts.append(jnp.zeros((slots - own - arrived, pair_width), f32))
        pieces.append(jnp.concatenate(parts, axis=0).astype(bf16))
    keys = jnp.concatenate(pieces, axis=0)

    scores = lax.dot_general(query_all, keys, (((1,), (1,)), ((), ())), preferred_element_type=f32) * score_scale

    column = lax.broadcasted_iota(jnp.int32, (1, pairs * slots), 1)
    pair = column // slots
    place = column - pair * slots
    slot = place
    for i, s in enumerate(senders):
        source = jnp.bitwise_xor(me, s)
        for k in range(MCAP):
            slot = jnp.where(place == own + i * MCAP + k, own + source * MCAP + k, slot)
    limits = []
    for r in range(rows_dev):
        limit = jnp.full(column.shape, -1, jnp.int32)
        for p in range(table_ref.shape[1]):
            limit = jnp.where(slot == table_ref[r, p], length_ref[r] - p * PAGE, limit)
        limit = jnp.where(place < own + arrived, limit, -1)
        limits.append(limit - 2 * pair)
    half = scores.shape[0] // 2
    row = lax.broadcasted_iota(jnp.int32, (half, 1), 0) % rows_dev
    limit = limits[0]
    for r in range(1, rows_dev):
        limit = jnp.where(row == r, limits[r], limit)
    even = jnp.where(limit > 0, scores[:half], -jnp.inf)
    odd = jnp.where(limit > 1, scores[half:], -jnp.inf)
    peak = jnp.maximum(jnp.max(even, axis=1, keepdims=True), jnp.max(odd, axis=1, keepdims=True))
    even = jnp.exp(even - peak)
    odd = jnp.exp(odd - peak)
    total = jnp.sum(even, axis=1, keepdims=True) + jnp.sum(odd, axis=1, keepdims=True)
    even = (even / total).astype(bf16)
    odd = (odd / total).astype(bf16)
    from_even = jnp.dot(even, keys[:, :VL], preferred_element_type=f32)
    from_odd = jnp.dot(odd, keys[:, VL:], preferred_element_type=f32)
    shift = LAT - VL
    wide = pair_width - VL
    attended = from_even + pltpu.roll(from_odd, wide - shift, 1)[:, :VL]
    for h in range(HEADS):
        at = (h % 2) * (half // 2) + (h // 2) * rows_dev
        out_ref[:, h * VL : (h + 1) * VL] = attended[at : at + rows_dev].astype(bf16)


def attend(lengths, page_table, queries, latent_pool, arrived, senders):
    rows_dev = queries.shape[0]
    return pl.pallas_call(
        functools.partial(attend_kernel, senders),
        out_shape=jax.ShapeDtypeStruct((rows_dev, HEADS * VL), bf16),
        in_specs=[in_smem(), in_smem(), in_vmem(), in_vmem(), in_vmem()],
        out_specs=in_vmem(),
        scratch_shapes=[pltpu.VMEM((HEADS // 2 * rows_dev, 2 * LAT), f32)],
        compiler_params=pltpu.CompilerParams(vmem_limit_bytes=16 * MIB),
        cost_estimate=pl.CostEstimate(flops=1 << 30, bytes_accessed=4 << 20, transcendentals=1 << 17),
    )(lengths, page_table, queries, vmem(latent_pool), vmem(arrived))


def body(
    hidden,
    routes,
    route_weight,
    gate_weight,
    up_weight,
    down_weight,
    queries,
    latent_pool,
    lengths,
    page_table,
    moved_page,
    moved_dest,
):
    ep_count = lax.axis_size("ep")
    dp_count = lax.axis_size("dp")
    count = ep_count * dp_count
    stages = stage_partners(count)

    def trade(x, bit):
        return swap(x, AXES, pairs_of(count, bit))

    mine = (hidden, routes, route_weight)
    got = [trade(x, 1) for x in mine]
    *mine, pool = fetch(*mine, latent_pool)
    near = make_payload(mine, got, ep_count)
    for number, partners in enumerate(stages):
        got = [trade(near, bit) for bit in partners]
        after = []
        if number == 0:
            low, high = pick_pages(moved_page, moved_dest, pool, near, dp_count)
            after = [high]
            bit = partner_bits(dp_count)[0]
            first = swap(high, "dp", pairs_of(dp_count, bit))
        if number == len(stages) - 1:
            after = [first]
        near = merge([near] + got, MERGE_FLOPS if number < len(stages) - 1 else MERGE_FLOPS // 4, *after)
    far = trade(near, 1)
    arrived, senders, moves = exchange_pages(low, first, dp_count, near)
    gate_acc, up_acc = near_products(near, gate_weight, up_weight, down_weight, *[sent for sent, _ in moves])
    inner, keep_a, send_a = far_products(
        near, far, gate_weight, up_weight, gate_acc, up_acc, down_weight, ep_count, *[got for _, got in moves]
    )
    got_a = trade(send_a, 1)
    keep_b, send_b = rest_products(near, inner, down_weight, ep_count)
    got_b = trade(send_b, 1)
    (sum_a,) = fold([(keep_a, [got_a])], 1, out=pltpu.VMEM(keep_a.shape, f32), flops=MERGE_FLOPS // 4)
    held = [(sum_a, []), (keep_b, [got_b])]
    after = []
    for number, partners in enumerate(reversed(stages)):
        keep, *send = fold(held, len(partners) + 1, *(after if number == 1 else []))
        held = [(keep, [trade(x, bit) for x, bit in zip(send, partners)])]
        if number == 0:
            attended = attend(lengths, page_table, queries, pool, arrived, senders)
            after = [hbm(attended)]
    (expert_mix,) = fold(held, 1, out=jax.ShapeDtypeStruct(hidden.shape, bf16))
    return expert_mix, attended


def solution(mesh):
    rows = P(("inst", "ep", "dp"), None)
    in_specs = (
        rows,
        rows,
        rows,
        P("ep", None, "dp"),
        P("ep", None, "dp"),
        P("ep", "dp", None),
        rows,
        rows,
        P(("inst", "ep", "dp")),
        rows,
        rows,
        rows,
    )
    return jax.shard_map(body, mesh=mesh, in_specs=in_specs, out_specs=(rows, rows), check_vma=False)
```

```python
import functools

import jax
import jax.numpy as jnp
from jax import lax
from jax.experimental import pallas as pl
from jax.experimental.pallas import tpu as pltpu
from jax.sharding import PartitionSpec as P

HEADS = 64
LAT = 576
VL = 512
MCAP = 2
PAGE = 32
LANES = 128
AXES = ("ep", "dp")
MIB = 1 << 20
MERGE_FLOPS = 20_000_000_000

score_scale = 192.0 ** (-0.5)
bf16 = jnp.bfloat16
f32 = jnp.float32


def in_vmem():
    return pl.BlockSpec(memory_space=pltpu.VMEM)


def in_smem():
    return pl.BlockSpec(memory_space=pltpu.SMEM)


def vmem(x):
    return pltpu.with_memory_space_constraint(x, pltpu.VMEM)


def hbm(x):
    return pltpu.with_memory_space_constraint(x, pltpu.HBM)


def anywhere():
    return pl.BlockSpec(memory_space=pl.ANY)


def in_hbm():
    return pl.BlockSpec(memory_space=pltpu.HBM)


def partner_bits(count):
    bits = []
    b = count // 2
    while b:
        bits.append(b)
        b //= 2
    return bits


def swap(x, axes, pairs):
    return lax.ppermute(x, axes, pairs)


def stage_partners(count):
    bits = partner_bits(count)[:-1]
    stages = [(bits[0],)] if len(bits) % 2 else []
    bits = bits[len(bits) % 2 :]
    for high, low in zip(bits[::2], bits[1::2]):
        stages.append((high, high ^ low, low))
    high, far, low = stages[-1]
    return stages[:-1] + [(far, high, low)]


def pairs_of(count, bit):
    return [(i, i ^ bit) for i in range(count)]


def fetch_kernel(*refs):
    count = (len(refs) - 1) // 2
    copies = [pltpu.make_async_copy(refs[i], refs[count + i], refs[-1].at[i]) for i in range(count)]
    for c in copies:
        c.start()
    for c in copies:
        c.wait()


def fetch(*arrays):
    return pl.pallas_call(
        fetch_kernel,
        out_shape=tuple(pltpu.VMEM(x.shape, x.dtype) for x in arrays),
        in_specs=[in_hbm()] * len(arrays),
        out_specs=(in_vmem(),) * len(arrays),
        scratch_shapes=[pltpu.SemaphoreType.DMA((len(arrays),))],
        compiler_params=pltpu.CompilerParams(vmem_limit_bytes=4 * MIB),
        cost_estimate=pl.CostEstimate(flops=MERGE_FLOPS // 16, bytes_accessed=MIB, transcendentals=0),
    )(*[hbm(x) for x in arrays])


def payload_kernel(ep_count, mine_hidden, mine_routes, mine_weight, got_hidden, got_routes, got_weight, out_ref):
    first = lax.rem(lax.axis_index("dp"), 2) == 0
    rows, width = mine_hidden.shape
    half = width // 2

    def in_order(mine, got):
        return jnp.where(first, jnp.concatenate([mine, got], axis=0), jnp.concatenate([got, mine], axis=0))

    def my_half(ref):
        return jnp.where(first, ref[:, :half].astype(f32), ref[:, half:].astype(f32))

    out_ref[:, :half] = in_order(my_half(mine_hidden), my_half(got_hidden)).astype(bf16)
    routes = in_order(mine_routes[...], got_routes[...])
    weight = in_order(mine_weight[...], got_weight[...])
    column = lax.broadcasted_iota(jnp.int32, (2 * rows, LANES), 1)
    expert = jnp.where(column < ep_count, column, column - ep_count)
    total = jnp.zeros((2 * rows, LANES), f32)
    for k in range(routes.shape[1]):
        total += jnp.where(routes[:, k : k + 1] == expert, weight[:, k : k + 1], 0.0)
    high = total.astype(bf16).astype(f32)
    low = total - high
    out_ref[:, half:] = jnp.where(column < ep_count, high, jnp.where(column < 2 * ep_count, low, 0.0)).astype(bf16)


def make_payload(mine, got, ep_count):
    rows, width = mine[0].shape
    return pl.pallas_call(
        functools.partial(payload_kernel, ep_count),
        out_shape=pltpu.VMEM((2 * rows, width // 2 + LANES), bf16),
        in_specs=[in_vmem()] * 6,
        out_specs=in_vmem(),
        compiler_params=pltpu.CompilerParams(vmem_limit_bytes=4 * MIB),
        cost_estimate=pl.CostEstimate(flops=0, bytes_accessed=4 * rows * width, transcendentals=0),
    )(*[vmem(x) for x in mine], *[vmem(x) for x in got])


def merge_kernel(parts, *refs):
    out_ref = refs[-1]
    half = refs[0].shape[0] // 2
    pieces = [r[...].astype(f32) for r in [refs[0], *refs[1:parts][::-1]]]
    cores = [p[:half] for p in pieces] + [p[half:] for p in pieces]
    out_ref[...] = jnp.concatenate(cores, axis=0).astype(bf16)


def merge(pieces, flops, *after):
    rows, width = pieces[0].shape
    return pl.pallas_call(
        functools.partial(merge_kernel, len(pieces)),
        out_shape=pltpu.VMEM((len(pieces) * rows, width), bf16),
        in_specs=[in_vmem()] * len(pieces) + [anywhere()] * len(after),
        out_specs=in_vmem(),
        compiler_params=pltpu.CompilerParams(vmem_limit_bytes=4 * MIB),
        cost_estimate=pl.CostEstimate(flops=flops, bytes_accessed=8 * rows * width, transcendentals=0),
    )(*[vmem(p) for p in pieces[:1] + pieces[:0:-1]], *after)


def half_start(width, near):
    core = lax.rem(lax.axis_index("dp"), 2)
    core = core if near else 1 - core
    return pl.multiple_of(core * (width // 2), width // 2)


def padded(x):
    rows = x.shape[0]
    return x if rows >= 128 else jnp.concatenate([x] * (128 // rows), axis=0)


def near_kernel(near_ref, gate_ref, up_ref, *refs):
    gate_out, up_out = refs[-2:]
    rows, width = near_ref.shape[0], gate_ref.shape[1]
    at = pl.ds(half_start(width, True), width // 2)
    x = padded(near_ref[:, : width // 2])
    gate_out[...] = jnp.dot(x, gate_ref[0, at, :], preferred_element_type=f32)[:rows]
    up_out[...] = jnp.dot(x, up_ref[0, at, :], preferred_element_type=f32)[:rows]


def row_weights(near_ref, half, ep_count):
    ep = lax.axis_index("ep")
    table = near_ref[:, half:].astype(f32)
    column = lax.broadcasted_iota(jnp.int32, table.shape, 1)
    mine = (column == ep) | (column == ep + ep_count)
    return jnp.sum(jnp.where(mine, table, 0.0), axis=1, keepdims=True)


STEPS = 7


def down_half(inner, row_weight, down_ref, start, keep_ref, send_ref):
    first = lax.rem(lax.axis_index("dp"), 2) == 0
    rows, half = keep_ref.shape
    step = half // STEPS
    x = padded(inner)
    for i in range(STEPS):
        columns = slice(i * step, (i + 1) * step)
        out = jnp.dot(x, down_ref[0, :, start + i * step : start + (i + 1) * step], preferred_element_type=f32)
        out = out[: 2 * rows] * row_weight
        keep_ref[:, columns] = jnp.where(first, out[:rows], out[rows:])
        send_ref[:, columns] = jnp.where(first, out[rows:], out[:rows]).astype(bf16)


def far_kernel(ep_count, near_ref, far_ref, gate_ref, up_ref, gate_in, up_in, down_ref, *refs):
    inner_ref, keep_ref, send_ref = refs[-3:]
    rows, width = near_ref.shape[0], gate_ref.shape[1]
    half = width // 2
    at = pl.ds(half_start(width, False), half)
    row_weight = row_weights(near_ref, half, ep_count)
    x = padded(far_ref[:, :half])
    gate = gate_in[...] + jnp.dot(x, gate_ref[0, at, :], preferred_element_type=f32)[:rows]
    up = up_in[...] + jnp.dot(x, up_ref[0, at, :], preferred_element_type=f32)[:rows]
    inner = (gate / (1.0 + jnp.exp(-gate)) * up).astype(bf16)
    inner_ref[...] = inner
    down_half(inner, row_weight, down_ref, 0, keep_ref, send_ref)


def rest_kernel(ep_count, near_ref, inner_ref, down_ref, keep_ref, send_ref):
    half = keep_ref.shape[1]
    down_half(inner_ref[...], row_weights(near_ref, half, ep_count), down_ref, half, keep_ref, send_ref)


def estimate(rows, weights):
    return pl.CostEstimate(flops=2 * rows * weights, bytes_accessed=2 * weights, transcendentals=0)


def near_products(near, gate, up, down, *after):
    rows = near.shape[0]
    width, units = gate.shape[1:]
    acc = pltpu.VMEM((rows, units), f32)
    return pl.pallas_call(
        near_kernel,
        out_shape=(acc, acc),
        in_specs=[in_vmem()] * 4 + [anywhere()] * len(after),
        out_specs=(in_vmem(),) * 2,
        compiler_params=pltpu.CompilerParams(vmem_limit_bytes=8 * MIB),
        cost_estimate=estimate(rows, width * units),
    )(vmem(near), gate, up, down, *after)


def far_products(near, far, gate, up, gate_acc, up_acc, down, ep_count, *after):
    rows = near.shape[0]
    units, width = down.shape[1:]
    half = width // 2
    return pl.pallas_call(
        functools.partial(far_kernel, ep_count),
        out_shape=(
            pltpu.VMEM((rows, units), bf16),
            pltpu.VMEM((rows // 2, half), f32),
            pltpu.VMEM((rows // 2, half), bf16),
        ),
        in_specs=[in_vmem()] * 7 + [anywhere()] * len(after),
        out_specs=(in_vmem(),) * 3,
        compiler_params=pltpu.CompilerParams(vmem_limit_bytes=8 * MIB),
        cost_estimate=estimate(rows, 3 * half * units),
    )(vmem(near), vmem(far), gate, up, vmem(gate_acc), vmem(up_acc), down, *after)


def rest_products(near, inner, down, ep_count):
    rows = near.shape[0]
    units, width = down.shape[1:]
    half = width // 2
    return pl.pallas_call(
        functools.partial(rest_kernel, ep_count),
        out_shape=(pltpu.VMEM((rows // 2, half), f32), pltpu.VMEM((rows // 2, half), bf16)),
        in_specs=[in_vmem()] * 3,
        out_specs=(in_vmem(),) * 2,
        compiler_params=pltpu.CompilerParams(vmem_limit_bytes=8 * MIB),
        cost_estimate=estimate(rows, half * units),
    )(vmem(near), vmem(inner), down)


def fold_kernel(arrived, parts, *refs):
    outs = refs[-parts:]
    rows = outs[0].shape[0]
    start = at = 0
    for number in arrived:
        ours = refs[at : at + 1 + number]
        at += 1 + number
        total = ours[0][...]
        for g in ours[1:]:
            total += g[...].astype(f32)
        columns = slice(start, start + total.shape[1])
        start += total.shape[1]
        for i, out in enumerate(outs):
            out[:, columns] = total[i * rows : (i + 1) * rows].astype(out.dtype)


def fold(held, parts, *after, out=None, flops=0):
    rows = held[0][0].shape[0]
    width = sum(keep.shape[1] for keep, _ in held)
    part = (rows // parts, width)
    operands = [vmem(x) for keep, gots in held for x in [keep] + gots]
    shapes = (pltpu.VMEM(part, f32),) + (pltpu.VMEM(part, bf16),) * (parts - 1)
    return pl.pallas_call(
        functools.partial(fold_kernel, [len(gots) for _, gots in held], parts),
        out_shape=shapes if out is None else (out,),
        in_specs=[in_vmem()] * len(operands) + [anywhere()] * len(after),
        out_specs=(in_vmem(),) * parts,
        compiler_params=pltpu.CompilerParams(vmem_limit_bytes=4 * MIB),
        cost_estimate=pl.CostEstimate(flops=flops, bytes_accessed=8 * rows * width, transcendentals=0),
    )(*operands, *after)


def pages_kernel(dp_count, page_ref, dest_ref, pool_ref, after_ref, low_ref, high_ref):
    own, width = pool_ref.shape
    me = lax.axis_index("dp")
    slots = dp_count * MCAP
    row = lax.broadcasted_iota(jnp.int32, (slots, own), 0)
    column = lax.broadcasted_iota(jnp.int32, (slots, own), 1)
    pick = jnp.zeros((slots, own), f32)
    entries = page_ref.shape[1]
    pages = [page_ref[:, m : m + 1] for m in range(entries)]
    dests = [dest_ref[:, m : m + 1] for m in range(entries)]
    for m in range(entries):
        rank = jnp.zeros((1, 1), jnp.int32)
        for n in range(m):
            rank += jnp.where(dests[n] == dests[m], 1, 0)
        bucket = jnp.bitwise_xor(dests[m], me) * MCAP + rank
        pick = jnp.where((row == bucket) & (column == pages[m]), 1.0, pick)
    pick = pick.astype(bf16)
    step = 2048
    for i in range(width // step):
        columns = slice(i * step, (i + 1) * step)
        out = jnp.dot(pick, pool_ref[:, columns], preferred_element_type=f32)
        low_ref[:, columns] = out[: slots // 2].astype(bf16)
        high_ref[:, columns] = out[slots // 2 :].astype(bf16)


def pick_pages(moved_page, moved_dest, latent_pool, after, dp_count):
    width = latent_pool.shape[1]
    half = pltpu.VMEM((dp_count * MCAP // 2, width), bf16)
    return pl.pallas_call(
        functools.partial(pages_kernel, dp_count),
        out_shape=(half, half),
        in_specs=[in_vmem()] * 3 + [anywhere()],
        out_specs=(in_vmem(),) * 2,
        compiler_params=pltpu.CompilerParams(vmem_limit_bytes=4 * MIB),
        cost_estimate=pl.CostEstimate(flops=0, bytes_accessed=4 * latent_pool.size, transcendentals=0),
    )(vmem(moved_page), vmem(moved_dest), vmem(latent_pool), after)


def rows_kernel(places, *refs):
    out_ref = refs[-1]
    width = out_ref.shape[1]
    step = 2048
    for i in range(width // step):
        columns = slice(i * step, (i + 1) * step)
        pieces = [ref[:, columns].astype(f32)[low:high] for ref, (low, high) in zip(refs, places)]
        out_ref[:, columns] = jnp.concatenate(pieces, axis=0).astype(bf16)


def rows_of(pieces, *after):
    rows = sum(high - low for _, low, high in pieces)
    width = pieces[0][0].shape[1]
    return pl.pallas_call(
        functools.partial(rows_kernel, [(low, high) for _, low, high in pieces]),
        out_shape=pltpu.VMEM((rows, width), bf16),
        in_specs=[in_vmem()] * len(pieces) + [anywhere()] * len(after),
        out_specs=in_vmem(),
        compiler_params=pltpu.CompilerParams(vmem_limit_bytes=4 * MIB),
        cost_estimate=pl.CostEstimate(flops=0, bytes_accessed=4 * rows * width, transcendentals=0),
    )(*[vmem(x) for x, _, _ in pieces], *after)


def exchange_pages(low, first, dp_count, after):
    blocks, senders = [(low, 0, low.shape[0])], [0]
    got = first
    moves = []
    for number, bit in enumerate(partner_bits(dp_count)):
        if number:
            got = swap(sent, "dp", pairs_of(dp_count, bit))
            moves.append((sent, got))
        size = got.shape[0] // len(blocks)
        blocks = blocks + [(got, i * size, (i + 1) * size) for i in range(len(blocks))]
        senders = senders + [s ^ bit for s in senders]
        if size > MCAP:
            sent = rows_of([(x, start + size // 2, end) for x, start, end in blocks], after)
            blocks = [(x, start, start + size // 2) for x, start, _ in blocks]
    return rows_of(blocks), senders, moves


def attend_kernel(senders, length_ref, table_ref, query_ref, pool_ref, arrived_ref, out_ref, query_rows):
    rows_dev = query_ref.shape[0]
    own, width = pool_ref.shape
    arrived = arrived_ref.shape[0]
    slots = -(-(own + arrived) // 16) * 16
    pair_width = 2 * LAT
    pairs = width // pair_width
    me = lax.axis_index("dp")

    for h in range(HEADS // 2):
        query_rows[h * rows_dev : (h + 1) * rows_dev, :] = query_ref[:, h * pair_width : (h + 1) * pair_width].astype(f32)
    straight = query_rows[...]
    turned = pltpu.roll(straight, LAT, 1)
    first = lax.broadcasted_iota(jnp.int32, straight.shape, 1) < LAT
    query_all = jnp.concatenate(
        [
            jnp.where(first, straight, 0.0),
            jnp.where(first, turned, 0.0),
            jnp.where(first, 0.0, turned),
            jnp.where(first, 0.0, straight),
        ],
        axis=0,
    ).astype(bf16)

    pieces = []
    for j in range(pairs):
        columns = slice(j * pair_width, (j + 1) * pair_width)
        parts = [pool_ref[:, columns].astype(f32), arrived_ref[:, columns].astype(f32)]
        if slots > own + arrived:
            parts.append(jnp.zeros((slots - own - arrived, pair_width), f32))
        pieces.append(jnp.concatenate(parts, axis=0).astype(bf16))
    keys = jnp.concatenate(pieces, axis=0)

    scores = lax.dot_general(query_all, keys, (((1,), (1,)), ((), ())), preferred_element_type=f32) * score_scale

    column = lax.broadcasted_iota(jnp.int32, (1, pairs * slots), 1)
    pair = column // slots
    place = column - pair * slots
    slot = place
    for i, s in enumerate(senders):
        source = jnp.bitwise_xor(me, s)
        for k in range(MCAP):
            slot = jnp.where(place == own + i * MCAP + k, own + source * MCAP + k, slot)
    limits = []
    for r in range(rows_dev):
        limit = jnp.full(column.shape, -1, jnp.int32)
        for p in range(table_ref.shape[1]):
            limit = jnp.where(slot == table_ref[r, p], length_ref[r] - p * PAGE, limit)
        limit = jnp.where(place < own + arrived, limit, -1)
        limits.append(limit - 2 * pair)
    half = scores.shape[0] // 2
    row = lax.broadcasted_iota(jnp.int32, (half, 1), 0) % rows_dev
    limit = limits[0]
    for r in range(1, rows_dev):
        limit = jnp.where(row == r, limits[r], limit)
    even = jnp.where(limit > 0, scores[:half], -jnp.inf)
    odd = jnp.where(limit > 1, scores[half:], -jnp.inf)
    peak = jnp.maximum(jnp.max(even, axis=1, keepdims=True), jnp.max(odd, axis=1, keepdims=True))
    even = jnp.exp(even - peak)
    odd = jnp.exp(odd - peak)
    total = jnp.sum(even, axis=1, keepdims=True) + jnp.sum(odd, axis=1, keepdims=True)
    even = (even / total).astype(bf16)
    odd = (odd / total).astype(bf16)
    from_even = jnp.dot(even, keys[:, :VL], preferred_element_type=f32)
    from_odd = jnp.dot(odd, keys[:, VL:], preferred_element_type=f32)
    shift = LAT - VL
    wide = pair_width - VL
    attended = from_even + pltpu.roll(from_odd, wide - shift, 1)[:, :VL]
    for h in range(HEADS):
        at = (h % 2) * (half // 2) + (h // 2) * rows_dev
        out_ref[:, h * VL : (h + 1) * VL] = attended[at : at + rows_dev].astype(bf16)


def attend(lengths, page_table, queries, latent_pool, arrived, senders):
    rows_dev = queries.shape[0]
    return pl.pallas_call(
        functools.partial(attend_kernel, senders),
        out_shape=jax.ShapeDtypeStruct((rows_dev, HEADS * VL), bf16),
        in_specs=[in_smem(), in_smem(), in_vmem(), in_vmem(), in_vmem()],
        out_specs=in_vmem(),
        scratch_shapes=[pltpu.VMEM((HEADS // 2 * rows_dev, 2 * LAT), f32)],
        compiler_params=pltpu.CompilerParams(vmem_limit_bytes=16 * MIB),
        cost_estimate=pl.CostEstimate(flops=1 << 30, bytes_accessed=4 << 20, transcendentals=1 << 17),
    )(lengths, page_table, queries, vmem(latent_pool), vmem(arrived))


def body(
    hidden,
    routes,
    route_weight,
    gate_weight,
    up_weight,
    down_weight,
    queries,
    latent_pool,
    lengths,
    page_table,
    moved_page,
    moved_dest,
):
    ep_count = lax.axis_size("ep")
    dp_count = lax.axis_size("dp")
    count = ep_count * dp_count
    stages = stage_partners(count)

    def trade(x, bit):
        return swap(x, AXES, pairs_of(count, bit))

    mine = (hidden, routes, route_weight)
    got = [trade(x, 1) for x in mine]
    *mine, pool, moved_page, moved_dest = fetch(*mine, latent_pool, moved_page, moved_dest)
    near = make_payload(mine, got, ep_count)
    for number, partners in enumerate(stages):
        got = [trade(near, bit) for bit in partners]
        after = []
        if number == 0:
            low, high = pick_pages(moved_page, moved_dest, pool, near, dp_count)
            after = [high]
            bit = partner_bits(dp_count)[0]
            first = swap(high, "dp", pairs_of(dp_count, bit))
        if number == len(stages) - 1:
            after = [first]
        near = merge([near] + got, MERGE_FLOPS if number < len(stages) - 1 else MERGE_FLOPS // 4, *after)
    far = trade(near, 1)
    arrived, senders, moves = exchange_pages(low, first, dp_count, near)
    gate_acc, up_acc = near_products(near, gate_weight, up_weight, down_weight, *[sent for sent, _ in moves])
    inner, keep_a, send_a = far_products(
        near, far, gate_weight, up_weight, gate_acc, up_acc, down_weight, ep_count, *[got for _, got in moves]
    )
    got_a = trade(send_a, 1)
    keep_b, send_b = rest_products(near, inner, down_weight, ep_count)
    got_b = trade(send_b, 1)
    (sum_a,) = fold([(keep_a, [got_a])], 1, out=pltpu.VMEM(keep_a.shape, f32), flops=MERGE_FLOPS // 4)
    held = [(sum_a, []), (keep_b, [got_b])]
    after = []
    for number, partners in enumerate(reversed(stages)):
        keep, *send = fold(held, len(partners) + 1, *(after if number == 1 else []))
        held = [(keep, [trade(x, bit) for x, bit in zip(send, partners)])]
        if number == 0:
            attended = attend(lengths, page_table, queries, pool, arrived, senders)
            after = [hbm(attended)]
    (expert_mix,) = fold(held, 1, out=jax.ShapeDtypeStruct(hidden.shape, bf16))
    return expert_mix, attended


def solution(mesh):
    rows = P(("inst", "ep", "dp"), None)
    in_specs = (
        rows,
        rows,
        rows,
        P("ep", None, "dp"),
        P("ep", None, "dp"),
        P("ep", "dp", None),
        rows,
        rows,
        P(("inst", "ep", "dp")),
        rows,
        rows,
        rows,
    )
    return jax.shard_map(body, mesh=mesh, in_specs=in_specs, out_specs=(rows, rows), check_vma=False)
```

```python
import functools

import jax
import jax.numpy as jnp
from jax import lax
from jax.experimental import pallas as pl
from jax.experimental.pallas import tpu as pltpu
from jax.sharding import PartitionSpec as P

HEADS = 64
LAT = 576
VL = 512
MCAP = 2
PAGE = 32
LANES = 128
AXES = ("ep", "dp")
MIB = 1 << 20
MERGE_FLOPS = 20_000_000_000

score_scale = 192.0 ** (-0.5)
bf16 = jnp.bfloat16
f32 = jnp.float32


def in_vmem():
    return pl.BlockSpec(memory_space=pltpu.VMEM)


def in_smem():
    return pl.BlockSpec(memory_space=pltpu.SMEM)


def vmem(x):
    return pltpu.with_memory_space_constraint(x, pltpu.VMEM)


def hbm(x):
    return pltpu.with_memory_space_constraint(x, pltpu.HBM)


def anywhere():
    return pl.BlockSpec(memory_space=pl.ANY)


def in_hbm():
    return pl.BlockSpec(memory_space=pltpu.HBM)


def partner_bits(count):
    bits = []
    b = count // 2
    while b:
        bits.append(b)
        b //= 2
    return bits


def swap(x, axes, pairs):
    return lax.ppermute(x, axes, pairs)


def stage_partners(count):
    bits = partner_bits(count)[:-1]
    stages = [(bits[0],)] if len(bits) % 2 else []
    bits = bits[len(bits) % 2 :]
    for high, low in zip(bits[::2], bits[1::2]):
        stages.append((high, high ^ low, low))
    high, far, low = stages[-1]
    return stages[:-1] + [(far, high, low)]


def pairs_of(count, bit):
    return [(i, i ^ bit) for i in range(count)]


def fetch_kernel(*refs):
    count = (len(refs) - 1) // 2
    copies = [pltpu.make_async_copy(refs[i], refs[count + i], refs[-1].at[i]) for i in range(count)]
    for c in copies:
        c.start()
    for c in copies:
        c.wait()


def fetch(*arrays):
    return pl.pallas_call(
        fetch_kernel,
        out_shape=tuple(pltpu.VMEM(x.shape, x.dtype) for x in arrays),
        in_specs=[in_hbm()] * len(arrays),
        out_specs=(in_vmem(),) * len(arrays),
        scratch_shapes=[pltpu.SemaphoreType.DMA((len(arrays),))],
        compiler_params=pltpu.CompilerParams(vmem_limit_bytes=4 * MIB),
        cost_estimate=pl.CostEstimate(flops=MERGE_FLOPS // 16, bytes_accessed=MIB, transcendentals=0),
    )(*[hbm(x) for x in arrays])


def payload_kernel(ep_count, mine_hidden, mine_routes, mine_weight, got_hidden, got_routes, got_weight, out_ref):
    first = lax.rem(lax.axis_index("dp"), 2) == 0
    rows, width = mine_hidden.shape
    half = width // 2

    def in_order(mine, got):
        return jnp.where(first, jnp.concatenate([mine, got], axis=0), jnp.concatenate([got, mine], axis=0))

    def my_half(ref):
        return jnp.where(first, ref[:, :half].astype(f32), ref[:, half:].astype(f32))

    out_ref[:, :half] = in_order(my_half(mine_hidden), my_half(got_hidden)).astype(bf16)
    routes = in_order(mine_routes[...], got_routes[...])
    weight = in_order(mine_weight[...], got_weight[...])
    column = lax.broadcasted_iota(jnp.int32, (2 * rows, LANES), 1)
    expert = jnp.where(column < ep_count, column, column - ep_count)
    total = jnp.zeros((2 * rows, LANES), f32)
    for k in range(routes.shape[1]):
        total += jnp.where(routes[:, k : k + 1] == expert, weight[:, k : k + 1], 0.0)
    high = total.astype(bf16).astype(f32)
    low = total - high
    out_ref[:, half:] = jnp.where(column < ep_count, high, jnp.where(column < 2 * ep_count, low, 0.0)).astype(bf16)


def make_payload(mine, got, ep_count):
    rows, width = mine[0].shape
    return pl.pallas_call(
        functools.partial(payload_kernel, ep_count),
        out_shape=pltpu.VMEM((2 * rows, width // 2 + LANES), bf16),
        in_specs=[in_vmem()] * 6,
        out_specs=in_vmem(),
        compiler_params=pltpu.CompilerParams(vmem_limit_bytes=4 * MIB),
        cost_estimate=pl.CostEstimate(flops=0, bytes_accessed=4 * rows * width, transcendentals=0),
    )(*[vmem(x) for x in mine], *[vmem(x) for x in got])


def merge_kernel(parts, *refs):
    out_ref = refs[-1]
    half = refs[0].shape[0] // 2
    pieces = [r[...].astype(f32) for r in [refs[0], *refs[1:parts][::-1]]]
    cores = [p[:half] for p in pieces] + [p[half:] for p in pieces]
    out_ref[...] = jnp.concatenate(cores, axis=0).astype(bf16)


def merge(pieces, flops, *after):
    rows, width = pieces[0].shape
    return pl.pallas_call(
        functools.partial(merge_kernel, len(pieces)),
        out_shape=pltpu.VMEM((len(pieces) * rows, width), bf16),
        in_specs=[in_vmem()] * len(pieces) + [anywhere()] * len(after),
        out_specs=in_vmem(),
        compiler_params=pltpu.CompilerParams(vmem_limit_bytes=4 * MIB),
        cost_estimate=pl.CostEstimate(flops=flops, bytes_accessed=8 * rows * width, transcendentals=0),
    )(*[vmem(p) for p in pieces[:1] + pieces[:0:-1]], *after)


def half_start(width, near):
    core = lax.rem(lax.axis_index("dp"), 2)
    core = core if near else 1 - core
    return pl.multiple_of(core * (width // 2), width // 2)


def padded(x):
    rows = x.shape[0]
    return x if rows >= 128 else jnp.concatenate([x] * (128 // rows), axis=0)


def near_kernel(ep_count, near_ref, gate_ref, up_ref, *refs):
    gate_out, up_out, weight_out = refs[-3:]
    weight_out[...] = jnp.broadcast_to(row_weights(near_ref, gate_ref.shape[1] // 2, ep_count), weight_out.shape)
    rows, width = near_ref.shape[0], gate_ref.shape[1]
    at = pl.ds(half_start(width, True), width // 2)
    x = padded(near_ref[:, : width // 2])
    gate_out[...] = jnp.dot(x, gate_ref[0, at, :], preferred_element_type=f32)[:rows]
    up_out[...] = jnp.dot(x, up_ref[0, at, :], preferred_element_type=f32)[:rows]


def row_weights(near_ref, half, ep_count):
    ep = lax.axis_index("ep")
    table = near_ref[:, half:].astype(f32)
    column = lax.broadcasted_iota(jnp.int32, table.shape, 1)
    mine = (column == ep) | (column == ep + ep_count)
    return jnp.sum(jnp.where(mine, table, 0.0), axis=1, keepdims=True)


STEPS = 7


def down_half(inner, row_weight, down_ref, start, keep_ref, send_ref):
    first = lax.rem(lax.axis_index("dp"), 2) == 0
    rows, half = keep_ref.shape
    step = half // STEPS
    x = padded(inner)
    for i in range(STEPS):
        columns = slice(i * step, (i + 1) * step)
        out = jnp.dot(x, down_ref[0, :, start + i * step : start + (i + 1) * step], preferred_element_type=f32)
        out = out[: 2 * rows] * row_weight
        keep_ref[:, columns] = jnp.where(first, out[:rows], out[rows:])
        send_ref[:, columns] = jnp.where(first, out[rows:], out[:rows]).astype(bf16)


def far_kernel(weight_ref, far_ref, gate_ref, up_ref, gate_in, up_in, down_ref, *refs):
    inner_ref, keep_ref, send_ref = refs[-3:]
    rows, width = weight_ref.shape[0], gate_ref.shape[1]
    half = width // 2
    at = pl.ds(half_start(width, False), half)
    row_weight = weight_ref[:, :1]
    x = padded(far_ref[:, :half])
    gate = gate_in[...] + jnp.dot(x, gate_ref[0, at, :], preferred_element_type=f32)[:rows]
    up = up_in[...] + jnp.dot(x, up_ref[0, at, :], preferred_element_type=f32)[:rows]
    inner = (gate / (1.0 + jnp.exp(-gate)) * up).astype(bf16)
    inner_ref[...] = inner
    down_half(inner, row_weight, down_ref, 0, keep_ref, send_ref)


def rest_kernel(weight_ref, inner_ref, down_ref, keep_ref, send_ref):
    half = keep_ref.shape[1]
    down_half(inner_ref[...], weight_ref[:, :1], down_ref, half, keep_ref, send_ref)


def estimate(rows, weights):
    return pl.CostEstimate(flops=2 * rows * weights, bytes_accessed=2 * weights, transcendentals=0)


def near_products(near, gate, up, down, ep_count, *after):
    rows = near.shape[0]
    width, units = gate.shape[1:]
    acc = pltpu.VMEM((rows, units), f32)
    return pl.pallas_call(
        functools.partial(near_kernel, ep_count),
        out_shape=(acc, acc, pltpu.VMEM((rows, LANES), f32)),
        in_specs=[in_vmem()] * 4 + [anywhere()] * len(after),
        out_specs=(in_vmem(),) * 3,
        compiler_params=pltpu.CompilerParams(vmem_limit_bytes=8 * MIB),
        cost_estimate=estimate(rows, width * units),
    )(vmem(near), gate, up, down, *after)


def far_products(weight, far, gate, up, gate_acc, up_acc, down, *after):
    rows = weight.shape[0]
    units, width = down.shape[1:]
    half = width // 2
    return pl.pallas_call(
        far_kernel,
        out_shape=(
            pltpu.VMEM((rows, units), bf16),
            pltpu.VMEM((rows // 2, half), f32),
            pltpu.VMEM((rows // 2, half), bf16),
        ),
        in_specs=[in_vmem()] * 7 + [anywhere()] * len(after),
        out_specs=(in_vmem(),) * 3,
        compiler_params=pltpu.CompilerParams(vmem_limit_bytes=8 * MIB),
        cost_estimate=estimate(rows, 3 * half * units),
    )(vmem(weight), vmem(far), gate, up, vmem(gate_acc), vmem(up_acc), down, *after)


def rest_products(weight, inner, down):
    rows = weight.shape[0]
    units, width = down.shape[1:]
    half = width // 2
    return pl.pallas_call(
        rest_kernel,
        out_shape=(pltpu.VMEM((rows // 2, half), f32), pltpu.VMEM((rows // 2, half), bf16)),
        in_specs=[in_vmem()] * 3,
        out_specs=(in_vmem(),) * 2,
        compiler_params=pltpu.CompilerParams(vmem_limit_bytes=8 * MIB),
        cost_estimate=estimate(rows, half * units),
    )(vmem(weight), vmem(inner), down)


def fold_kernel(arrived, parts, *refs):
    outs = refs[-parts:]
    rows = outs[0].shape[0]
    start = at = 0
    for number in arrived:
        ours = refs[at : at + 1 + number]
        at += 1 + number
        total = ours[0][...]
        for g in ours[1:]:
            total += g[...].astype(f32)
        columns = slice(start, start + total.shape[1])
        start += total.shape[1]
        for i, out in enumerate(outs):
            out[:, columns] = total[i * rows : (i + 1) * rows].astype(out.dtype)


def fold(held, parts, *after, out=None, flops=0):
    rows = held[0][0].shape[0]
    width = sum(keep.shape[1] for keep, _ in held)
    part = (rows // parts, width)
    operands = [vmem(x) for keep, gots in held for x in [keep] + gots]
    shapes = (pltpu.VMEM(part, f32),) + (pltpu.VMEM(part, bf16),) * (parts - 1)
    return pl.pallas_call(
        functools.partial(fold_kernel, [len(gots) for _, gots in held], parts),
        out_shape=shapes if out is None else (out,),
        in_specs=[in_vmem()] * len(operands) + [anywhere()] * len(after),
        out_specs=(in_vmem(),) * parts,
        compiler_params=pltpu.CompilerParams(vmem_limit_bytes=4 * MIB),
        cost_estimate=pl.CostEstimate(flops=flops, bytes_accessed=8 * rows * width, transcendentals=0),
    )(*operands, *after)


def pages_kernel(dp_count, page_ref, dest_ref, pool_ref, after_ref, low_ref, high_ref):
    own, width = pool_ref.shape
    me = lax.axis_index("dp")
    slots = dp_count * MCAP
    row = lax.broadcasted_iota(jnp.int32, (slots, own), 0)
    column = lax.broadcasted_iota(jnp.int32, (slots, own), 1)
    pick = jnp.zeros((slots, own), f32)
    entries = page_ref.shape[1]
    pages = [page_ref[:, m : m + 1] for m in range(entries)]
    dests = [dest_ref[:, m : m + 1] for m in range(entries)]
    for m in range(entries):
        rank = jnp.zeros((1, 1), jnp.int32)
        for n in range(m):
            rank += jnp.where(dests[n] == dests[m], 1, 0)
        bucket = jnp.bitwise_xor(dests[m], me) * MCAP + rank
        pick = jnp.where((row == bucket) & (column == pages[m]), 1.0, pick)
    pick = pick.astype(bf16)
    step = 2048
    for i in range(width // step):
        columns = slice(i * step, (i + 1) * step)
        out = jnp.dot(pick, pool_ref[:, columns], preferred_element_type=f32)
        low_ref[:, columns] = out[: slots // 2].astype(bf16)
        high_ref[:, columns] = out[slots // 2 :].astype(bf16)


def pick_pages(moved_page, moved_dest, latent_pool, after, dp_count):
    width = latent_pool.shape[1]
    half = pltpu.VMEM((dp_count * MCAP // 2, width), bf16)
    return pl.pallas_call(
        functools.partial(pages_kernel, dp_count),
        out_shape=(half, half),
        in_specs=[in_vmem()] * 3 + [anywhere()],
        out_specs=(in_vmem(),) * 2,
        compiler_params=pltpu.CompilerParams(vmem_limit_bytes=4 * MIB),
        cost_estimate=pl.CostEstimate(flops=0, bytes_accessed=4 * latent_pool.size, transcendentals=0),
    )(vmem(moved_page), vmem(moved_dest), vmem(latent_pool), after)


def rows_kernel(places, *refs):
    out_ref = refs[-1]
    width = out_ref.shape[1]
    step = 2048
    for i in range(width // step):
        columns = slice(i * step, (i + 1) * step)
        pieces = [ref[:, columns].astype(f32)[low:high] for ref, (low, high) in zip(refs, places)]
        out_ref[:, columns] = jnp.concatenate(pieces, axis=0).astype(bf16)


def rows_of(pieces, *after):
    rows = sum(high - low for _, low, high in pieces)
    width = pieces[0][0].shape[1]
    return pl.pallas_call(
        functools.partial(rows_kernel, [(low, high) for _, low, high in pieces]),
        out_shape=pltpu.VMEM((rows, width), bf16),
        in_specs=[in_vmem()] * len(pieces) + [anywhere()] * len(after),
        out_specs=in_vmem(),
        compiler_params=pltpu.CompilerParams(vmem_limit_bytes=4 * MIB),
        cost_estimate=pl.CostEstimate(flops=0, bytes_accessed=4 * rows * width, transcendentals=0),
    )(*[vmem(x) for x, _, _ in pieces], *after)


def exchange_pages(low, first, dp_count, after):
    blocks, senders = [(low, 0, low.shape[0])], [0]
    got = first
    moves = []
    for number, bit in enumerate(partner_bits(dp_count)):
        if number:
            got = swap(sent, "dp", pairs_of(dp_count, bit))
            moves.append((sent, got))
        size = got.shape[0] // len(blocks)
        blocks = blocks + [(got, i * size, (i + 1) * size) for i in range(len(blocks))]
        senders = senders + [s ^ bit for s in senders]
        if size > MCAP:
            sent = rows_of([(x, start + size // 2, end) for x, start, end in blocks], after)
            blocks = [(x, start, start + size // 2) for x, start, _ in blocks]
    return rows_of(blocks), senders, moves


def attend_kernel(senders, length_ref, table_ref, query_ref, pool_ref, arrived_ref, out_ref, query_rows):
    rows_dev = query_ref.shape[0]
    own, width = pool_ref.shape
    arrived = arrived_ref.shape[0]
    slots = -(-(own + arrived) // 16) * 16
    pair_width = 2 * LAT
    pairs = width // pair_width
    me = lax.axis_index("dp")

    for h in range(HEADS // 2):
        query_rows[h * rows_dev : (h + 1) * rows_dev, :] = query_ref[:, h * pair_width : (h + 1) * pair_width].astype(f32)
    straight = query_rows[...]
    turned = pltpu.roll(straight, LAT, 1)
    first = lax.broadcasted_iota(jnp.int32, straight.shape, 1) < LAT
    query_all = jnp.concatenate(
        [
            jnp.where(first, straight, 0.0),
            jnp.where(first, turned, 0.0),
            jnp.where(first, 0.0, turned),
            jnp.where(first, 0.0, straight),
        ],
        axis=0,
    ).astype(bf16)

    pieces = []
    for j in range(pairs):
        columns = slice(j * pair_width, (j + 1) * pair_width)
        parts = [pool_ref[:, columns].astype(f32), arrived_ref[:, columns].astype(f32)]
        if slots > own + arrived:
            parts.append(jnp.zeros((slots - own - arrived, pair_width), f32))
        pieces.append(jnp.concatenate(parts, axis=0).astype(bf16))
    keys = jnp.concatenate(pieces, axis=0)

    scores = lax.dot_general(query_all, keys, (((1,), (1,)), ((), ())), preferred_element_type=f32) * score_scale

    column = lax.broadcasted_iota(jnp.int32, (1, pairs * slots), 1)
    pair = column // slots
    place = column - pair * slots
    slot = place
    for i, s in enumerate(senders):
        source = jnp.bitwise_xor(me, s)
        for k in range(MCAP):
            slot = jnp.where(place == own + i * MCAP + k, own + source * MCAP + k, slot)
    limits = []
    for r in range(rows_dev):
        limit = jnp.full(column.shape, -1, jnp.int32)
        for p in range(table_ref.shape[1]):
            limit = jnp.where(slot == table_ref[r, p], length_ref[r] - p * PAGE, limit)
        limit = jnp.where(place < own + arrived, limit, -1)
        limits.append(limit - 2 * pair)
    half = scores.shape[0] // 2
    row = lax.broadcasted_iota(jnp.int32, (half, 1), 0) % rows_dev
    limit = limits[0]
    for r in range(1, rows_dev):
        limit = jnp.where(row == r, limits[r], limit)
    even = jnp.where(limit > 0, scores[:half], -jnp.inf)
    odd = jnp.where(limit > 1, scores[half:], -jnp.inf)
    peak = jnp.maximum(jnp.max(even, axis=1, keepdims=True), jnp.max(odd, axis=1, keepdims=True))
    even = jnp.exp(even - peak)
    odd = jnp.exp(odd - peak)
    total = jnp.sum(even, axis=1, keepdims=True) + jnp.sum(odd, axis=1, keepdims=True)
    even = (even / total).astype(bf16)
    odd = (odd / total).astype(bf16)
    from_even = jnp.dot(even, keys[:, :VL], preferred_element_type=f32)
    from_odd = jnp.dot(odd, keys[:, VL:], preferred_element_type=f32)
    shift = LAT - VL
    wide = pair_width - VL
    attended = from_even + pltpu.roll(from_odd, wide - shift, 1)[:, :VL]
    for h in range(HEADS):
        at = (h % 2) * (half // 2) + (h // 2) * rows_dev
        out_ref[:, h * VL : (h + 1) * VL] = attended[at : at + rows_dev].astype(bf16)


def attend(lengths, page_table, queries, latent_pool, arrived, senders):
    rows_dev = queries.shape[0]
    return pl.pallas_call(
        functools.partial(attend_kernel, senders),
        out_shape=jax.ShapeDtypeStruct((rows_dev, HEADS * VL), bf16),
        in_specs=[in_smem(), in_smem(), in_vmem(), in_vmem(), in_vmem()],
        out_specs=in_vmem(),
        scratch_shapes=[pltpu.VMEM((HEADS // 2 * rows_dev, 2 * LAT), f32)],
        compiler_params=pltpu.CompilerParams(vmem_limit_bytes=16 * MIB),
        cost_estimate=pl.CostEstimate(flops=1 << 30, bytes_accessed=4 << 20, transcendentals=1 << 17),
    )(lengths, page_table, queries, vmem(latent_pool), vmem(arrived))


def body(
    hidden,
    routes,
    route_weight,
    gate_weight,
    up_weight,
    down_weight,
    queries,
    latent_pool,
    lengths,
    page_table,
    moved_page,
    moved_dest,
):
    ep_count = lax.axis_size("ep")
    dp_count = lax.axis_size("dp")
    count = ep_count * dp_count
    stages = stage_partners(count)

    def trade(x, bit):
        return swap(x, AXES, pairs_of(count, bit))

    mine = (hidden, routes, route_weight)
    got = [trade(x, 1) for x in mine]
    *mine, pool, moved_page, moved_dest = fetch(*mine, latent_pool, moved_page, moved_dest)
    near = make_payload(mine, got, ep_count)
    for number, partners in enumerate(stages):
        got = [trade(near, bit) for bit in partners]
        after = []
        if number == 0:
            low, high = pick_pages(moved_page, moved_dest, pool, near, dp_count)
            after = [high]
            bit = partner_bits(dp_count)[0]
            first = swap(high, "dp", pairs_of(dp_count, bit))
        if number == len(stages) - 1:
            after = [first]
        near = merge([near] + got, MERGE_FLOPS if number < len(stages) - 1 else MERGE_FLOPS // 4, *after)
    far = trade(near, 1)
    arrived, senders, moves = exchange_pages(low, first, dp_count, near)
    gate_acc, up_acc, weight = near_products(near, gate_weight, up_weight, down_weight, ep_count, *[sent for sent, _ in moves])
    inner, keep_a, send_a = far_products(
        weight, far, gate_weight, up_weight, gate_acc, up_acc, down_weight, *[got for _, got in moves]
    )
    got_a = trade(send_a, 1)
    keep_b, send_b = rest_products(weight, inner, down_weight)
    got_b = trade(send_b, 1)
    (sum_a,) = fold([(keep_a, [got_a])], 1, out=pltpu.VMEM(keep_a.shape, f32), flops=MERGE_FLOPS // 4)
    held = [(sum_a, []), (keep_b, [got_b])]
    after = []
    for number, partners in enumerate(reversed(stages)):
        keep, *send = fold(held, len(partners) + 1, *(after if number == 1 else []))
        held = [(keep, [trade(x, bit) for x, bit in zip(send, partners)])]
        if number == 0:
            attended = attend(lengths, page_table, queries, pool, arrived, senders)
            after = [hbm(attended)]
    (expert_mix,) = fold(held, 1, out=jax.ShapeDtypeStruct(hidden.shape, bf16))
    return expert_mix, attended


def solution(mesh):
    rows = P(("inst", "ep", "dp"), None)
    in_specs = (
        rows,
        rows,
        rows,
        P("ep", None, "dp"),
        P("ep", None, "dp"),
        P("ep", "dp", None),
        rows,
        rows,
        P(("inst", "ep", "dp")),
        rows,
        rows,
        rows,
    )
    return jax.shard_map(body, mesh=mesh, in_specs=in_specs, out_specs=(rows, rows), check_vma=False)
```
